32 devices in a mesh: dp: 2 (over y), expert: 16 (over z, x, core).
Axes of the slice: x: 2, y: 2, z: 4, core: 2. Of those that a mesh axis runs over, the one named last changes fastest.
Arguments:
- tokens: bfloat16 [4096, 2048], P(('dp', 'expert')), may hold values from -6 to 6
- attn_gain: bfloat16 [2048], P(('dp', 'expert')), may hold values from 0.25 to 1.75
- q_gain: bfloat16 [2048], P(('dp', 'expert')), may hold values from 0.25 to 1.75
- k_gain: bfloat16 [2048], P(('dp', 'expert')), may hold values from 0.25 to 1.75
- ffn_gain: bfloat16 [2048], P(('dp', 'expert')), may hold values from 0.25 to 1.75
- w_query: bfloat16 [2048, 2048], P(('dp', 'expert')), may hold values from -0.125 to 0.125
- w_key: bfloat16 [2048, 2048], P(('dp', 'expert')), may hold values from -0.125 to 0.125
- w_value: bfloat16 [2048, 2048], P(('dp', 'expert')), may hold values from -0.125 to 0.125
- w_out: bfloat16 [2048, 2048], P(('dp', 'expert')), may hold values from -5 to 5
- router: bfloat16 [2048, 16], P(('dp', 'expert')), may hold values from -0.0625 to 0.0625
- w_gate: bfloat16 [16, 2048, 1024], P('expert', 'dp'), may hold values from -0.125 to 0.125
- w_up: bfloat16 [16, 2048, 1024], P('expert', 'dp'), may hold values from -0.125 to 0.125
- w_down: bfloat16 [16, 1024, 2048], P('expert', 'dp'), may hold values from -4 to 4
- cotangent: bfloat16 [4096, 2048], P(('dp', 'expert')), may hold values from -6 to 6
- routes: int32 [4096, 8], P(('dp', 'expert')), may hold values from 0 to 15, all different within a row; in each aligned block of 128 rows (0 to 127, 128 to 255, ...) at most 96 rows name the same one
- parents: int32 [32], replicated, may hold values from -1 to 30, as said below
Outputs:
- output: bfloat16 [4096, 2048], P(('dp', 'expert'))
- grad_tokens: float32 [4096, 2048], P(('dp', 'expert'))
- grad_attn_gain: float32 [2048], P(('dp', 'expert'))
- grad_q_gain: float32 [2048], P(('dp', 'expert'))
- grad_k_gain: float32 [2048], P(('dp', 'expert'))
- grad_ffn_gain: float32 [2048], P(('dp', 'expert'))
- grad_w_query: float32 [2048, 2048], P(('dp', 'expert'))
- grad_w_key: float32 [2048, 2048], P(('dp', 'expert'))
- grad_w_value: float32 [2048, 2048], P(('dp', 'expert'))
- grad_w_out: float32 [2048, 2048], P(('dp', 'expert'))
- grad_router: float32 [2048, 16], P(('dp', 'expert'))
- grad_w_gate: float32 [16, 2048, 1024], P('expert', 'dp')
- grad_w_up: float32 [16, 2048, 1024], P('expert', 'dp')
- grad_w_down: float32 [16, 1024, 2048], P('expert', 'dp')
The draws below stay inside these ranges and needn't reach their ends.
Inputs may be any that keep to these rules, and one draw needn't show every extreme that they name: `routes`: no expert is named by more than 96 of the 128 rows of one device, and 96 is reached. Segments come in runs of 16, one tree a run. parents[s] is -1 where s is a multiple of 16; the last segment of a run has parent s - 1; otherwise it is one of s - 1, s - 2, s - 3 that is not before the run's first segment.
All inputs are finite; a program needn't handle non-finite values.
Results may differ from the reference program's by a relative error of at most 0.04.
Values may be sent and summed in bfloat16 or wider, within the bound.
A program may use at most 384 MiB of HBM per device.

```python
import math
import jax
import jax.numpy as jnp
import numpy as np
from jax import lax

D = 2048
HEADS = 16
HEAD_DIM = 128
FF = 1024
TOP = 8
TOK_DEV = 128
EXPERTS = 16
TOKENS = 4096
GROUP_SEGS = 16
SEGS = 32
CAP = 96
N_DP = 2
N_EXPERT = 16


def draw_parents(key, part):
    segment_index = jnp.arange(SEGS, dtype=jnp.int32)
    local_index = segment_index % GROUP_SEGS
    jumps = jax.random.randint(key, (SEGS,), 0, 3, dtype=jnp.int32)
    jumps = jumps % jnp.maximum(local_index, 1)
    jumps = jnp.where(local_index == GROUP_SEGS - 1, 0, jumps)
    return jnp.where(local_index == 0, -1, segment_index - 1 - jumps).astype(jnp.int32)


def spiked(values, key, source, target, shards_of, factor):
    def block_of(axis_at):
        return (jnp.arange(values.shape[axis_at]) // (values.shape[axis_at] // shards_of)).reshape((-1,) + (1,) * (values.ndim - 1 - axis_at))

    first = jax.random.permutation(key, shards_of)[block_of(target)]
    far = (block_of(target) + shards_of // 2) % shards_of
    return jnp.where((block_of(source) == first) | (block_of(source) == far), factor * values, values)


def shard_levels(key, dims, pieces, smallest, high):
    def one(axis_at, blocks):
        steps = jax.random.uniform(jax.random.fold_in(jax.random.fold_in(key, 6), axis_at), (blocks,), jnp.float32, smallest / len(pieces), high / len(pieces))
        return jnp.repeat(jnp.exp(steps), dims[axis_at] // blocks).reshape((-1,) + (1,) * (len(dims) - axis_at - 1))

    gain = one(*pieces[0])
    for cut in pieces[1:]:
        gain = gain * one(*cut)
    return gain


def deal_out(own_key, own, number, rows, amount, top, reach, lean):
    ranking = jax.random.permutation(own_key, amount)
    crowded, usual = load_shares(amount, rows * top, reach, lean, True), load_shares(amount, rows * top, reach, lean, False)
    places = jnp.arange(amount)

    def named(sizes, rotation):
        used = int((sizes > 0).sum())
        fixed = max(1, used // 4)
        passed = fixed + (places - fixed + rotation * (used - fixed)) % max(1, amount - fixed)
        return jnp.zeros((amount,), jnp.int32).at[ranking[jnp.where(places < fixed, places, passed)]].set(jnp.asarray(sizes, jnp.int32))

    sizes = jnp.where(number % 4 == 0, named(crowded, number // 4), named(usual, number - number // 4 - 1))
    mixed = jax.random.permutation(jax.random.fold_in(own, 3), amount)
    donor, taker = mixed[0:amount // 2 * 2:2], mixed[1:amount // 2 * 2:2]
    margin = jnp.minimum(sizes[donor] - 1, reach - sizes[taker]) // 2
    margin = jnp.where((donor == ranking[0]) | (taker == ranking[0]) | (sizes[taker] == 0), 0, jnp.maximum(margin, 0))
    passed = jax.random.randint(jax.random.fold_in(own, 4), (amount // 2,), 0, 1 << 20) % (margin + 1)
    sizes = sizes.at[donor].add(-passed).at[taker].add(passed)
    items = jnp.searchsorted(jnp.cumsum(sizes), jnp.arange(rows * top), side="right").astype(jnp.int32)
    grid = items.reshape(top, rows).T
    grid = grid[jax.random.permutation(jax.random.fold_in(own, 1), rows)]
    rotation = jax.random.randint(jax.random.fold_in(own, 2), (rows, 1), 0, top)
    return jnp.take_along_axis(grid, (jnp.arange(top)[None, :] + rotation) % top, axis=1)


def load_shares(number_of, total, most, slope, full):
    loads = [(1 << 20) // math.isqrt(rank ** slope) + 1 for rank in range(1, number_of + 1)]
    largest = most if full else min(most, max(-(-total // number_of), total * loads[0] // sum(loads)))
    least = 1 if total - largest >= number_of - 1 else 0
    holding, rest = [largest] + [least] * (number_of - 1), total - largest - least * (number_of - 1)
    while rest > 0:
        movable = [i for i in range(1, number_of) if holding[i] < largest] or [i for i in range(1, number_of) if holding[i] < most]
        mass, remaining = sum([loads[i] for i in movable]), rest
        for i in movable:
            extra = min(most - holding[i], max(1, remaining * loads[i] // mass), rest)
            holding[i] = holding[i] + extra
            rest = rest - extra
    return np.array(holding)


def normal_values(own_key, extent, deviation, reach, split=(), kind=jnp.bfloat16):
    factor_of = shard_levels(own_key, extent, split, -0.22, 0.18) if split else 1.0
    values = jax.random.normal(own_key, extent, jnp.float32) * deviation * factor_of
    return jnp.minimum(jnp.maximum(values, -reach), reach).astype(kind)


def gaussian_with(key, shape, spread, bound, split, heavy, kind=jnp.bfloat16):
    array = spread * jax.random.normal(key, shape, jnp.float32)
    if split:
        array = array * shard_levels(key, shape, split, -0.22, 0.18)
    return jnp.clip(spiked(array, jax.random.fold_in(key, 3), *heavy), -bound, bound).astype(kind)


def setup_inputs(seed: int = 0) -> dict:
    streams_of = jax.random.split(jax.random.key(seed), 17)
    tokens = gaussian_with(streams_of[0], (TOKENS, D), 1.0, 6.0, ((0, 32),), (0, 1, 32, 2.75))
    attn_gain = jnp.clip(1.0 + 0.15 * jax.random.normal(streams_of[1], (D,), jnp.float32), 0.25, 1.75).astype(jnp.bfloat16)
    q_gain = jnp.clip(1.0 + 0.15 * jax.random.normal(streams_of[2], (D,), jnp.float32), 0.25, 1.75).astype(jnp.bfloat16)
    k_gain = jnp.clip(1.0 + 0.15 * jax.random.normal(streams_of[3], (D,), jnp.float32), 0.25, 1.75).astype(jnp.bfloat16)
    ffn_gain = jnp.clip(1.0 + 0.15 * jax.random.normal(streams_of[4], (D,), jnp.float32), 0.25, 1.75).astype(jnp.bfloat16)
    w_query = normal_values(streams_of[5], (D, D), D ** -0.5, 0.125, ((0, 32),))
    w_key = normal_values(streams_of[6], (D, D), D ** -0.5, 0.125, ((0, 32),))
    w_value = normal_values(streams_of[7], (D, D), D ** -0.5, 0.125, ((0, 32),))
    w_out = normal_values(streams_of[8], (D, D), ((TOK_DEV * N_EXPERT // 8) ** 0.5 * D ** -0.5), 5.0, ((0, 32),))
    router = normal_values(streams_of[9], (D, EXPERTS), (4 * D) ** -0.5, 0.0625, ((0, 32),))
    w_gate = normal_values(streams_of[10], (EXPERTS, D, FF), D ** -0.5, 0.125, ((0, 16), (1, 2)))
    w_up = normal_values(streams_of[11], (EXPERTS, D, FF), D ** -0.5, 0.125, ((0, 16), (1, 2)))
    w_down = normal_values(streams_of[12], (EXPERTS, FF, D), (EXPERTS * 1.7 * (TOP * FF) ** -0.5), 4.0, ((0, 16), (1, 2)))
    cotangent = normal_values(streams_of[13], (TOKENS, D), 1.0, 6.0, ((0, 32),))
    routes_keys = jax.random.split(jax.random.fold_in(streams_of[14], 1), TOKENS // TOK_DEV)
    routes_turns = jax.random.permutation(jax.random.fold_in(streams_of[14], 3), TOKENS // TOK_DEV)
    routes = jax.vmap(lambda own, number: deal_out(jax.random.fold_in(streams_of[14], 2), own, number, TOK_DEV, EXPERTS, TOP, CAP, 1))(routes_keys, routes_turns).reshape((TOKENS, TOP))
    parents = draw_parents(jax.random.fold_in(streams_of[16], 71), 0)
    return dict(tokens=tokens, attn_gain=attn_gain, q_gain=q_gain, k_gain=k_gain, ffn_gain=ffn_gain, w_query=w_query, w_key=w_key, w_value=w_value, w_out=w_out, router=router, w_gate=w_gate, w_up=w_up, w_down=w_down, cotangent=cotangent, routes=routes, parents=parents)


EPSILON = 1e-05
THETA = 10000.0
NEGATIVE = -1e+30

@jax.custom_vjp
def low(v):
    return lax.optimization_barrier(v.astype(jnp.bfloat16)).astype(jnp.float32)

@jax.custom_vjp
def low_back(v):
    return v

def low_keep(v):
    return (low(v), None)

def low_pass(kept, grad):
    return (grad,)

def back_keep(v):
    return (v, None)

def back_low(kept, grad):
    return (low(grad),)
low.defvjp(low_keep, low_pass)
low_back.defvjp(back_keep, back_low)

def matmul(matrix_left, matrix_right):
    return jnp.dot(matrix_left, matrix_right, precision=lax.Precision.HIGHEST, preferred_element_type=jnp.float32)

def inverse_rms(values):
    return lax.rsqrt(lax.optimization_barrier(jnp.mean(values * values, axis=-1, keepdims=True)) + EPSILON)

def ancestry(parents):
    segment_count = parents.shape[0]
    labels = jnp.arange(segment_count, dtype=jnp.int32)
    reach_table = (parents[:, None] == labels[None, :]).astype(jnp.float32)
    for doubling in range(segment_count.bit_length()):
        reach_table = jnp.minimum(reach_table + matmul(reach_table, reach_table), 1.0)
    return reach_table

def token_positions(parents):
    reach_table = ancestry(parents)
    seg_depth = lax.optimization_barrier(jnp.sum(reach_table, axis=1)).astype(jnp.int32)
    row_index = jnp.arange(TOKENS, dtype=jnp.int32)
    positions = (seg_depth[row_index // TOK_DEV] * TOK_DEV + row_index % TOK_DEV).astype(jnp.float32)
    return (positions, reach_table)

def rotate(values, positions, direction):
    row_count = values.shape[0]
    half_dim = HEAD_DIM // 2
    frequencies = THETA ** (-2.0 * jnp.arange(half_dim, dtype=jnp.float32) / HEAD_DIM)
    angles = positions[:, None] * frequencies[None, :]
    cosine = jnp.cos(angles)[:, None, :]
    sine = direction * jnp.sin(angles)[:, None, :]
    split_heads = values.reshape(row_count, HEADS, HEAD_DIM)
    first_half = split_heads[..., :half_dim]
    second_half = split_heads[..., half_dim:]
    turned = jnp.concatenate([first_half * cosine - second_half * sine, second_half * cosine + first_half * sine], axis=-1)
    return turned.reshape(row_count, D)

def attention(queries, key_rows, value_rows, reach_table):
    span = N_EXPERT * TOK_DEV
    block_rows = math.gcd(512, span)
    seen_table = reach_table + jnp.eye(SEGS, dtype=jnp.float32)
    score_scale = HEAD_DIM ** (-0.5)

    def one_group(group_pack):
        group_queries, group_keys, group_values, first_row = group_pack
        key_heads = group_keys.reshape(span, HEADS, HEAD_DIM)
        value_heads = group_values.reshape(span, HEADS, HEAD_DIM)
        key_index = first_row + jnp.arange(span, dtype=jnp.int32)
        key_segment = key_index // TOK_DEV
        key_place = key_index % TOK_DEV

        def one_block(block_pack):
            query_block, start_row = block_pack
            query_index = start_row + jnp.arange(block_rows, dtype=jnp.int32)
            query_segment = query_index // TOK_DEV
            query_place = query_index % TOK_DEV
            ancestor = seen_table[query_segment][:, key_segment] > 0.5
            causal = (query_segment[:, None] != key_segment[None, :]) | (key_place[None, :] <= query_place[:, None])
            allowed = ancestor & causal
            raw_scores = jnp.einsum('qhd,khd->hqk', query_block.reshape(block_rows, HEADS, HEAD_DIM), key_heads, precision=lax.Precision.HIGHEST) * score_scale
            scores = jnp.where(allowed[None], low_back(raw_scores), NEGATIVE)
            weights = low(jax.nn.softmax(scores, axis=-1))
            result = jnp.einsum('hqk,khd->qhd', weights, value_heads, precision=lax.Precision.HIGHEST)
            return result.reshape(block_rows, D)
        block_count = span // block_rows
        starts = first_row + block_rows * jnp.arange(block_count, dtype=jnp.int32)
        blocks = group_queries.reshape(block_count, block_rows, D)
        return lax.map(jax.checkpoint(one_block), (blocks, starts)).reshape(span, D)
    firsts = span * jnp.arange(N_DP, dtype=jnp.int32)
    grouped = (queries.reshape(N_DP, span, D), key_rows.reshape(N_DP, span, D), value_rows.reshape(N_DP, span, D), firsts)
    return lax.map(one_group, grouped).reshape(TOKENS, D)

def experts_mix(normed_two, mix_weights, w_gate, w_up, w_down):
    rows_block = math.gcd(1024, TOKENS)

    def one_block(block_pack):
        block_input, block_mix = block_pack

        def one_expert(running_sum, expert_pack):
            gate_weight, up_weight, down_weight, weight_column = expert_pack
            copied = low_back(block_input)
            gate_pre = low_back(matmul(copied, gate_weight))
            up_pre = low_back(matmul(copied, up_weight))
            hidden = low_back(low(jax.nn.silu(gate_pre) * up_pre))
            result = low_back(low(matmul(hidden, down_weight)))
            return (running_sum + weight_column[:, None] * result, None)
        start_sum = jnp.zeros(block_input.shape, block_input.dtype)
        running_sum, unused = lax.scan(jax.checkpoint(one_expert), start_sum, (w_gate, w_up, w_down, block_mix.T))
        return running_sum
    block_count = TOKENS // rows_block
    blocks = (normed_two.reshape(block_count, rows_block, D), mix_weights.reshape(block_count, rows_block, EXPERTS))
    return lax.map(jax.checkpoint(one_block), blocks).reshape(TOKENS, D)

def layer(packed, chosen, positions, reach_table):
    token_f, attn_gain, q_gain, k_gain, ffn_gain, w_query, w_key, w_value, w_out, router, w_gate, w_up, w_down = packed
    normed = low(token_f * inverse_rms(token_f) * attn_gain)
    query_pre = low_back(matmul(normed, w_query))
    key_pre = low_back(matmul(normed, w_key))
    value_rows = low_back(low(matmul(normed, w_value)))
    queries = low(rotate(query_pre * inverse_rms(query_pre) * q_gain, positions, 1.0))
    key_rows = low(rotate(key_pre * inverse_rms(key_pre) * k_gain, positions, 1.0))
    mixed = low_back(low(attention(queries, key_rows, value_rows, reach_table)))
    residual = token_f + low_back(matmul(mixed, w_out))
    normed_two = low(residual * inverse_rms(residual) * ffn_gain)
    logits = low_back(matmul(normed_two, router))
    router_probs = jax.nn.softmax(logits, axis=-1)
    expert_sum = experts_mix(normed_two, router_probs * chosen, w_gate, w_up, w_down)
    return residual + expert_sum

def reference(tokens, attn_gain, q_gain, k_gain, ffn_gain, w_query, w_key, w_value, w_out, router, w_gate, w_up, w_down, cotangent, routes, parents):
    positions, reach_table = token_positions(parents)
    expert_labels = jnp.arange(EXPERTS, dtype=jnp.int32)
    chosen = lax.optimization_barrier(jnp.sum((routes[:, :, None] == expert_labels[None, None, :]).astype(jnp.float32), axis=1))
    floats = (tokens.astype(jnp.float32), attn_gain.astype(jnp.float32), q_gain.astype(jnp.float32), k_gain.astype(jnp.float32), ffn_gain.astype(jnp.float32), w_query.astype(jnp.float32), w_key.astype(jnp.float32), w_value.astype(jnp.float32), w_out.astype(jnp.float32), router.astype(jnp.float32), w_gate.astype(jnp.float32), w_up.astype(jnp.float32), w_down.astype(jnp.float32))

    def forward(packed):
        return layer(packed, chosen, positions, reach_table)
    result, pullback = jax.vjp(forward, floats)
    grads = pullback(cotangent.astype(jnp.float32))[0]
    return (result.astype(jnp.bfloat16), grads[0], grads[1], grads[2], grads[3], grads[4], grads[5], grads[6], grads[7], grads[8], grads[9], grads[10], grads[11], grads[12])
```

```python
import functools
import math

import jax
import jax.numpy as jnp
from jax import lax
from jax.experimental import pallas as pl
from jax.experimental.pallas import tpu as pltpu
from jax.sharding import PartitionSpec as P

HEAD_DIM = 128
EPSILON = 1e-05
THETA = 10000.0
NEGATIVE = -1e30
BOTH = ("dp", "expert")
F32 = jnp.float32
BF16 = jnp.bfloat16
MESH = pl.DeviceIdType.MESH


def mm(a, b):
    return lax.dot_general(a, b, (((1,), (0,)), ((), ())), preferred_element_type=F32)


def mm_t(a, b):
    return lax.dot_general(a, b, (((1,), (1,)), ((), ())), preferred_element_type=F32)


def t_mm(a, b):
    return lax.dot_general(a, b, (((0,), (0,)), ((), ())), preferred_element_type=F32)


def inverse_rms(values):
    return lax.rsqrt(jnp.mean(values * values, axis=-1, keepdims=True) + EPSILON)


def turn(values, cosine, sine):
    half = HEAD_DIM // 2
    a, b = values[:, :half], values[:, half:]
    return jnp.concatenate([a * cosine - b * sine, b * cosine + a * sine], axis=-1)


def ancestry(parents):
    count = parents.shape[0]
    labels = jnp.arange(count, dtype=jnp.int32)
    table = (parents[:, None] == labels[None, :]).astype(F32)
    for _ in range((count - 1).bit_length()):
        product = jnp.dot(table, table, precision=lax.Precision.HIGHEST, preferred_element_type=F32)
        table = jnp.minimum(table + product, 1.0)
    return table


def spot():
    me = lax.axis_index("expert")
    return me // 4, (me // 2) % 2, me % 2

def at(z, x, c):
    return (z * 2 + x) * 2 + c

def greet(z, x, c, far):
    barrier = pltpu.get_barrier_semaphore()
    def hello(e):
        pl.semaphore_signal(barrier, inc=1, device_id={"expert": e}, device_id_type=MESH)
    hello(at(z, x, 1 - c)); hello(at(z, 1 - x, c))
    @pl.when(z > 0)
    def _(): hello(at(z - 1, x, c))
    @pl.when(z < far)
    def _(): hello(at(z + 1, x, c))
    count = 2 + jnp.where(z > 0, 1, 0) + jnp.where(z < far, 1, 0)
    pl.semaphore_wait(barrier, count)

def gather_kernel(zs, in_ref, out_ref, send, recv, local):
    z, x, c = spot()
    far = zs - 1
    me = at(z, x, c)
    greet(z, x, c, far)
    mine = pltpu.make_async_copy(in_ref, out_ref.at[me], local)
    mine.start()
    def copy(src, block, kind, e):
        return pltpu.make_async_remote_copy(
            src_ref=src, dst_ref=out_ref.at[block], send_sem=send.at[kind, block],
            recv_sem=recv.at[block], device_id={"expert": e}, device_id_type=MESH)
    SIB, X, UP, DOWN = range(4)
    def forward(src, block, zz):
        @pl.when((zz <= z) & (z < far))
        def _(): copy(src, block, UP, at(z + 1, x, c)).start()
        @pl.when((zz >= z) & (z > 0))
        def _(): copy(src, block, DOWN, at(z - 1, x, c)).start()
        copy(src, block, X, at(z, 1 - x, c)).start()
        copy(src, block, SIB, at(z, x, 1 - c)).start()
    def arrived(block):
        copy(in_ref, block, SIB, at(z, x, 1 - c)).wait_recv()
    forward(in_ref, me, z)
    def across(zz):
        block = at(zz, 1 - x, c)
        arrived(block)
        copy(out_ref.at[block], block, SIB, at(z, x, 1 - c)).start()
    across(z)
    for d in range(1, zs):
        for zz, ok in ((z - d, z >= d), (z + d, z + d <= far)):
            @pl.when(ok)
            def _():
                block = at(zz, x, c)
                arrived(block)
                forward(out_ref.at[block], block, zz)
        for zz, ok in ((z - d, z >= d), (z + d, z + d <= far)):
            @pl.when(ok)
            def _(): across(zz)
    for zz in range(zs):
        for xx in range(2):
            arrived(at(zz, xx, 1 - c))
    mine.wait()
    def sent(block, kind):
        copy(in_ref, block, kind, at(z, x, 1 - c)).wait_send()
    for zz in range(zs):
        block = at(zz, x, c)
        sent(block, X); sent(block, SIB); sent(at(zz, 1 - x, c), SIB)
        @pl.when((zz <= z) & (z < far))
        def _(): sent(block, UP)
        @pl.when((zz >= z) & (z > 0))
        def _(): sent(block, DOWN)

def gather(values, group, cid):
    return pl.pallas_call(
        functools.partial(gather_kernel, group // 4),
        out_shape=jax.ShapeDtypeStruct((group, *values.shape), values.dtype),
        in_specs=[pl.BlockSpec(memory_space=pl.ANY)],
        out_specs=pl.BlockSpec(memory_space=pl.ANY),
        scratch_shapes=[pltpu.SemaphoreType.DMA((4, group)), pltpu.SemaphoreType.DMA((group,)), pltpu.SemaphoreType.DMA],
        compiler_params=pltpu.CompilerParams(collective_id=cid, has_side_effects=True),
    )(values)

def scatter_kernel(zs, in_ref, out_ref, r_sib, r_x, r_z, s_x, s_z, send, recv):
    z, x, c = spot()
    far = zs - 1
    greet(z, x, c, far)
    SIB, X, UP, DOWN = range(4)
    def to_sibling(zz, xx):
        return pltpu.make_async_remote_copy(
            src_ref=in_ref.at[at(zz, xx, 1 - c)], dst_ref=r_sib.at[zz * 2 + xx],
            send_sem=send.at[SIB, zz * 2 + xx], recv_sem=recv.at[SIB, zz * 2 + xx],
            device_id={"expert": at(z, x, 1 - c)}, device_id_type=MESH)
    def to_x(zz):
        return pltpu.make_async_remote_copy(
            src_ref=s_x.at[zz], dst_ref=r_x.at[zz], send_sem=send.at[X, zz], recv_sem=recv.at[X, zz],
            device_id={"expert": at(z, 1 - x, c)}, device_id_type=MESH)
    def along(zz, kind, e):
        return pltpu.make_async_remote_copy(
            src_ref=s_z.at[zz], dst_ref=r_z.at[kind - UP, zz], send_sem=send.at[kind, zz], recv_sem=recv.at[kind, zz],
            device_id={"expert": e}, device_id_type=MESH)
    def up(zz): return along(zz, UP, at(z + 1, x, c))
    def down(zz): return along(zz, DOWN, at(z - 1, x, c))
    def order(f):
        for d in range(far, 0, -1):
            @pl.when(z + d <= far)
            def _(): f(z + d)
            @pl.when(z >= d)
            def _(): f(z - d)
        f(z)
    order(lambda zz: to_sibling(zz, 1 - x).start())
    order(lambda zz: to_sibling(zz, x).start())
    def cross(zz):
        to_sibling(zz, 1 - x).wait_recv()
        s_x[zz] = (in_ref[at(zz, 1 - x, c)].astype(F32) + r_sib[zz * 2 + 1 - x].astype(F32)).astype(BF16)
        to_x(zz).start()
    order(cross)
    def finish(zz):
        to_sibling(zz, x).wait_recv()
        to_x(zz).wait_recv()
        def here():
            return in_ref[at(zz, x, c)].astype(F32) + r_sib[zz * 2 + x].astype(F32) + r_x[zz].astype(F32)
        @pl.when(zz > z)
        def _():
            @pl.when(z > 0)
            def _():
                up(zz).wait_recv()
                s_z[zz] = (here() + r_z[0, zz].astype(F32)).astype(BF16)
            @pl.when(z == 0)
            def _(): s_z[zz] = here().astype(BF16)
            up(zz).start()
        @pl.when(zz < z)
        def _():
            @pl.when(z < far)
            def _():
                down(zz).wait_recv()
                s_z[zz] = (here() + r_z[1, zz].astype(F32)).astype(BF16)
            @pl.when(z == far)
            def _(): s_z[zz] = here().astype(BF16)
            down(zz).start()
        @pl.when(zz == z)
        def _():
            out_ref[...] = here()
            @pl.when(z > 0)
            def _():
                up(zz).wait_recv()
                out_ref[...] += r_z[0, zz].astype(F32)
            @pl.when(z < far)
            def _():
                down(zz).wait_recv()
                out_ref[...] += r_z[1, zz].astype(F32)
    order(finish)
    for zz in range(zs):
        for xx in range(2):
            to_sibling(zz, xx).wait_send()
        to_x(zz).wait_send()
        @pl.when(zz > z)
        def _(): up(zz).wait_send()
        @pl.when(zz < z)
        def _(): down(zz).wait_send()

def scatter(values, cid):
    group, rows, width = values.shape
    zs = group // 4
    buf = lambda *n: pltpu.VMEM((*n, rows, width), BF16)
    return pl.pallas_call(
        functools.partial(scatter_kernel, zs),
        out_shape=jax.ShapeDtypeStruct((rows, width), F32),
        in_specs=[pl.BlockSpec(memory_space=pltpu.VMEM)],
        out_specs=pl.BlockSpec(memory_space=pltpu.VMEM),
        scratch_shapes=[buf(2 * zs), buf(zs), buf(2, zs), buf(zs), buf(zs),
            pltpu.SemaphoreType.DMA((4, 2 * zs)), pltpu.SemaphoreType.DMA((4, 2 * zs))],
        compiler_params=pltpu.CompilerParams(collective_id=cid, has_side_effects=True, vmem_limit_bytes=48 * 2**20),
    )(values)

def swap_kernel(axes, sizes, in_ref, out_ref, send, recv, local):
    count = 1
    for size in sizes:
        count *= size
    me = jnp.int32(0)
    for axis, size in zip(axes, sizes):
        me = me * size + lax.axis_index(axis)
    same = in_ref.shape[0] == 1

    def spread(d):
        where = {}
        for axis, size in zip(axes[::-1], sizes[::-1]):
            where[axis] = d % size
            d = d // size
        return where

    barrier = pltpu.get_barrier_semaphore()

    def hello(k, carry):
        pl.semaphore_signal(
            barrier, inc=1, device_id=spread((me + k) % count), device_id_type=MESH
        )
        return carry

    lax.fori_loop(1, count, hello, 0)
    pl.semaphore_wait(barrier, count - 1)

    def copy(k):
        d = (me + k) % count
        return pltpu.make_async_remote_copy(
            src_ref=in_ref.at[0 if same else d],
            dst_ref=out_ref.at[me],
            send_sem=send.at[k],
            recv_sem=recv.at[me],
            device_id=spread(d),
            device_id_type=MESH,
        )

    def start(k, carry):
        copy(k).start()
        return carry

    lax.fori_loop(1, count, start, 0)
    mine = pltpu.make_async_copy(in_ref.at[0 if same else me], out_ref.at[me], local)
    mine.start()
    mine.wait()

    def finish(k, carry):
        d = (me + k) % count
        pltpu.make_async_remote_copy(
            src_ref=in_ref.at[0],
            dst_ref=out_ref.at[d],
            send_sem=send.at[k],
            recv_sem=recv.at[d],
            device_id=spread(d),
            device_id_type=MESH,
        ).wait_recv()
        copy(k).wait_send()
        return carry

    lax.fori_loop(1, count, finish, 0)


def swap(values, axes, cid):
    sizes = tuple(lax.axis_size(axis) for axis in axes)
    count = 1
    for size in sizes:
        count *= size
    return pl.pallas_call(
        functools.partial(swap_kernel, axes, sizes),
        out_shape=jax.ShapeDtypeStruct((count, *values.shape[1:]), values.dtype),
        in_specs=[pl.BlockSpec(memory_space=pltpu.VMEM)],
        out_specs=pl.BlockSpec(memory_space=pltpu.VMEM),
        scratch_shapes=[
            pltpu.SemaphoreType.DMA((count,)),
            pltpu.SemaphoreType.DMA((count,)),
            pltpu.SemaphoreType.DMA,
        ],
        compiler_params=pltpu.CompilerParams(
            collective_id=cid, has_side_effects=True, vmem_limit_bytes=32 * 2**20
        ),
    )(values)


SCALE = HEAD_DIM ** (-0.5)


def attention(queries, mask, keys, values):
    scores = jnp.where(mask, mm_t(queries, keys) * SCALE, NEGATIVE)
    row_max = jnp.max(scores, axis=-1, keepdims=True)
    weights = jnp.exp(scores - row_max)
    total = jnp.sum(weights, axis=-1, keepdims=True)
    attn = mm(weights.astype(BF16), values) / total
    return attn, row_max + jnp.log(total)


def attention_back(queries, mask, log_total, mixed_grad, row_delta, keys, values):
    probs = jnp.exp(jnp.where(mask, mm_t(queries, keys) * SCALE - log_total, NEGATIVE))
    score_grad = (probs * (mm_t(mixed_grad, values) - row_delta)).astype(BF16)
    query_grad = mm(score_grad, keys) * SCALE
    key_grad = t_mm(score_grad, queries) * SCALE
    return query_grad, key_grad, t_mm(probs.astype(BF16), mixed_grad)


def expert_step(rows_in, cot_in, gates, gate_w, up_w, down_w):
    cot_in = cot_in.astype(F32)
    gate_pre = mm(rows_in, gate_w)
    up_pre = mm(rows_in, up_w)
    sig = jax.nn.sigmoid(gate_pre)
    silu = gate_pre * sig
    hidden = (silu * up_pre).astype(BF16)
    expert_out = mm(hidden, down_w).astype(BF16).astype(F32)
    sent_out = (gates * expert_out).astype(BF16)
    gate_grad = jnp.sum(cot_in * expert_out, axis=-1)
    out_grad = (gates * cot_in).astype(BF16)
    hidden_grad = mm_t(out_grad, down_w).astype(BF16).astype(F32)
    gate_pre_grad = (hidden_grad * up_pre * sig * (1.0 + gate_pre * (1.0 - sig))).astype(BF16)
    up_pre_grad = (hidden_grad * silu).astype(BF16)
    row_grad = (mm_t(gate_pre_grad, gate_w) + mm_t(up_pre_grad, up_w)).astype(BF16)
    sums = (t_mm(rows_in, gate_pre_grad), t_mm(rows_in, up_pre_grad), t_mm(hidden, out_grad))
    return (sent_out, gate_grad, row_grad), sums


def per_device(
    tokens, attn_gain, q_gain, k_gain, ffn_gain, w_query, w_key, w_value, w_out, router,
    w_gate, w_up, w_down, cotangent, routes, parents,
):
    rows, width = tokens.shape
    heads = width // HEAD_DIM
    group = lax.axis_size("expert")
    n_dp = lax.axis_size("dp")
    devices = group * n_dp
    share = max(1, group // heads)
    tree_rows = group * rows
    own_rows = tree_rows // share
    shard = w_query.shape[0]
    dp = lax.axis_index("dp")
    me = lax.axis_index("expert")
    head = me // share
    part = me % share
    peers = [[h * share + j for h in range(heads)] for j in range(share)]
    siblings = [[h * share + j for j in range(share)] for h in range(heads)]

    reach = ancestry(parents)
    start = dp * group
    tree = lax.dynamic_slice(reach, (start, start), (group, group))
    depth = jnp.sum(lax.dynamic_slice_in_dim(reach, start, group, 0), axis=1)
    sees = tree + jnp.eye(group, dtype=F32)
    own_segs = own_rows // rows
    first_seg = part * own_segs
    my_depth = lax.dynamic_slice_in_dim(depth, first_seg, own_segs, 0)
    my_sees = lax.dynamic_slice_in_dim(sees, first_seg, own_segs, 0)
    place = jnp.arange(rows, dtype=F32)
    positions = (my_depth[:, None] * rows + place[None, :]).reshape(own_rows)
    frequencies = THETA ** (-2.0 * jnp.arange(HEAD_DIM // 2, dtype=F32) / HEAD_DIM)
    angles = positions[:, None] * frequencies[None, :]
    cosine, sine = jnp.cos(angles), jnp.sin(angles)
    key_index = jnp.arange(tree_rows, dtype=jnp.int32)
    query_index = first_seg * rows + jnp.arange(own_rows, dtype=jnp.int32)
    seen = jnp.repeat(jnp.repeat(my_sees, rows, axis=0), rows, axis=1) > 0.5
    mask = seen & (key_index[None, :] <= query_index[:, None])

    def own_part(values):
        return lax.dynamic_slice_in_dim(values, first_seg * rows, own_rows, 0)

    def head_sum(values, cid):
        if share > 1:
            return lax.psum(values, "expert", axis_index_groups=peers)
        return jnp.sum(swap(values[None], ("expert",), cid), axis=0)

    def tree_gather(values, cid):
        if share > 1:
            return lax.all_gather(values, "expert", axis=0, tiled=True)
        return gather(values, group, cid).reshape(tree_rows, -1)

    def tree_scatter(values, cid):
        if share > 1:
            return lax.psum_scatter(values, "expert", scatter_dimension=0, tiled=True).astype(F32)
        return scatter(values.reshape(group, rows, -1), cid)

    def both_swap(values, cid):
        if share > 1:
            return lax.all_to_all(values, BOTH, 0, 0, tiled=True)
        return swap(values, BOTH, cid)

    def expert_swap(values, cid):
        if share > 1:
            return lax.all_to_all(values, "expert", 0, 0, tiled=True)
        return swap(values, ("expert",), cid)

    others = [(d, (d + 1) % n_dp) for d in range(n_dp)]

    def dp_join(values):
        if n_dp != 2:
            return lax.all_gather(values, "dp", axis=0, tiled=True)
        other = lax.ppermute(values, "dp", others)
        return jnp.where(
            dp == 0, jnp.concatenate([values, other]), jnp.concatenate([other, values])
        )

    def dp_sum(values):
        if n_dp != 2:
            return lax.psum_scatter(values, "dp", scatter_dimension=0, tiled=True)
        halves = values.reshape(2, values.shape[0] // 2, -1)
        theirs = lax.dynamic_index_in_dim(halves, 1 - dp, 0, keepdims=False)
        ours = lax.dynamic_index_in_dim(halves, dp, 0, keepdims=False)
        return ours.astype(F32) + lax.ppermute(theirs, "dp", others).astype(F32)

    gains = lax.all_gather(
        jnp.stack([attn_gain, q_gain, k_gain, ffn_gain], axis=1), BOTH, axis=0, tiled=True
    ).astype(F32)
    attn_g, query_g, key_g, ffn_g = gains[:, 0], gains[:, 1], gains[:, 2], gains[:, 3]
    my_query_g = lax.dynamic_slice_in_dim(query_g, head * HEAD_DIM, HEAD_DIM, 0)[None, :]
    my_key_g = lax.dynamic_slice_in_dim(key_g, head * HEAD_DIM, HEAD_DIM, 0)[None, :]
    by_head = jnp.stack([w_query, w_key, w_value], axis=1).reshape(shard, 3, heads, HEAD_DIM)
    by_head = by_head.transpose(2, 0, 1, 3).reshape(1, heads, 1, shard, 3 * HEAD_DIM)
    by_head = jnp.broadcast_to(by_head, (n_dp, heads, share, shard, 3 * HEAD_DIM))
    w_head = both_swap(by_head.reshape(devices, shard, 3 * HEAD_DIM), 0).reshape(
        width, 3 * HEAD_DIM
    )
    out_w = lax.all_gather(w_out, BOTH, axis=0, tiled=True)
    out_head = lax.dynamic_slice_in_dim(out_w, head * HEAD_DIM, HEAD_DIM, 0)
    router_w = lax.all_gather(router, BOTH, axis=0, tiled=True)
    gate_w = dp_join(w_gate[0])
    up_w = dp_join(w_up[0])
    down_w = dp_join(w_down[0])

    token_f = tokens.astype(F32)
    first_scale = inverse_rms(token_f)
    normed = (token_f * first_scale * attn_g[None, :]).astype(BF16)
    normed_all = own_part(tree_gather(normed, 1))
    pre = mm(normed_all, w_head)
    query_pre, key_pre = pre[:, :HEAD_DIM], pre[:, HEAD_DIM : 2 * HEAD_DIM]
    values = pre[:, 2 * HEAD_DIM :].astype(BF16)
    squares = jnp.stack([jnp.sum(query_pre**2, axis=-1), jnp.sum(key_pre**2, axis=-1)])
    scales = lax.rsqrt(head_sum(squares, 2) / width + EPSILON)
    query_scale, key_scale = scales[0][:, None], scales[1][:, None]
    queries = turn(query_pre * query_scale * my_query_g, cosine, sine).astype(BF16)
    keys = turn(key_pre * key_scale * my_key_g, cosine, sine).astype(BF16)
    if share > 1:
        keys_all = lax.all_gather(keys, "expert", axis=0, tiled=True, axis_index_groups=siblings)
        values_all = lax.all_gather(values, "expert", axis=0, tiled=True, axis_index_groups=siblings)
    else:
        keys_all, values_all = keys, values
    turns = max(1, tree_rows // 2048)

    def cut_rows(values):
        return values.reshape(turns, own_rows // turns, -1)

    def attend(cut):
        return attention(*cut, keys_all, values_all)

    if turns == 1:
        attn, log_total = attention(queries, mask, keys_all, values_all)
    else:
        attn, log_total = lax.map(attend, (cut_rows(queries), cut_rows(mask)))
        attn, log_total = attn.reshape(own_rows, HEAD_DIM), log_total.reshape(own_rows, 1)
    mixed_head = attn.astype(BF16)

    def to_owners(block):
        cut = block.reshape(own_segs, rows, -1)
        if share > 1:
            cut = lax.dynamic_update_slice_in_dim(
                jnp.zeros((group, *cut.shape[1:]), cut.dtype), cut, first_seg, 0
            )
        got = expert_swap(cut, 3)
        if share > 1:
            got = jnp.sum(got.reshape(heads, share, rows, -1), axis=1, dtype=cut.dtype)
        return got

    mixed = to_owners(mixed_head).transpose(1, 0, 2).reshape(rows, width)
    residual = token_f + mm(mixed, out_w)
    second_scale = inverse_rms(residual)
    normed_two = (residual * second_scale * ffn_g[None, :]).astype(BF16)
    logits = mm(normed_two, router_w)
    router_probs = jax.nn.softmax(logits, axis=-1)
    experts = router_w.shape[1]
    labels = jnp.arange(experts, dtype=jnp.int32)
    routed = jnp.any(routes[:, :, None] == labels[None, None, :], axis=1)
    gates_own = jnp.where(routed, router_probs, 0.0)
    gates = expert_swap(gates_own.T[:, None], 4).reshape(tree_rows, 1)

    rows_in = tree_gather(normed_two, 5)
    cot_in = lax.all_gather(cotangent, "expert", axis=0, tiled=True)
    pieces = max(1, tree_rows // 2048)
    if pieces == 1:
        (sent_out, gate_grad, row_grad), sums = expert_step(
            rows_in, cot_in, gates, gate_w, up_w, down_w
        )
    else:

        def expert_turn(sums, cut):
            result, more = expert_step(*cut, gate_w, up_w, down_w)
            return tuple(s + m for s, m in zip(sums, more)), result

        zeros = tuple(jnp.zeros(w.shape, F32) for w in (gate_w, up_w, down_w))
        cuts = tuple(v.reshape(pieces, -1, v.shape[1]) for v in (rows_in, cot_in, gates))
        sums, results = lax.scan(expert_turn, zeros, cuts)
        sent_out, gate_grad, row_grad = (
            r.reshape(tree_rows, *r.shape[2:]) for r in results
        )
    gate_w_grad, up_w_grad, down_w_grad = (s.astype(BF16) for s in sums)
    combined = lax.psum_scatter(sent_out, "expert", scatter_dimension=0, tiled=True)
    output = (residual + combined.astype(F32)).astype(BF16)
    gate_grad_own = expert_swap(gate_grad.reshape(group, 1, rows), 6).reshape(group, rows).T
    expert_grad = tree_scatter(row_grad, 7)
    grad_gate, grad_up, grad_down = (
        dp_sum(g).astype(F32)[None]
        for g in (gate_w_grad, up_w_grad, down_w_grad)
    )

    prob_grad = jnp.where(routed, gate_grad_own, 0.0)
    logit_grad = (
        router_probs * (prob_grad - jnp.sum(router_probs * prob_grad, axis=-1, keepdims=True))
    ).astype(BF16)
    router_grad = t_mm(normed_two, logit_grad)
    normed_two_grad = expert_grad + mm_t(logit_grad, router_w)
    ffn_gain_grad = jnp.sum(normed_two_grad * residual * second_scale, axis=0)
    weighted = normed_two_grad * ffn_g[None, :]
    residual_grad = (
        cotangent.astype(F32)
        + second_scale * weighted
        - residual * second_scale**3 * jnp.mean(weighted * residual, axis=-1, keepdims=True)
    )
    proj_grad = residual_grad.astype(BF16)

    proj_all = own_part(tree_gather(proj_grad, 8))
    mixed_grad = mm_t(proj_all, out_head).astype(BF16)
    out_w_grad = t_mm(mixed_head, proj_all)
    row_delta = jnp.sum(mixed_grad.astype(F32) * attn, axis=-1, keepdims=True)
    back_args = (queries, mask, log_total, mixed_grad, row_delta)
    if turns == 1:
        query_grad, key_grad, value_grad = attention_back(*back_args, keys_all, values_all)
    else:

        def attention_turn(sums, cut):
            first, *more = attention_back(*cut, keys_all, values_all)
            return tuple(s + m for s, m in zip(sums, more)), first

        zeros = jnp.zeros((tree_rows, HEAD_DIM), F32)
        (key_grad, value_grad), query_grad = lax.scan(
            attention_turn, (zeros, zeros), tuple(cut_rows(v) for v in back_args)
        )
        query_grad = query_grad.reshape(own_rows, HEAD_DIM)
    if share > 1:
        key_grad = lax.psum_scatter(
            key_grad, "expert", scatter_dimension=0, tiled=True, axis_index_groups=siblings
        )
        value_grad = lax.psum_scatter(
            value_grad, "expert", scatter_dimension=0, tiled=True, axis_index_groups=siblings
        )
    query_turned = turn(query_grad, cosine, -sine)
    key_turned = turn(key_grad, cosine, -sine)
    dots = jnp.stack(
        [
            jnp.sum(query_turned * my_query_g * query_pre, axis=-1),
            jnp.sum(key_turned * my_key_g * key_pre, axis=-1),
        ]
    )
    means = head_sum(dots, 9) / width
    query_low = query_scale * my_query_g * query_turned - query_pre * query_scale**3 * means[0][:, None]
    key_low = key_scale * my_key_g * key_turned - key_pre * key_scale**3 * means[1][:, None]
    low = jnp.concatenate([query_low, key_low, value_grad], axis=1).astype(BF16)
    query_gain_grad = jnp.sum(query_turned * query_pre * query_scale, axis=0)
    key_gain_grad = jnp.sum(key_turned * key_pre * key_scale, axis=0)
    normed_part = mm_t(low, w_head).astype(BF16)
    if share > 1:
        normed_part = lax.dynamic_update_slice_in_dim(
            jnp.zeros((tree_rows, width), BF16), normed_part, first_seg * rows, 0
        )
    normed_grad = tree_scatter(normed_part, 10)
    attn_gain_grad = jnp.sum(normed_grad * token_f * first_scale, axis=0)
    weighted = normed_grad * attn_g[None, :]
    token_grad = (
        residual_grad
        + first_scale * weighted
        - token_f * first_scale**3 * jnp.mean(weighted * token_f, axis=-1, keepdims=True)
    )

    head_grad = t_mm(normed_all, low)
    got = both_swap(head_grad.reshape(devices, shard, 3 * HEAD_DIM), 11).reshape(n_dp, heads, share, shard, 3, HEAD_DIM)
    got = jnp.sum(got, axis=(0, 2)).transpose(2, 1, 0, 3).reshape(3, shard, width)
    shards_a_head = HEAD_DIM // shard
    source = dp * share + part
    flat = [(d, h * share + j) for d in range(n_dp) for h in range(heads) for j in range(share)]
    grad_out = jnp.zeros((shard, width), F32)
    for turn_index in range(shards_a_head):
        pairs = []
        for d, e in flat:
            s = d * share + e % share
            target = (e // share) * shards_a_head + (s + turn_index) % shards_a_head
            pairs.append((d * group + e, target))
        block = lax.dynamic_slice_in_dim(
            out_w_grad, ((source + turn_index) % shards_a_head) * shard, shard, 0
        )
        grad_out = grad_out + lax.ppermute(block, BOTH, pairs)
    head_gains = jnp.stack([query_gain_grad, key_gain_grad], axis=1)
    head_gains = lax.dynamic_update_slice_in_dim(
        jnp.zeros((width, 2), F32), head_gains, head * HEAD_DIM, 0
    )
    small = jnp.concatenate(
        [router_grad, attn_gain_grad[:, None], head_gains, ffn_gain_grad[:, None]], axis=1
    )
    small = jnp.sum(both_swap(small.reshape(devices, shard, -1), 12), axis=0)
    return (
        output,
        token_grad,
        small[:, experts],
        small[:, experts + 1],
        small[:, experts + 2],
        small[:, experts + 3],
        got[0],
        got[1],
        got[2],
        grad_out,
        small[:, :experts],
        grad_gate,
        grad_up,
        grad_down,
    )


def solution(mesh):
    row, vec = P(BOTH, None), P(BOTH)
    expert = P("expert", "dp", None)
    return jax.shard_map(
        per_device,
        mesh=mesh,
        in_specs=(row, vec, vec, vec, vec, row, row, row, row, row, expert, expert, expert, row, row, P()),
        out_specs=(row, row, vec, vec, vec, vec, row, row, row, row, row, expert, expert, expert),
        check_vma=False,
    )
```

```python
import functools
import math

import jax
import jax.numpy as jnp
from jax import lax
from jax.experimental import pallas as pl
from jax.experimental.pallas import tpu as pltpu
from jax.sharding import PartitionSpec as P

HEAD_DIM = 128
HEADS = 16
EPSILON = 1e-05
THETA = 10000.0
NEGATIVE = -1e30
BOTH = ("dp", "expert")
F32 = jnp.float32
BF16 = jnp.bfloat16
MESH = pl.DeviceIdType.MESH


def mm(a, b):
    return lax.dot_general(a, b, (((1,), (0,)), ((), ())), preferred_element_type=F32)


def mm_t(a, b):
    return lax.dot_general(a, b, (((1,), (1,)), ((), ())), preferred_element_type=F32)


def t_mm(a, b):
    return lax.dot_general(a, b, (((0,), (0,)), ((), ())), preferred_element_type=F32)


def inverse_rms(values):
    return lax.rsqrt(jnp.mean(values * values, axis=-1, keepdims=True) + EPSILON)


def turn(values, cosine, sine):
    half = HEAD_DIM // 2
    a, b = values[:, :half], values[:, half:]
    return jnp.concatenate([a * cosine - b * sine, b * cosine + a * sine], axis=-1)


def ancestry(parents):
    count = parents.shape[0]
    labels = jnp.arange(count, dtype=jnp.int32)
    table = (parents[:, None] == labels[None, :]).astype(F32)
    for _ in range((count - 1).bit_length()):
        product = jnp.dot(table, table, precision=lax.Precision.HIGHEST, preferred_element_type=F32)
        table = jnp.minimum(table + product, 1.0)
    return table


SCALE = HEAD_DIM ** (-0.5)


SIB, ACROSS, UP, DOWN = range(4)


def spot():
    me = lax.axis_index("expert")
    return me // 4, (me // 2) % 2, me % 2


def at(z, x, c):
    return (z * 2 + x) * 2 + c


def greet_all(group, n_dp):
    me, dp = lax.axis_index("expert"), lax.axis_index("dp")
    barrier = pltpu.get_barrier_semaphore()

    def hello(k, carry):
        pl.semaphore_signal(
            barrier, inc=1, device_id={"expert": (me + k) % group}, device_id_type=MESH
        )
        return carry

    lax.fori_loop(1, group, hello, 0)
    if n_dp == 2:
        pl.semaphore_signal(barrier, inc=1, device_id={"dp": 1 - dp}, device_id_type=MESH)
    pl.semaphore_wait(barrier, group if n_dp == 2 else group - 1)


def nearest(zs, z, i):
    low = jnp.minimum(z, zs - 1 - z)
    step = (i + 1) // 2
    paired = jnp.where(i % 2 == 1, z - step, z + step)
    alone = jnp.where(z > zs - 1 - z, z - (i - low), z + (i - low))
    return jnp.where(i <= 2 * low, paired, alone)


def gather_blocks(zs, buffers, process):
    z, x, c = spot()
    far = zs - 1

    def copies(block, kind, e):
        return [
            pltpu.make_async_remote_copy(
                src_ref=all_ref.at[block],
                dst_ref=all_ref.at[block],
                send_sem=send.at[kind, block],
                recv_sem=recv.at[block],
                device_id={"expert": e},
                device_id_type=MESH,
            )
            for all_ref, send, recv in buffers
        ]

    def to_sibling(block):
        return copies(block, SIB, at(z, x, 1 - c))

    def to_across(block):
        return copies(block, ACROSS, at(z, 1 - x, c))

    def to_up(block):
        return copies(block, UP, at(z + 1, x, c))

    def to_down(block):
        return copies(block, DOWN, at(z - 1, x, c))

    def step(i, carry):
        @pl.when(i < zs)
        def _():
            zz = nearest(zs, z, i)
            block = at(zz, x, c)
            over = at(zz, 1 - x, c)
            for n in range(len(buffers)):

                @pl.when(i > 0)
                def _():
                    to_sibling(block)[n].wait_recv()

                @pl.when((zz <= z) & (z < far))
                def _():
                    to_up(block)[n].start()

                @pl.when((zz >= z) & (z > 0))
                def _():
                    to_down(block)[n].start()

                to_across(block)[n].start()
                to_sibling(block)[n].start()
            for n in range(len(buffers)):
                to_sibling(over)[n].wait_recv()
                to_sibling(over)[n].start()

        @pl.when(i > 0)
        def _():
            zz = nearest(zs, z, i - 1)
            for xx in range(2):
                for copy in to_sibling(at(zz, xx, 1 - c)):
                    copy.wait_recv()
            process(i - 1, zz)

        return carry

    lax.fori_loop(0, zs + 1, step, 0)

    def done(zz, carry):
        block = at(zz, x, c)
        for copy in to_across(block) + to_sibling(block) + to_sibling(at(zz, 1 - x, c)):
            copy.wait_send()

        @pl.when((zz <= z) & (z < far))
        def _():
            for copy in to_up(block):
                copy.wait_send()

        @pl.when((zz >= z) & (z > 0))
        def _():
            for copy in to_down(block):
                copy.wait_send()

        return carry

    lax.fori_loop(0, zs, done, 0)


def joined(own_ref, full_ref, local, send, recv):
    dp = lax.axis_index("dp")
    half = own_ref.shape[0]
    here = full_ref.at[pl.ds(dp * half, half)]
    mine = pltpu.make_async_copy(own_ref, here, local)
    theirs = over_dp(own_ref, here, send, recv)

    def start():
        mine.start()
        theirs.start()

    def finish():
        mine.wait()
        theirs.wait()

    return start, finish


def gather_sems(group):
    return [pltpu.SemaphoreType.DMA((4, group)), pltpu.SemaphoreType.DMA((group,))]


def scatter_blocks(zs, part_ref, out_ref, r_sib, r_x, r_z, s_x, s_z, send, recv, produce, pause=None):
    z, x, c = spot()
    far = zs - 1

    def to_sibling(zz, xx):
        return pltpu.make_async_remote_copy(
            src_ref=part_ref.at[at(zz, xx, 1 - c)],
            dst_ref=r_sib.at[zz * 2 + xx],
            send_sem=send.at[SIB, zz * 2 + xx],
            recv_sem=recv.at[SIB, zz * 2 + xx],
            device_id={"expert": at(z, x, 1 - c)},
            device_id_type=MESH,
        )

    def to_across(zz):
        return pltpu.make_async_remote_copy(
            src_ref=s_x.at[zz],
            dst_ref=r_x.at[zz],
            send_sem=send.at[ACROSS, zz],
            recv_sem=recv.at[ACROSS, zz],
            device_id={"expert": at(z, 1 - x, c)},
            device_id_type=MESH,
        )

    def along(zz, kind, e):
        return pltpu.make_async_remote_copy(
            src_ref=s_z.at[zz],
            dst_ref=r_z.at[kind - UP, zz],
            send_sem=send.at[kind, zz],
            recv_sem=recv.at[kind, zz],
            device_id={"expert": e},
            device_id_type=MESH,
        )

    def up(zz):
        return along(zz, UP, at(z + 1, x, c))

    def down(zz):
        return along(zz, DOWN, at(z - 1, x, c))

    def order(do):
        for d in range(far, 0, -1):

            @pl.when(z + d <= far)
            def _():
                do(z + d)

            @pl.when(z >= d)
            def _():
                do(z - d)

        do(z)

    def cross(zz):
        produce(at(zz, 1 - x, 1 - c))
        to_sibling(zz, 1 - x).start()
        produce(at(zz, 1 - x, c))
        to_sibling(zz, 1 - x).wait_recv()
        mine = part_ref[at(zz, 1 - x, c)].astype(F32)
        s_x[zz] = (mine + r_sib[zz * 2 + 1 - x].astype(F32)).astype(BF16)
        to_across(zz).start()

    order(cross)

    def near(zz):
        produce(at(zz, x, 1 - c))
        to_sibling(zz, x).start()
        produce(at(zz, x, c))

    order(near)
    if pause is not None:
        pause()

    def finish(zz):
        to_sibling(zz, x).wait_recv()
        to_across(zz).wait_recv()

        def here():
            mine = part_ref[at(zz, x, c)].astype(F32)
            return mine + r_sib[zz * 2 + x].astype(F32) + r_x[zz].astype(F32)

        @pl.when(zz > z)
        def _():
            @pl.when(z > 0)
            def _():
                up(zz).wait_recv()
                s_z[zz] = (here() + r_z[0, zz].astype(F32)).astype(BF16)

            @pl.when(z == 0)
            def _():
                s_z[zz] = here().astype(BF16)

            up(zz).start()

        @pl.when(zz < z)
        def _():
            @pl.when(z < far)
            def _():
                down(zz).wait_recv()
                s_z[zz] = (here() + r_z[1, zz].astype(F32)).astype(BF16)

            @pl.when(z == far)
            def _():
                s_z[zz] = here().astype(BF16)

            down(zz).start()

        @pl.when(zz == z)
        def _():
            out_ref[...] = here()

            @pl.when(z > 0)
            def _():
                up(zz).wait_recv()
                out_ref[...] += r_z[0, zz].astype(F32)

            @pl.when(z < far)
            def _():
                down(zz).wait_recv()
                out_ref[...] += r_z[1, zz].astype(F32)

    order(finish)

    def done(zz, carry):
        to_sibling(zz, 0).wait_send()
        to_sibling(zz, 1).wait_send()
        to_across(zz).wait_send()

        @pl.when(zz > z)
        def _():
            up(zz).wait_send()

        @pl.when(zz < z)
        def _():
            down(zz).wait_send()

        return carry

    lax.fori_loop(0, zs, done, 0)


def scatter_scratch(group, rows, width):
    zs = group // 4

    def buffer(*n):
        return pltpu.VMEM((*n, rows, width), BF16)

    return [
        buffer(2 * zs),
        buffer(zs),
        buffer(2, zs),
        buffer(zs),
        buffer(zs),
        pltpu.SemaphoreType.DMA((4, 2 * zs)),
        pltpu.SemaphoreType.DMA((4, 2 * zs)),
    ]


def over_dp(src, dst, send, recv):
    return pltpu.make_async_remote_copy(
        src_ref=src,
        dst_ref=dst,
        send_sem=send,
        recv_sem=recv,
        device_id={"dp": 1 - lax.axis_index("dp")},
        device_id_type=MESH,
    )


def tree_swap(group, make, send, recv):
    me = lax.axis_index("expert")

    def copy(k, back):
        d = (me + k) % group
        src, _ = make(d, me)
        _, dst = make(d, d if back else me)
        return pltpu.make_async_remote_copy(
            src_ref=src,
            dst_ref=dst,
            send_sem=send.at[k],
            recv_sem=recv.at[d if back else me],
            device_id={"expert": d},
            device_id_type=MESH,
        )

    def start():
        def one(k, carry):
            copy(k, False).start()
            return carry

        lax.fori_loop(1, group, one, 0)

    def finish_recv():
        def one(k, carry):
            copy(k, True).wait_recv()
            return carry

        lax.fori_loop(1, group, one, 0)

    def finish_send():
        def one(k, carry):
            copy(k, False).wait_send()
            return carry

        lax.fori_loop(1, group, one, 0)

    return start, finish_recv, finish_send


VMEM = pl.BlockSpec(memory_space=pltpu.VMEM)
HBM = pl.BlockSpec(memory_space=pl.ANY)
DMA = pltpu.SemaphoreType.DMA


def params(cid):
    return pltpu.CompilerParams(
        collective_id=cid, has_side_effects=True, vmem_limit_bytes=56 * 2**20
    )


def project_kernel(
    group, n_dp, shard,
    x_ref, w_ref, pay_ref,
    normed_ref, pre_ref, w_all, gains_ref, pay_out,
    x_all, send, recv, local, w_send, w_recv, dp_send, dp_recv,
):
    me, dp = lax.axis_index("expert"), lax.axis_index("dp")
    mine = pltpu.make_async_copy(x_ref, x_all.at[me], local.at[0])
    mine.start()
    half = group * shard

    def rows_of(d, e):
        return w_all.at[pl.ds(d * half + e * shard, shard)]

    own = pltpu.make_async_copy(w_ref.at[me], rows_of(dp, me), local.at[1])
    own.start()
    greet_all(group, n_dp)
    start, finish_recv, finish_send = tree_swap(
        group, lambda d, src: (w_ref.at[d], rows_of(dp, src)), w_send, w_recv
    )
    start()
    mine.wait()
    own.wait()

    def bundle(d):
        piece = w_all.at[pl.ds(d * half, half)]
        return over_dp(piece, piece, dp_send.at[0], dp_recv.at[0])

    pay_start, pay_finish = joined(pay_ref, pay_out, local.at[2], dp_send.at[1], dp_recv.at[1])

    def compute(block):
        rows = x_ref.shape[0]
        values = x_all[block].astype(F32)
        scale = lax.rsqrt(jnp.mean(values * values, axis=-1, keepdims=True) + EPSILON)
        normed = (values * scale * gains_ref[0:1, :]).astype(BF16)
        normed_ref[block] = normed
        pre_ref[pl.ds(block * rows, rows), :] = mm(normed, w_all[:, : 3 * HEAD_DIM])

    def weights_here():
        finish_recv()
        bundle(dp).start()
        pay_start()

    def weights_done():
        bundle(1 - dp).wait_recv()
        pick = lax.broadcasted_iota(jnp.int32, (8, HEAD_DIM), 0)
        lane = lax.broadcasted_iota(jnp.int32, (8, HEAD_DIM), 1)
        pick = jnp.where(pick == lane, 1.0, 0.0).astype(BF16)
        gains_ref[...] = mm_t(pick, w_all[:, 3 * HEAD_DIM :])

    def process(i, zz):
        @pl.when(i == 0)
        def _():
            weights_here()
            weights_done()

        def one(j, carry):
            compute(zz * 4 + j)
            return carry

        lax.fori_loop(0, 4, one, 0)

    gather_blocks(group // 4, [(x_all, send, recv)], process)
    finish_send()
    bundle(dp).wait_send()
    pay_finish()


def project(tokens, w_cut, payload, n_dp, cid):
    group, shard = w_cut.shape[0], w_cut.shape[1]
    rows, width = tokens.shape
    wide = w_cut.shape[2]
    return pl.pallas_call(
        functools.partial(project_kernel, group, n_dp, shard),
        out_shape=[
            jax.ShapeDtypeStruct((group, rows, width), BF16),
            jax.ShapeDtypeStruct((group * rows, 3 * HEAD_DIM), F32),
            jax.ShapeDtypeStruct((n_dp * group * shard, wide), BF16),
            jax.ShapeDtypeStruct((8, width), F32),
            jax.ShapeDtypeStruct((n_dp * payload.shape[0], payload.shape[1]), payload.dtype),
        ],
        in_specs=[HBM, VMEM, HBM],
        out_specs=[VMEM, VMEM, VMEM, VMEM, HBM],
        scratch_shapes=[
            pltpu.VMEM((group, rows, width), BF16),
            *gather_sems(group),
            DMA((3,)),
            DMA((group,)),
            DMA((group,)),
            DMA((2,)),
            DMA((2,)),
        ],
        compiler_params=params(cid),
    )(tokens, w_cut, payload)


def attend_kernel(
    group, n_dp,
    q_ref, k_ref, v_ref, bias_ref, w_ref, pay_ref,
    attn_ref, lse_ref, sum_ref, pay_out,
    part, r_sib, r_x, r_z, s_x, s_z, send, recv, local, dp_send, dp_recv,
):
    rows = sum_ref.shape[0]
    count = k_ref.shape[0]
    greet_all(group, n_dp)
    pay_start, pay_finish = joined(pay_ref, pay_out, local, dp_send, dp_recv)
    pay_start()

    def produce(block):
        first = block * rows
        scores = mm_t(q_ref[pl.ds(first, rows), :], k_ref[...]) * SCALE
        scores = scores + bias_ref[pl.ds(block, 1), :]
        key = lax.broadcasted_iota(jnp.int32, (rows, count), 1)
        query = first + lax.broadcasted_iota(jnp.int32, (rows, count), 0)
        scores = jnp.where(key <= query, scores, NEGATIVE)
        row_max = jnp.max(scores, axis=-1, keepdims=True)
        weights = jnp.exp(scores - row_max)
        total = jnp.sum(weights, axis=-1, keepdims=True)
        attn = mm(weights.astype(BF16), v_ref[...]) / total
        attn_ref[pl.ds(first, rows), :] = attn
        lse_ref[pl.ds(first, rows), :] = jnp.broadcast_to(row_max + jnp.log(total), (rows, HEAD_DIM))
        part[block] = mm(attn.astype(BF16), w_ref[...]).astype(BF16)

    scatter_blocks(group // 4, part, sum_ref, r_sib, r_x, r_z, s_x, s_z, send, recv, produce)
    pay_finish()


def attend(queries, keys, values, bias, w_rows, payload, n_dp, cid):
    group = bias.shape[0]
    count, width = queries.shape[0], w_rows.shape[1]
    rows = count // group
    return pl.pallas_call(
        functools.partial(attend_kernel, group, n_dp),
        out_shape=[
            jax.ShapeDtypeStruct((count, HEAD_DIM), F32),
            jax.ShapeDtypeStruct((count, HEAD_DIM), F32),
            jax.ShapeDtypeStruct((rows, width), F32),
            jax.ShapeDtypeStruct((n_dp * payload.shape[0], payload.shape[1]), payload.dtype),
        ],
        in_specs=[VMEM] * 5 + [HBM],
        out_specs=[VMEM, VMEM, VMEM, HBM],
        scratch_shapes=[
            pltpu.VMEM((group, rows, width), BF16),
            *scatter_scratch(group, rows, width),
            DMA,
            DMA,
            DMA,
        ],
        compiler_params=params(cid),
    )(queries, keys, values, bias, w_rows, payload)


def attend_back_kernel(
    group, n_dp,
    g_ref, q_ref, k_ref, v_ref, bias_ref, w_ref, attn_ref, lse_ref,
    dq_ref, dk_ref, dv_ref, dw_ref,
    g_all, send, recv, local,
):
    me = lax.axis_index("expert")
    rows = g_ref.shape[0]
    count = k_ref.shape[0]
    chunk = min(count, 512)
    mine = pltpu.make_async_copy(g_ref, g_all.at[me], local)
    mine.start()
    greet_all(group, n_dp)
    mine.wait()
    dk_ref[...] = jnp.zeros_like(dk_ref)
    dv_ref[...] = jnp.zeros_like(dv_ref)
    dw_ref[...] = jnp.zeros_like(dw_ref)

    def process(block):
        first = block * rows
        here = pl.ds(first, rows)
        grad = g_all[block]
        attn = attn_ref[here, :]
        mixed_grad = mm_t(grad, w_ref[...]).astype(BF16)
        dw_ref[...] += t_mm(attn.astype(BF16), grad)
        delta = jnp.sum(mixed_grad.astype(F32) * attn, axis=-1, keepdims=True)
        queries = q_ref[here, :]
        lse = lse_ref[here, :][:, :1]
        query = first + lax.broadcasted_iota(jnp.int32, (rows, chunk), 0)

        def turn_keys(j, dq):
            cut = pl.ds(j * chunk, chunk)
            keys = k_ref[cut, :]
            scores = mm_t(queries, keys) * SCALE + bias_ref[pl.ds(block, 1), cut]
            key = j * chunk + lax.broadcasted_iota(jnp.int32, (rows, chunk), 1)
            probs = jnp.exp(jnp.where(key <= query, scores - lse, NEGATIVE))
            score_grad = probs * (mm_t(mixed_grad, v_ref[cut, :]) - delta)
            score_grad = score_grad.astype(BF16)
            dk_ref[cut, :] += t_mm(score_grad, queries)
            dv_ref[cut, :] += t_mm(probs.astype(BF16), mixed_grad)
            return dq + mm(score_grad, keys)

        turns = (first + rows + chunk - 1) // chunk
        dq = lax.fori_loop(0, turns, turn_keys, jnp.zeros((rows, HEAD_DIM), F32))
        dq_ref[here, :] = dq

    def four(i, zz):
        def one(j, carry):
            process(zz * 4 + j)
            return carry

        lax.fori_loop(0, 4, one, 0)

    gather_blocks(group // 4, [(g_all, send, recv)], four)


def attend_back(grad, queries, keys, values, bias, w_rows, attn, lse, n_dp, cid):
    group = bias.shape[0]
    rows, width = grad.shape
    count = queries.shape[0]
    long = jax.ShapeDtypeStruct((count, HEAD_DIM), F32)
    return pl.pallas_call(
        functools.partial(attend_back_kernel, group, n_dp),
        out_shape=[long, long, long, jax.ShapeDtypeStruct((HEAD_DIM, width), F32)],
        in_specs=[HBM] + [VMEM] * 7,
        out_specs=[VMEM] * 4,
        scratch_shapes=[pltpu.VMEM((group, rows, width), BF16), *gather_sems(group), DMA],
        compiler_params=params(cid),
    )(grad, queries, keys, values, bias, w_rows, attn, lse)


def unproject_kernel(
    group, n_dp, shard,
    low_ref, w_ref, normed_ref,
    sum_ref, got_ref,
    part, r_sib, r_x, r_z, s_x, s_z, send, recv,
    mine, theirs, w_send, w_recv, dp_send, dp_recv,
):
    me, dp = lax.axis_index("expert"), lax.axis_index("dp")
    rows = sum_ref.shape[0]
    half = group * shard
    greet_all(group, n_dp)
    step = min(half, 256)

    def slice_grad(d, ref):
        def one(i, carry):
            cols = pl.ds(pl.multiple_of(d * half + i * step, step), step)
            total = jnp.zeros((step, low_ref.shape[1]), F32)
            grad = t_mm(normed_ref[:, cols], low_ref[...])
            ref[pl.ds(i * step, step), :] = (total + grad).astype(ref.dtype)
            return carry

        lax.fori_loop(0, half // step, one, 0)

    to_dp = over_dp(theirs.at[0], theirs.at[1], dp_send, dp_recv)

    def produce(block):
        low = low_ref[pl.ds(block * rows, rows), :]
        part[block] = mm_t(low, w_ref[:, : 3 * HEAD_DIM]).astype(BF16)

    def make(d, src):
        return mine.at[pl.ds(d * shard, shard)], got_ref.at[src]

    start, finish_recv, finish_send = tree_swap(group, make, w_send, w_recv)

    def pause():
        slice_grad(1 - dp, theirs.at[0])
        to_dp.start()
        slice_grad(dp, mine)
        to_dp.wait_recv()
        mine[...] = (mine[...].astype(F32) + theirs[1].astype(F32)).astype(BF16)
        start()
        got_ref[me] = mine[pl.ds(me * shard, shard), :]

    scatter_blocks(group // 4, part, sum_ref, r_sib, r_x, r_z, s_x, s_z, send, recv, produce, pause)
    finish_recv()
    finish_send()
    to_dp.wait_send()


def unproject(low, w_all, normed, rows, shard, n_dp, cid):
    count, wide = low.shape
    width = w_all.shape[0]
    group = count // rows
    return pl.pallas_call(
        functools.partial(unproject_kernel, group, n_dp, shard),
        out_shape=[
            jax.ShapeDtypeStruct((rows, width), F32),
            jax.ShapeDtypeStruct((group, shard, wide), BF16),
        ],
        in_specs=[VMEM] * 3,
        out_specs=[VMEM] * 2,
        scratch_shapes=[
            pltpu.VMEM((group, rows, width), BF16),
            *scatter_scratch(group, rows, width),
            pltpu.VMEM((group * shard, wide), BF16),
            pltpu.VMEM((2, group * shard, wide), BF16),
            DMA((group,)),
            DMA((group,)),
            DMA,
            DMA,
        ],
        compiler_params=params(cid),
    )(low, w_all, normed)


def swap_kernel(axes, sizes, in_ref, out_ref, send, recv, local):
    count = 1
    for size in sizes:
        count *= size
    me = jnp.int32(0)
    for axis, size in zip(axes, sizes):
        me = me * size + lax.axis_index(axis)
    same = in_ref.shape[0] == 1

    def spread(d):
        where = {}
        for axis, size in zip(axes[::-1], sizes[::-1]):
            where[axis] = d % size
            d = d // size
        return where

    barrier = pltpu.get_barrier_semaphore()

    def hello(k, carry):
        pl.semaphore_signal(
            barrier, inc=1, device_id=spread((me + k) % count), device_id_type=MESH
        )
        return carry

    lax.fori_loop(1, count, hello, 0)
    pl.semaphore_wait(barrier, count - 1)

    def copy(k):
        d = (me + k) % count
        return pltpu.make_async_remote_copy(
            src_ref=in_ref.at[0 if same else d],
            dst_ref=out_ref.at[me],
            send_sem=send.at[k],
            recv_sem=recv.at[me],
            device_id=spread(d),
            device_id_type=MESH,
        )

    def start(k, carry):
        copy(k).start()
        return carry

    lax.fori_loop(1, count, start, 0)
    mine = pltpu.make_async_copy(in_ref.at[0 if same else me], out_ref.at[me], local)
    mine.start()
    mine.wait()

    def finish(k, carry):
        d = (me + k) % count
        pltpu.make_async_remote_copy(
            src_ref=in_ref.at[0],
            dst_ref=out_ref.at[d],
            send_sem=send.at[k],
            recv_sem=recv.at[d],
            device_id=spread(d),
            device_id_type=MESH,
        ).wait_recv()
        copy(k).wait_send()
        return carry

    lax.fori_loop(1, count, finish, 0)


def swap(values, axes, cid):
    sizes = tuple(lax.axis_size(axis) for axis in axes)
    count = 1
    for size in sizes:
        count *= size
    return pl.pallas_call(
        functools.partial(swap_kernel, axes, sizes),
        out_shape=jax.ShapeDtypeStruct((count, *values.shape[1:]), values.dtype),
        in_specs=[pl.BlockSpec(memory_space=pltpu.VMEM)],
        out_specs=pl.BlockSpec(memory_space=pltpu.VMEM),
        scratch_shapes=[
            pltpu.SemaphoreType.DMA((count,)),
            pltpu.SemaphoreType.DMA((count,)),
            pltpu.SemaphoreType.DMA,
        ],
        compiler_params=pltpu.CompilerParams(
            collective_id=cid, has_side_effects=True, vmem_limit_bytes=32 * 2**20
        ),
    )(values)


def expert_kernel(
    group, n_dp, cap,
    x_ref, cot_ref, gate_ref, gate_w, up_w, down_ref,
    rows_out, grads_out, hidden_out, gate_out, up_out, sent_out, row_out, gate_grads,
    x_all, c_all, down_w, gates, stage,
    x_send, x_recv, c_send, c_recv, g_send, g_recv, local, dp_send, dp_recv,
):
    me = lax.axis_index("expert")
    rows, width = x_ref.shape
    pair = 2 * cap
    own = [
        pltpu.make_async_copy(x_ref, x_all.at[me], local.at[0]),
        pltpu.make_async_copy(cot_ref, c_all.at[me], local.at[1]),
    ]
    for copy in own:
        copy.start()
    greet_all(group, n_dp)
    start, finish_recv, finish_send = tree_swap(
        group, lambda d, src: (gate_ref.at[d], gates.at[src]), g_send, g_recv
    )
    start()
    down_start, down_finish = joined(down_ref, down_w, local.at[2], dp_send, dp_recv)
    down_start()
    gates[me] = gate_ref[me]
    for copy in own:
        copy.wait()

    def put(kind, p):
        ref = (sent_out, row_out)[kind]
        return pltpu.make_async_copy(
            stage.at[kind], ref.at[pl.ds(p * 2 * rows, 2 * rows)], local.at[3 + kind]
        )

    lane = lax.broadcasted_iota(jnp.int32, (rows, rows), 1)
    row = lax.broadcasted_iota(jnp.int32, (rows, rows), 0)
    before = jnp.where(row < lane, 1.0, 0.0).astype(BF16)
    slot = lax.broadcasted_iota(jnp.int32, (cap, rows), 0).astype(F32)

    def run(p):
        base = p * pair
        picks, gate_cols = [], []
        for i in range(2):
            segment = p * 2 + i
            gate_row = gates[segment]
            routed = jnp.where(gate_row > 0.0, 1.0, 0.0)
            rank = mm(jnp.broadcast_to(routed, (16, rows)).astype(BF16), before)[0:1, :]
            pick = jnp.where((slot == rank) & (routed > 0.5), 1.0, 0.0)
            gate_cols.append(jnp.sum(pick * gate_row, axis=1, keepdims=True))
            pick_low = pick.astype(BF16)
            picks.append((pick, pick_low))
            here = pl.ds(base + i * cap, cap)
            rows_out[here, :] = mm(pick_low, x_all[segment]).astype(BF16)
            grads_out[here, :] = mm(pick_low, c_all[segment]).astype(BF16)
        here = pl.ds(base, pair)
        gate_col = jnp.concatenate(gate_cols)
        taken = rows_out[here, :]
        gate_pre = mm(taken, gate_w[...])
        up_pre = mm(taken, up_w[...])
        sig = 1.0 / (1.0 + jnp.exp(-gate_pre))
        silu = gate_pre * sig
        hidden = (silu * up_pre).astype(BF16)
        hidden_out[here, :] = hidden
        result = mm(hidden, down_w[...]).astype(BF16).astype(F32)
        cot = grads_out[here, :].astype(F32)
        dots = jnp.sum(cot * result, axis=1, keepdims=True)
        sent = (gate_col * result).astype(BF16)
        grads_out[here, :] = (gate_col * cot).astype(BF16)
        for i, (pick, pick_low) in enumerate(picks):
            part = slice(i * cap, (i + 1) * cap)
            gate_grads[p * 2 + i] = jnp.sum(pick * dots[part], axis=0, keepdims=True)
            stage[0, i * rows : (i + 1) * rows, :] = t_mm(pick_low, sent[part]).astype(BF16)
        put(0, p).start()
        hidden_grad = mm_t(grads_out[here, :], down_w[...]).astype(BF16).astype(F32)
        slope = sig * (1.0 + gate_pre * (1.0 - sig))
        gate_pre_grad = (hidden_grad * up_pre * slope).astype(BF16)
        up_pre_grad = (hidden_grad * silu).astype(BF16)
        gate_out[here, :] = gate_pre_grad
        up_out[here, :] = up_pre_grad
        row_grad = (mm_t(gate_pre_grad, gate_w[...]) + mm_t(up_pre_grad, up_w[...])).astype(BF16)
        for i, (_, pick_low) in enumerate(picks):
            part = slice(i * cap, (i + 1) * cap)
            stage[1, i * rows : (i + 1) * rows, :] = t_mm(pick_low, row_grad[part]).astype(BF16)
        put(1, p).start()
        put(0, p).wait()
        put(1, p).wait()

    def process(i, zz):
        @pl.when(i == 0)
        def _():
            finish_recv()
            down_finish()

        def one(j, carry):
            run(zz * 2 + j)
            return carry

        lax.fori_loop(0, 2, one, 0)

    gather_blocks(group // 4, [(x_all, x_send, x_recv), (c_all, c_send, c_recv)], process)
    finish_send()


def expert(x, cot, gates, gate_w, up_w, down_w, n_dp, cap, cid):
    group = gates.shape[0]
    rows, width = x.shape
    hidden = gate_w.shape[1]
    total = group * cap

    def shape(*dims, dtype=BF16):
        return jax.ShapeDtypeStruct(dims, dtype)

    def buffer(*dims):
        return pltpu.VMEM(dims, BF16)

    return pl.pallas_call(
        functools.partial(expert_kernel, group, n_dp, cap),
        out_shape=[
            shape(total, width),
            shape(total, width),
            shape(total, hidden),
            shape(total, hidden),
            shape(total, hidden),
            shape(group * rows, width),
            shape(group * rows, width),
            shape(*gates.shape, dtype=F32),
        ],
        in_specs=[HBM, HBM, VMEM, VMEM, VMEM, HBM],
        out_specs=[VMEM] * 5 + [HBM, HBM, VMEM],
        scratch_shapes=[
            buffer(group, rows, width),
            buffer(group, rows, width),
            buffer(n_dp * down_w.shape[0], width),
            pltpu.VMEM(gates.shape, F32),
            buffer(2, 2 * rows, width),
            *gather_sems(group),
            *gather_sems(group),
            DMA((group,)),
            DMA((group,)),
            DMA((5,)),
            DMA,
            DMA,
        ],
        compiler_params=pltpu.CompilerParams(
            collective_id=cid, has_side_effects=True, vmem_limit_bytes=63 * 2**20
        ),
    )(x, cot, gates, gate_w, up_w, down_w)


def collect_kernel(
    group, n_dp, part, gate_ref, sum_ref, gates_ref,
    r_sib, r_x, r_z, s_x, s_z, send, recv, g_send, g_recv,
):
    me = lax.axis_index("expert")
    greet_all(group, n_dp)
    start, finish_recv, finish_send = tree_swap(
        group, lambda d, src: (gate_ref.at[d], gates_ref.at[src]), g_send, g_recv
    )
    start()
    gates_ref[me] = gate_ref[me]
    scatter_blocks(
        group // 4, part, sum_ref, r_sib, r_x, r_z, s_x, s_z, send, recv, lambda block: None
    )
    finish_recv()
    finish_send()


def collect(parts, gates, n_dp, cid):
    group, rows, width = parts.shape
    return pl.pallas_call(
        functools.partial(collect_kernel, group, n_dp),
        out_shape=[
            jax.ShapeDtypeStruct((rows, width), F32),
            jax.ShapeDtypeStruct(gates.shape, gates.dtype),
        ],
        in_specs=[VMEM, VMEM],
        out_specs=[VMEM, VMEM],
        scratch_shapes=[*scatter_scratch(group, rows, width), DMA((group,)), DMA((group,))],
        compiler_params=params(cid),
    )(parts, gates)


def attention(queries, mask, keys, values):
    scores = jnp.where(mask, mm_t(queries, keys) * SCALE, NEGATIVE)
    row_max = jnp.max(scores, axis=-1, keepdims=True)
    weights = jnp.exp(scores - row_max)
    total = jnp.sum(weights, axis=-1, keepdims=True)
    attn = mm(weights.astype(BF16), values) / total
    return attn, row_max + jnp.log(total)


def attention_back(queries, mask, log_total, mixed_grad, row_delta, keys, values):
    probs = jnp.exp(jnp.where(mask, mm_t(queries, keys) * SCALE - log_total, NEGATIVE))
    score_grad = (probs * (mm_t(mixed_grad, values) - row_delta)).astype(BF16)
    query_grad = mm(score_grad, keys) * SCALE
    key_grad = t_mm(score_grad, queries) * SCALE
    return query_grad, key_grad, t_mm(probs.astype(BF16), mixed_grad)


def expert_step(rows_in, cot_in, gates, gate_w, up_w, down_w):
    cot_in = cot_in.astype(F32)
    gate_pre = mm(rows_in, gate_w)
    up_pre = mm(rows_in, up_w)
    sig = jax.nn.sigmoid(gate_pre)
    silu = gate_pre * sig
    hidden = (silu * up_pre).astype(BF16)
    expert_out = mm(hidden, down_w).astype(BF16).astype(F32)
    sent_out = (gates * expert_out).astype(BF16)
    gate_grad = jnp.sum(cot_in * expert_out, axis=-1)
    out_grad = (gates * cot_in).astype(BF16)
    hidden_grad = mm_t(out_grad, down_w).astype(BF16).astype(F32)
    gate_pre_grad = (hidden_grad * up_pre * sig * (1.0 + gate_pre * (1.0 - sig))).astype(BF16)
    up_pre_grad = (hidden_grad * silu).astype(BF16)
    row_grad = (mm_t(gate_pre_grad, gate_w) + mm_t(up_pre_grad, up_w)).astype(BF16)
    sums = (t_mm(rows_in, gate_pre_grad), t_mm(rows_in, up_pre_grad), t_mm(hidden, out_grad))
    return (sent_out, gate_grad, row_grad), sums


def per_device(
    tokens, attn_gain, q_gain, k_gain, ffn_gain, w_query, w_key, w_value, w_out, router,
    w_gate, w_up, w_down, cotangent, routes, parents,
):
    rows, width = tokens.shape
    heads = width // HEAD_DIM
    group = lax.axis_size("expert")
    n_dp = lax.axis_size("dp")
    devices = group * n_dp
    share = max(1, group // heads)
    tree_rows = group * rows
    own_rows = tree_rows // share
    shard = w_query.shape[0]
    dp = lax.axis_index("dp")
    me = lax.axis_index("expert")
    head = me // share
    part = me % share
    peers = [[h * share + j for h in range(heads)] for j in range(share)]
    siblings = [[h * share + j for j in range(share)] for h in range(heads)]

    reach = ancestry(parents)
    start = dp * group
    tree = lax.dynamic_slice(reach, (start, start), (group, group))
    depth = jnp.sum(lax.dynamic_slice_in_dim(reach, start, group, 0), axis=1)
    sees = tree + jnp.eye(group, dtype=F32)
    own_segs = own_rows // rows
    first_seg = part * own_segs
    my_depth = lax.dynamic_slice_in_dim(depth, first_seg, own_segs, 0)
    my_sees = lax.dynamic_slice_in_dim(sees, first_seg, own_segs, 0)
    place = jnp.arange(rows, dtype=F32)
    positions = (my_depth[:, None] * rows + place[None, :]).reshape(own_rows)
    frequencies = THETA ** (-2.0 * jnp.arange(HEAD_DIM // 2, dtype=F32) / HEAD_DIM)
    angles = positions[:, None] * frequencies[None, :]
    cosine, sine = jnp.cos(angles), jnp.sin(angles)
    key_index = jnp.arange(tree_rows, dtype=jnp.int32)
    query_index = first_seg * rows + jnp.arange(own_rows, dtype=jnp.int32)
    seen = jnp.repeat(jnp.repeat(my_sees, rows, axis=0), rows, axis=1) > 0.5
    mask = seen & (key_index[None, :] <= query_index[:, None])

    def own_part(values):
        return lax.dynamic_slice_in_dim(values, first_seg * rows, own_rows, 0)

    def head_sum(values):
        return lax.psum(values, "expert", axis_index_groups=peers if share > 1 else None)

    def tree_gather(values):
        return lax.all_gather(values, "expert", axis=0, tiled=True)

    def tree_scatter(values):
        return lax.psum_scatter(values, "expert", scatter_dimension=0, tiled=True).astype(F32)

    def both_swap(values):
        return lax.all_to_all(values, BOTH, 0, 0, tiled=True)

    def expert_swap(values):
        return lax.all_to_all(values, "expert", 0, 0, tiled=True)

    others = [(d, (d + 1) % n_dp) for d in range(n_dp)]

    def dp_join(values):
        if n_dp != 2:
            return lax.all_gather(values, "dp", axis=0, tiled=True)
        other = lax.ppermute(values, "dp", others)
        return jnp.where(
            dp == 0, jnp.concatenate([values, other]), jnp.concatenate([other, values])
        )

    def dp_sum(values):
        if n_dp != 2:
            return lax.psum_scatter(values, "dp", scatter_dimension=0, tiled=True)
        halves = values.reshape(2, values.shape[0] // 2, -1)
        theirs = lax.dynamic_index_in_dim(halves, 1 - dp, 0, keepdims=False)
        ours = lax.dynamic_index_in_dim(halves, dp, 0, keepdims=False)
        return ours.astype(F32) + lax.ppermute(theirs, "dp", others).astype(F32)

    gains = lax.all_gather(
        jnp.stack([attn_gain, q_gain, k_gain, ffn_gain], axis=1), BOTH, axis=0, tiled=True
    ).astype(F32)
    attn_g, query_g, key_g, ffn_g = gains[:, 0], gains[:, 1], gains[:, 2], gains[:, 3]
    my_query_g = lax.dynamic_slice_in_dim(query_g, head * HEAD_DIM, HEAD_DIM, 0)[None, :]
    my_key_g = lax.dynamic_slice_in_dim(key_g, head * HEAD_DIM, HEAD_DIM, 0)[None, :]
    by_head = jnp.stack([w_query, w_key, w_value], axis=1).reshape(shard, 3, heads, HEAD_DIM)
    by_head = by_head.transpose(2, 0, 1, 3).reshape(1, heads, 1, shard, 3 * HEAD_DIM)
    by_head = jnp.broadcast_to(by_head, (n_dp, heads, share, shard, 3 * HEAD_DIM))
    w_head = both_swap(by_head.reshape(devices, shard, 3 * HEAD_DIM)).reshape(
        width, 3 * HEAD_DIM
    )
    out_w = lax.all_gather(w_out, BOTH, axis=0, tiled=True)
    out_head = lax.dynamic_slice_in_dim(out_w, head * HEAD_DIM, HEAD_DIM, 0)
    router_w = lax.all_gather(router, BOTH, axis=0, tiled=True)
    gate_w = dp_join(w_gate[0])
    up_w = dp_join(w_up[0])
    down_w = dp_join(w_down[0])

    token_f = tokens.astype(F32)
    first_scale = inverse_rms(token_f)
    normed = (token_f * first_scale * attn_g[None, :]).astype(BF16)
    normed_all = own_part(tree_gather(normed))
    pre = mm(normed_all, w_head)
    query_pre, key_pre = pre[:, :HEAD_DIM], pre[:, HEAD_DIM : 2 * HEAD_DIM]
    values = pre[:, 2 * HEAD_DIM :].astype(BF16)
    squares = jnp.stack([jnp.sum(query_pre**2, axis=-1), jnp.sum(key_pre**2, axis=-1)])
    scales = lax.rsqrt(head_sum(squares) / width + EPSILON)
    query_scale, key_scale = scales[0][:, None], scales[1][:, None]
    queries = turn(query_pre * query_scale * my_query_g, cosine, sine).astype(BF16)
    keys = turn(key_pre * key_scale * my_key_g, cosine, sine).astype(BF16)
    if share > 1:
        keys_all = lax.all_gather(keys, "expert", axis=0, tiled=True, axis_index_groups=siblings)
        values_all = lax.all_gather(values, "expert", axis=0, tiled=True, axis_index_groups=siblings)
    else:
        keys_all, values_all = keys, values
    turns = max(1, tree_rows // 2048)

    def cut_rows(values):
        return values.reshape(turns, own_rows // turns, -1)

    def attend(cut):
        return attention(*cut, keys_all, values_all)

    if turns == 1:
        attn, log_total = attention(queries, mask, keys_all, values_all)
    else:
        attn, log_total = lax.map(attend, (cut_rows(queries), cut_rows(mask)))
        attn, log_total = attn.reshape(own_rows, HEAD_DIM), log_total.reshape(own_rows, 1)
    mixed_head = attn.astype(BF16)

    def to_owners(block):
        cut = block.reshape(own_segs, rows, -1)
        if share > 1:
            cut = lax.dynamic_update_slice_in_dim(
                jnp.zeros((group, *cut.shape[1:]), cut.dtype), cut, first_seg, 0
            )
        got = expert_swap(cut)
        if share > 1:
            got = jnp.sum(got.reshape(heads, share, rows, -1), axis=1, dtype=cut.dtype)
        return got

    mixed = to_owners(mixed_head).transpose(1, 0, 2).reshape(rows, width)
    residual = token_f + mm(mixed, out_w)
    second_scale = inverse_rms(residual)
    normed_two = (residual * second_scale * ffn_g[None, :]).astype(BF16)
    logits = mm(normed_two, router_w)
    router_probs = jax.nn.softmax(logits, axis=-1)
    experts = router_w.shape[1]
    labels = jnp.arange(experts, dtype=jnp.int32)
    routed = jnp.any(routes[:, :, None] == labels[None, None, :], axis=1)
    gates_own = jnp.where(routed, router_probs, 0.0)
    gates = expert_swap(gates_own.T[:, None]).reshape(tree_rows, 1)

    rows_in = tree_gather(normed_two)
    cot_in = lax.all_gather(cotangent, "expert", axis=0, tiled=True)
    pieces = max(1, tree_rows // 2048)
    if pieces == 1:
        (sent_out, gate_grad, row_grad), sums = expert_step(
            rows_in, cot_in, gates, gate_w, up_w, down_w
        )
    else:

        def expert_turn(sums, cut):
            result, more = expert_step(*cut, gate_w, up_w, down_w)
            return tuple(s + m for s, m in zip(sums, more)), result

        zeros = tuple(jnp.zeros(w.shape, F32) for w in (gate_w, up_w, down_w))
        cuts = tuple(v.reshape(pieces, -1, v.shape[1]) for v in (rows_in, cot_in, gates))
        sums, results = lax.scan(expert_turn, zeros, cuts)
        sent_out, gate_grad, row_grad = (
            r.reshape(tree_rows, *r.shape[2:]) for r in results
        )
    gate_w_grad, up_w_grad, down_w_grad = (s.astype(BF16) for s in sums)
    combined = lax.psum_scatter(sent_out, "expert", scatter_dimension=0, tiled=True)
    output = (residual + combined.astype(F32)).astype(BF16)
    gate_grad_own = expert_swap(gate_grad.reshape(group, 1, rows)).reshape(group, rows).T
    expert_grad = tree_scatter(row_grad)
    grad_gate, grad_up, grad_down = (
        dp_sum(g).astype(F32)[None]
        for g in (gate_w_grad, up_w_grad, down_w_grad)
    )

    prob_grad = jnp.where(routed, gate_grad_own, 0.0)
    logit_grad = (
        router_probs * (prob_grad - jnp.sum(router_probs * prob_grad, axis=-1, keepdims=True))
    ).astype(BF16)
    router_grad = t_mm(normed_two, logit_grad)
    normed_two_grad = expert_grad + mm_t(logit_grad, router_w)
    ffn_gain_grad = jnp.sum(normed_two_grad * residual * second_scale, axis=0)
    weighted = normed_two_grad * ffn_g[None, :]
    residual_grad = (
        cotangent.astype(F32)
        + second_scale * weighted
        - residual * second_scale**3 * jnp.mean(weighted * residual, axis=-1, keepdims=True)
    )
    proj_grad = residual_grad.astype(BF16)

    proj_all = own_part(tree_gather(proj_grad))
    mixed_grad = mm_t(proj_all, out_head).astype(BF16)
    out_w_grad = t_mm(mixed_head, proj_all)
    row_delta = jnp.sum(mixed_grad.astype(F32) * attn, axis=-1, keepdims=True)
    back_args = (queries, mask, log_total, mixed_grad, row_delta)
    if turns == 1:
        query_grad, key_grad, value_grad = attention_back(*back_args, keys_all, values_all)
    else:

        def attention_turn(sums, cut):
            first, *more = attention_back(*cut, keys_all, values_all)
            return tuple(s + m for s, m in zip(sums, more)), first

        zeros = jnp.zeros((tree_rows, HEAD_DIM), F32)
        (key_grad, value_grad), query_grad = lax.scan(
            attention_turn, (zeros, zeros), tuple(cut_rows(v) for v in back_args)
        )
        query_grad = query_grad.reshape(own_rows, HEAD_DIM)
    if share > 1:
        key_grad = lax.psum_scatter(
            key_grad, "expert", scatter_dimension=0, tiled=True, axis_index_groups=siblings
        )
        value_grad = lax.psum_scatter(
            value_grad, "expert", scatter_dimension=0, tiled=True, axis_index_groups=siblings
        )
    query_turned = turn(query_grad, cosine, -sine)
    key_turned = turn(key_grad, cosine, -sine)
    dots = jnp.stack(
        [
            jnp.sum(query_turned * my_query_g * query_pre, axis=-1),
            jnp.sum(key_turned * my_key_g * key_pre, axis=-1),
        ]
    )
    means = head_sum(dots) / width
    query_low = query_scale * my_query_g * query_turned - query_pre * query_scale**3 * means[0][:, None]
    key_low = key_scale * my_key_g * key_turned - key_pre * key_scale**3 * means[1][:, None]
    low = jnp.concatenate([query_low, key_low, value_grad], axis=1).astype(BF16)
    query_gain_grad = jnp.sum(query_turned * query_pre * query_scale, axis=0)
    key_gain_grad = jnp.sum(key_turned * key_pre * key_scale, axis=0)
    normed_part = mm_t(low, w_head).astype(BF16)
    if share > 1:
        normed_part = lax.dynamic_update_slice_in_dim(
            jnp.zeros((tree_rows, width), BF16), normed_part, first_seg * rows, 0
        )
    normed_grad = tree_scatter(normed_part)
    attn_gain_grad = jnp.sum(normed_grad * token_f * first_scale, axis=0)
    weighted = normed_grad * attn_g[None, :]
    token_grad = (
        residual_grad
        + first_scale * weighted
        - token_f * first_scale**3 * jnp.mean(weighted * token_f, axis=-1, keepdims=True)
    )

    head_grad = t_mm(normed_all, low)
    got = both_swap(head_grad.reshape(devices, shard, 3 * HEAD_DIM)).reshape(n_dp, heads, share, shard, 3, HEAD_DIM)
    got = jnp.sum(got, axis=(0, 2)).transpose(2, 1, 0, 3).reshape(3, shard, width)
    shards_a_head = HEAD_DIM // shard
    source = dp * share + part
    flat = [(d, h * share + j) for d in range(n_dp) for h in range(heads) for j in range(share)]
    grad_out = jnp.zeros((shard, width), F32)
    for turn_index in range(shards_a_head):
        pairs = []
        for d, e in flat:
            s = d * share + e % share
            target = (e // share) * shards_a_head + (s + turn_index) % shards_a_head
            pairs.append((d * group + e, target))
        block = lax.dynamic_slice_in_dim(
            out_w_grad, ((source + turn_index) % shards_a_head) * shard, shard, 0
        )
        grad_out = grad_out + lax.ppermute(block, BOTH, pairs)
    head_gains = jnp.stack([query_gain_grad, key_gain_grad], axis=1)
    head_gains = lax.dynamic_update_slice_in_dim(
        jnp.zeros((width, 2), F32), head_gains, head * HEAD_DIM, 0
    )
    small = jnp.concatenate(
        [router_grad, attn_gain_grad[:, None], head_gains, ffn_gain_grad[:, None]], axis=1
    )
    small = jnp.sum(both_swap(small.reshape(devices, shard, -1)), axis=0)
    return (
        output,
        token_grad,
        small[:, experts],
        small[:, experts + 1],
        small[:, experts + 2],
        small[:, experts + 3],
        got[0],
        got[1],
        got[2],
        grad_out,
        small[:, :experts],
        grad_gate,
        grad_up,
        grad_down,
    )


def per_head(
    tokens, attn_gain, q_gain, k_gain, ffn_gain, w_query, w_key, w_value, w_out, router,
    w_gate, w_up, w_down, cotangent, routes, parents,
):
    rows, width = tokens.shape
    group = lax.axis_size("expert")
    n_dp = lax.axis_size("dp")
    devices = group * n_dp
    count = group * rows
    shard = w_query.shape[0]
    dp = lax.axis_index("dp")
    me = lax.axis_index("expert")
    experts = router.shape[1]

    reach = ancestry(parents)
    start = dp * group
    tree = lax.dynamic_slice(reach, (start, start), (group, group))
    depth = jnp.sum(lax.dynamic_slice_in_dim(reach, start, group, 0), axis=1)
    sees = tree + jnp.eye(group, dtype=F32)
    bias = jnp.repeat(jnp.where(sees > 0.5, 0.0, NEGATIVE), rows, axis=1)
    positions = (depth[:, None] * rows + jnp.arange(rows, dtype=F32)[None, :]).reshape(count)
    frequencies = THETA ** (-2.0 * jnp.arange(HEAD_DIM // 2, dtype=F32) / HEAD_DIM)
    angles = positions[:, None] * frequencies[None, :]
    cosine, sine = jnp.cos(angles), jnp.sin(angles)

    by_head = jnp.stack([w_query, w_key, w_value], axis=1).reshape(shard, 3, group, HEAD_DIM)
    by_head = by_head.transpose(2, 0, 1, 3).reshape(group, shard, 3 * HEAD_DIM)
    extra = jnp.concatenate(
        [
            jnp.stack([attn_gain, q_gain, k_gain, ffn_gain], axis=1),
            router,
            jnp.zeros((shard, HEAD_DIM - 4 - experts), BF16),
        ],
        axis=1,
    )
    extra = jnp.broadcast_to(extra[None], (group, shard, HEAD_DIM))
    w_cut = jnp.concatenate([by_head, extra], axis=2)
    normed_all, pre, w_all, gains, gate_w = project(tokens, w_cut, w_gate[0], n_dp, 0)
    attn_g, ffn_g = gains[0:1], gains[3:4]
    my_query_g = lax.dynamic_slice_in_dim(gains[1:2], me * HEAD_DIM, HEAD_DIM, 1)
    my_key_g = lax.dynamic_slice_in_dim(gains[2:3], me * HEAD_DIM, HEAD_DIM, 1)
    router_w = w_all[:, 3 * HEAD_DIM + 4 : 3 * HEAD_DIM + 4 + experts]
    flat = range(devices)
    blocks = []
    for r in range(n_dp):
        pairs = [(f, ((f + r) % n_dp) * group + f // n_dp) for f in flat]
        blocks.append(lax.ppermute(w_out, BOTH, pairs))
    blocks = jnp.stack(blocks)
    out_head = jnp.concatenate(
        [
            lax.dynamic_index_in_dim(blocks, (dp - i) % n_dp, 0, keepdims=False)
            for i in range(n_dp)
        ]
    )

    query_pre, key_pre = pre[:, :HEAD_DIM], pre[:, HEAD_DIM : 2 * HEAD_DIM]
    values = pre[:, 2 * HEAD_DIM :].astype(BF16)

    def head_sum(a, b, cid):
        sums = jnp.stack([jnp.sum(a, axis=-1), jnp.sum(b, axis=-1)]).reshape(1, -1, HEAD_DIM)
        sums = jnp.sum(swap(sums, ("expert",), cid), axis=0).reshape(2, count, 1)
        return sums[0] / width, sums[1] / width

    query_mean, key_mean = head_sum(query_pre**2, key_pre**2, 1)
    query_scale = lax.rsqrt(query_mean + EPSILON)
    key_scale = lax.rsqrt(key_mean + EPSILON)
    queries = turn(query_pre * query_scale * my_query_g, cosine, sine).astype(BF16)
    keys = turn(key_pre * key_scale * my_key_g, cosine, sine).astype(BF16)
    attn, lse, projected, up_w = attend(
        queries, keys, values, bias, out_head, w_up[0], n_dp, 2
    )
    token_f = tokens.astype(F32)
    residual = token_f + projected
    second_scale = inverse_rms(residual)
    normed_two = (residual * second_scale * ffn_g).astype(BF16)
    logits = mm(normed_two, router_w)
    router_probs = jax.nn.softmax(logits, axis=-1)
    labels = jnp.arange(experts, dtype=jnp.int32)
    routed = jnp.any(routes[:, :, None] == labels[None, None, :], axis=1)
    gates_own = jnp.where(routed, router_probs, 0.0)

    cap = 3 * rows * routes.shape[1] // (2 * experts)
    taken, taken_grad, hidden, gate_pre_grad, up_pre_grad, sent_out, row_grad, gate_grad = expert(
        normed_two, cotangent, gates_own.T[:, None], gate_w, up_w, w_down[0], n_dp, cap, 3
    )
    expert_grad, gate_grad_own = collect(
        row_grad.reshape(group, rows, width), gate_grad, n_dp, 4
    )
    sums = (
        t_mm(taken, gate_pre_grad),
        t_mm(taken, up_pre_grad),
        t_mm(hidden, taken_grad),
    )
    gate_grad_own = gate_grad_own.reshape(group, rows).T
    combined = lax.psum_scatter(sent_out, "expert", scatter_dimension=0, tiled=True)
    output = (residual + combined.astype(F32)).astype(BF16)

    def dp_sum(total):
        halves = total.reshape(n_dp, total.shape[0] // n_dp, -1)
        theirs = lax.dynamic_index_in_dim(halves, 1 - dp, 0, keepdims=False).astype(BF16)
        ours = lax.dynamic_index_in_dim(halves, dp, 0, keepdims=False)
        theirs = lax.ppermute(theirs, "dp", [(d, 1 - d) for d in range(n_dp)])
        return (ours + theirs.astype(F32))[None]

    grad_gate, grad_up, grad_down = (dp_sum(s) for s in sums)

    prob_grad = jnp.where(routed, gate_grad_own, 0.0)
    logit_grad = (
        router_probs * (prob_grad - jnp.sum(router_probs * prob_grad, axis=-1, keepdims=True))
    ).astype(BF16)
    router_grad = t_mm(logit_grad, normed_two)
    normed_two_grad = expert_grad + mm_t(logit_grad, router_w)
    ffn_gain_grad = jnp.sum(normed_two_grad * residual * second_scale, axis=0)
    weighted = normed_two_grad * ffn_g
    residual_grad = (
        cotangent.astype(F32)
        + second_scale * weighted
        - residual * second_scale**3 * jnp.mean(weighted * residual, axis=-1, keepdims=True)
    )
    proj_grad = residual_grad.astype(BF16)

    query_grad, key_grad, value_grad, out_w_grad = attend_back(
        proj_grad, queries, keys, values, bias, out_head, attn, lse, n_dp, 5
    )
    query_turned = turn(query_grad * SCALE, cosine, -sine)
    key_turned = turn(key_grad * SCALE, cosine, -sine)
    query_mean, key_mean = head_sum(
        query_turned * my_query_g * query_pre, key_turned * my_key_g * key_pre, 6
    )
    query_low = query_scale * my_query_g * query_turned - query_pre * query_scale**3 * query_mean
    key_low = key_scale * my_key_g * key_turned - key_pre * key_scale**3 * key_mean
    low = jnp.concatenate([query_low, key_low, value_grad], axis=1).astype(BF16)
    query_gain_grad = jnp.sum(query_turned * query_pre * query_scale, axis=0)
    key_gain_grad = jnp.sum(key_turned * key_pre * key_scale, axis=0)
    normed_grad, got = unproject(
        low, w_all, normed_all.reshape(count, width), rows, shard, n_dp, 7
    )
    attn_scale = inverse_rms(token_f)
    attn_gain_grad = jnp.sum(normed_grad * token_f * attn_scale, axis=0)
    weighted = normed_grad * attn_g
    token_grad = (
        residual_grad
        + attn_scale * weighted
        - token_f * attn_scale**3 * jnp.mean(weighted * token_f, axis=-1, keepdims=True)
    )

    got = got.reshape(group, shard, 3, HEAD_DIM).transpose(2, 1, 0, 3).reshape(3, shard, width)
    got = got.astype(F32)
    grad_out = jnp.zeros((shard, width), F32)
    halves = out_w_grad.reshape(n_dp, shard, width)
    for r in range(n_dp):
        pairs = []
        for d in range(n_dp):
            for e in range(group):
                pairs.append((d * group + e, e * n_dp + (d + r) % n_dp))
        block = lax.dynamic_index_in_dim(halves, (dp + r) % n_dp, 0, keepdims=False)
        grad_out = grad_out + lax.ppermute(block, BOTH, pairs)
    head_gains = jnp.stack([query_gain_grad, key_gain_grad])
    head_gains = lax.dynamic_update_slice_in_dim(
        jnp.zeros((2, width), F32), head_gains, me * HEAD_DIM, 1
    )
    small = jnp.concatenate([router_grad, head_gains, ffn_gain_grad[None], attn_gain_grad[None]])
    small = small.reshape(-1, devices, shard).transpose(1, 0, 2)
    small = jnp.sum(swap(small, BOTH, 8), axis=0)
    return (
        output,
        token_grad,
        small[experts + 3],
        small[experts],
        small[experts + 1],
        small[experts + 2],
        got[0],
        got[1],
        got[2],
        grad_out,
        small[:experts].T,
        grad_gate,
        grad_up,
        grad_down,
    )


def solution(mesh):
    row, vec = P(BOTH, None), P(BOTH)
    expert = P("expert", "dp", None)
    wide = mesh.shape["expert"] != HEADS or mesh.shape["dp"] != 2
    return jax.shard_map(
        per_device if wide else per_head,
        mesh=mesh,
        in_specs=(row, vec, vec, vec, vec, row, row, row, row, row, expert, expert, expert, row, row, P()),
        out_specs=(row, row, vec, vec, vec, vec, row, row, row, row, row, expert, expert, expert),
        check_vma=False,
    )
```

```python
import functools
import math

import jax
import jax.numpy as jnp
from jax import lax
from jax.experimental import pallas as pl
from jax.experimental.pallas import tpu as pltpu
from jax.sharding import PartitionSpec as P

HEAD_DIM = 128
HEADS = 16
EPSILON = 1e-05
THETA = 10000.0
NEGATIVE = -1e30
BOTH = ("dp", "expert")
F32 = jnp.float32
BF16 = jnp.bfloat16
MESH = pl.DeviceIdType.MESH


def mm(a, b):
    return lax.dot_general(a, b, (((1,), (0,)), ((), ())), preferred_element_type=F32)


def mm_t(a, b):
    return lax.dot_general(a, b, (((1,), (1,)), ((), ())), preferred_element_type=F32)


def t_mm(a, b):
    return lax.dot_general(a, b, (((0,), (0,)), ((), ())), preferred_element_type=F32)


def inverse_rms(values):
    return lax.rsqrt(jnp.mean(values * values, axis=-1, keepdims=True) + EPSILON)


def turn(values, cosine, sine):
    half = HEAD_DIM // 2
    a, b = values[:, :half], values[:, half:]
    return jnp.concatenate([a * cosine - b * sine, b * cosine + a * sine], axis=-1)


def ancestry(parents):
    count = parents.shape[0]
    labels = jnp.arange(count, dtype=jnp.int32)
    table = (parents[:, None] == labels[None, :]).astype(F32)
    for _ in range((count - 1).bit_length()):
        product = jnp.dot(table, table, precision=lax.Precision.HIGHEST, preferred_element_type=F32)
        table = jnp.minimum(table + product, 1.0)
    return table


SCALE = HEAD_DIM ** (-0.5)


SIB, ACROSS, UP, DOWN = range(4)


def spot():
    me = lax.axis_index("expert")
    return me // 4, (me // 2) % 2, me % 2


def at(z, x, c):
    return (z * 2 + x) * 2 + c


def greet_all(group, n_dp):
    me, dp = lax.axis_index("expert"), lax.axis_index("dp")
    barrier = pltpu.get_barrier_semaphore()

    def hello(k, carry):
        pl.semaphore_signal(
            barrier, inc=1, device_id={"expert": (me + k) % group}, device_id_type=MESH
        )
        return carry

    lax.fori_loop(1, group, hello, 0)
    if n_dp == 2:
        pl.semaphore_signal(barrier, inc=1, device_id={"dp": 1 - dp}, device_id_type=MESH)
    pl.semaphore_wait(barrier, group if n_dp == 2 else group - 1)


def gather_blocks(zs, buffers, process):
    z, x, c = spot()
    far = zs - 1

    def copy(n, block, kind, e):
        all_ref, send, recv = buffers[n]
        return pltpu.make_async_remote_copy(
            src_ref=all_ref.at[block],
            dst_ref=all_ref.at[block],
            send_sem=send.at[kind, block],
            recv_sem=recv.at[block],
            device_id={"expert": e},
            device_id_type=MESH,
        )

    def to_sibling(n, block):
        return copy(n, block, SIB, at(z, x, 1 - c))

    def to_across(n, block):
        return copy(n, block, ACROSS, at(z, 1 - x, c))

    def to_up(n, block):
        return copy(n, block, UP, at(z + 1, x, c))

    def to_down(n, block):
        return copy(n, block, DOWN, at(z - 1, x, c))

    def sides(d, do):
        def side(s, carry):
            zz = jnp.where(s == 0, z - d, z + d)

            @pl.when((zz >= 0) & (zz <= far) & ((d > 0) | (s == 0)))
            def _():
                do(zz)

            return carry

        lax.fori_loop(0, 2, side, 0)

    def column(n, d, zz):
        block = at(zz, x, c)

        @pl.when(d > 0)
        def _():
            to_sibling(n, block).wait_recv()

        @pl.when((zz <= z) & (z < far))
        def _():
            to_up(n, block).start()

        @pl.when((zz >= z) & (z > 0))
        def _():
            to_down(n, block).start()

        to_across(n, block).start()
        to_sibling(n, block).start()

    def across(n, zz):
        over = to_sibling(n, at(zz, 1 - x, c))
        over.wait_recv()
        over.start()

    def ready(d, zz):
        for n in range(len(buffers)):
            for xx in range(2):
                to_sibling(n, at(zz, xx, 1 - c)).wait_recv()
        process(d, zz)

    def step(d, carry):
        @pl.when(d < zs)
        def _():
            for n in range(len(buffers)):
                sides(d, lambda zz, n=n: column(n, d, zz))

        @pl.when(d > 0)
        def _():
            sides(d - 1, lambda zz: ready(d - 1, zz))

        @pl.when(d < zs)
        def _():
            for n in range(len(buffers)):
                sides(d, lambda zz, n=n: across(n, zz))

        return carry

    lax.fori_loop(0, zs + 1, step, 0)

    def done(zz, carry):
        block = at(zz, x, c)
        for n in range(len(buffers)):
            to_across(n, block).wait_send()
            to_sibling(n, block).wait_send()
            to_sibling(n, at(zz, 1 - x, c)).wait_send()

            @pl.when((zz <= z) & (z < far))
            def _():
                to_up(n, block).wait_send()

            @pl.when((zz >= z) & (z > 0))
            def _():
                to_down(n, block).wait_send()

        return carry

    lax.fori_loop(0, zs, done, 0)


def joined(own_ref, full_ref, local, send, recv):
    dp = lax.axis_index("dp")
    half = own_ref.shape[0]
    here = full_ref.at[pl.ds(dp * half, half)]
    mine = pltpu.make_async_copy(own_ref, here, local)
    theirs = over_dp(own_ref, here, send, recv)

    def start():
        mine.start()
        theirs.start()

    def finish():
        mine.wait()
        theirs.wait()

    return start, finish


def gather_sems(group):
    return [pltpu.SemaphoreType.DMA((4, group)), pltpu.SemaphoreType.DMA((group,))]


def scatter_blocks(zs, part_ref, out_ref, r_sib, r_x, r_z, s_x, s_z, send, recv, produce, pause=None, work=None):
    z, x, c = spot()
    far = zs - 1

    def to_sibling(zz, xx):
        return pltpu.make_async_remote_copy(
            src_ref=part_ref.at[at(zz, xx, 1 - c)],
            dst_ref=r_sib.at[zz * 2 + xx],
            send_sem=send.at[SIB, zz * 2 + xx],
            recv_sem=recv.at[SIB, zz * 2 + xx],
            device_id={"expert": at(z, x, 1 - c)},
            device_id_type=MESH,
        )

    def to_across(zz):
        return pltpu.make_async_remote_copy(
            src_ref=s_x.at[zz],
            dst_ref=r_x.at[zz],
            send_sem=send.at[ACROSS, zz],
            recv_sem=recv.at[ACROSS, zz],
            device_id={"expert": at(z, 1 - x, c)},
            device_id_type=MESH,
        )

    def along(zz, kind, e):
        return pltpu.make_async_remote_copy(
            src_ref=s_z.at[zz],
            dst_ref=r_z.at[kind - UP, zz],
            send_sem=send.at[kind, zz],
            recv_sem=recv.at[kind, zz],
            device_id={"expert": e},
            device_id_type=MESH,
        )

    def up(zz):
        return along(zz, UP, at(z + 1, x, c))

    def down(zz):
        return along(zz, DOWN, at(z - 1, x, c))

    def order(do, between=None):
        for d in range(far, 0, -1):
            if between is not None:
                between(far - d)

            @pl.when(z + d <= far)
            def _():
                do(z + d)

            @pl.when(z >= d)
            def _():
                do(z - d)

        if between is not None:
            between(far)
        do(z)

    def cross(zz):
        produce(at(zz, 1 - x, 1 - c))
        to_sibling(zz, 1 - x).start()
        produce(at(zz, 1 - x, c))
        to_sibling(zz, 1 - x).wait_recv()
        mine = part_ref[at(zz, 1 - x, c)].astype(F32)
        s_x[zz] = (mine + r_sib[zz * 2 + 1 - x].astype(F32)).astype(BF16)
        to_across(zz).start()

    order(cross)

    def near(zz):
        produce(at(zz, x, 1 - c))
        to_sibling(zz, x).start()
        produce(at(zz, x, c))

    order(near)
    if pause is not None:
        pause()

    def finish(zz):
        to_sibling(zz, x).wait_recv()
        to_across(zz).wait_recv()

        def here():
            mine = part_ref[at(zz, x, c)].astype(F32)
            return mine + r_sib[zz * 2 + x].astype(F32) + r_x[zz].astype(F32)

        @pl.when(zz > z)
        def _():
            @pl.when(z > 0)
            def _():
                up(zz).wait_recv()
                s_z[zz] = (here() + r_z[0, zz].astype(F32)).astype(BF16)

            @pl.when(z == 0)
            def _():
                s_z[zz] = here().astype(BF16)

            up(zz).start()

        @pl.when(zz < z)
        def _():
            @pl.when(z < far)
            def _():
                down(zz).wait_recv()
                s_z[zz] = (here() + r_z[1, zz].astype(F32)).astype(BF16)

            @pl.when(z == far)
            def _():
                s_z[zz] = here().astype(BF16)

            down(zz).start()

        @pl.when(zz == z)
        def _():
            out_ref[...] = here()

            @pl.when(z > 0)
            def _():
                up(zz).wait_recv()
                out_ref[...] += r_z[0, zz].astype(F32)

            @pl.when(z < far)
            def _():
                down(zz).wait_recv()
                out_ref[...] += r_z[1, zz].astype(F32)

    order(finish, work)

    def done(zz, carry):
        to_sibling(zz, 0).wait_send()
        to_sibling(zz, 1).wait_send()
        to_across(zz).wait_send()

        @pl.when(zz > z)
        def _():
            up(zz).wait_send()

        @pl.when(zz < z)
        def _():
            down(zz).wait_send()

        return carry

    lax.fori_loop(0, zs, done, 0)


def scatter_scratch(group, rows, width):
    zs = group // 4

    def buffer(*n):
        return pltpu.VMEM((*n, rows, width), BF16)

    return [
        buffer(2 * zs),
        buffer(zs),
        buffer(2, zs),
        buffer(zs),
        buffer(zs),
        pltpu.SemaphoreType.DMA((4, 2 * zs)),
        pltpu.SemaphoreType.DMA((4, 2 * zs)),
    ]


def over_dp(src, dst, send, recv):
    return pltpu.make_async_remote_copy(
        src_ref=src,
        dst_ref=dst,
        send_sem=send,
        recv_sem=recv,
        device_id={"dp": 1 - lax.axis_index("dp")},
        device_id_type=MESH,
    )


def tree_swap(group, make, send, recv):
    me = lax.axis_index("expert")

    def copy(k, back):
        d = (me + k) % group
        src, _ = make(d, me)
        _, dst = make(d, d if back else me)
        return pltpu.make_async_remote_copy(
            src_ref=src,
            dst_ref=dst,
            send_sem=send.at[k],
            recv_sem=recv.at[d if back else me],
            device_id={"expert": d},
            device_id_type=MESH,
        )

    def start():
        def one(k, carry):
            copy(k, False).start()
            return carry

        lax.fori_loop(1, group, one, 0)

    def finish_recv():
        def one(k, carry):
            copy(k, True).wait_recv()
            return carry

        lax.fori_loop(1, group, one, 0)

    def finish_send():
        def one(k, carry):
            copy(k, False).wait_send()
            return carry

        lax.fori_loop(1, group, one, 0)

    return start, finish_recv, finish_send


VMEM = pl.BlockSpec(memory_space=pltpu.VMEM)
HBM = pl.BlockSpec(memory_space=pl.ANY)
DMA = pltpu.SemaphoreType.DMA


def params(cid):
    return pltpu.CompilerParams(
        collective_id=cid, has_side_effects=True, vmem_limit_bytes=56 * 2**20
    )


def project_kernel(
    group, n_dp, shard,
    x_ref, w_ref, pay_ref,
    normed_ref, pre_ref, w_all, gains_ref, pay_out,
    x_all, send, recv, local, w_send, w_recv, dp_send, dp_recv, pay_send, pay_recv,
):
    me, dp = lax.axis_index("expert"), lax.axis_index("dp")
    rows = x_ref.shape[0]
    half = group * shard

    def rows_of(d, e):
        return w_all.at[pl.ds(d * half + e * shard, shard)]

    mine = pltpu.make_async_copy(x_ref, x_all.at[me], local.at[0])
    own = pltpu.make_async_copy(w_ref.at[me], rows_of(dp, me), local.at[1])
    pay_start, pay_finish = joined(pay_ref, pay_out, local.at[2], pay_send, pay_recv)
    mine.start()
    own.start()
    greet_all(group, n_dp)

    def piece(e):
        return over_dp(rows_of(dp, e), rows_of(dp, e), dp_send.at[e], dp_recv.at[e])

    def w_copy(d, src, k):
        return pltpu.make_async_remote_copy(
            src_ref=w_ref.at[d],
            dst_ref=rows_of(dp, src),
            send_sem=w_send.at[k],
            recv_sem=w_recv.at[src],
            device_id={"expert": d},
            device_id_type=MESH,
        )

    def w_start(k, carry):
        w_copy((me + k) % group, me, k).start()
        return carry

    def w_pass(k, carry):
        e = (me + group - k) % group
        w_copy((me + k) % group, e, k).wait_recv()
        piece(e).start()
        return carry

    lax.fori_loop(1, group, w_start, 0)
    pay_start()
    own.wait()
    piece(me).start()
    lax.fori_loop(1, group, w_pass, 0)
    mine.wait()
    pick = lax.broadcasted_iota(jnp.int32, (8, HEAD_DIM), 0)
    lane = lax.broadcasted_iota(jnp.int32, (8, HEAD_DIM), 1)
    pick = jnp.where(pick == lane, 1.0, 0.0).astype(BF16)

    def w_done(e, carry):
        piece(e).wait()
        return carry

    def compute(block, carry):
        values = x_all[block].astype(F32)
        scale = lax.rsqrt(jnp.mean(values * values, axis=-1, keepdims=True) + EPSILON)
        normed = (values * scale * gains_ref[0:1, :]).astype(BF16)
        normed_ref[block] = normed
        pre_ref[pl.ds(block * rows, rows), :] = mm(normed, w_all[:, : 3 * HEAD_DIM])
        return carry

    def process(d, zz):
        @pl.when(d == 0)
        def _():
            lax.fori_loop(0, group, w_done, 0)
            gains_ref[...] = mm_t(pick, w_all[:, 3 * HEAD_DIM :])

        lax.fori_loop(zz * 4, zz * 4 + 4, compute, 0)

    gather_blocks(group // 4, [(x_all, send, recv)], process)

    def w_sent(k, carry):
        w_copy((me + k) % group, me, k).wait_send()
        return carry

    lax.fori_loop(1, group, w_sent, 0)
    pay_finish()


def project(tokens, w_cut, payload, n_dp, cid):
    group, shard = w_cut.shape[0], w_cut.shape[1]
    rows, width = tokens.shape
    wide = w_cut.shape[2]
    return pl.pallas_call(
        functools.partial(project_kernel, group, n_dp, shard),
        out_shape=[
            jax.ShapeDtypeStruct((group, rows, width), BF16),
            jax.ShapeDtypeStruct((group * rows, 3 * HEAD_DIM), F32),
            jax.ShapeDtypeStruct((n_dp * group * shard, wide), BF16),
            jax.ShapeDtypeStruct((8, width), F32),
            jax.ShapeDtypeStruct((n_dp * payload.shape[0], payload.shape[1]), payload.dtype),
        ],
        in_specs=[HBM, VMEM, HBM],
        out_specs=[VMEM, VMEM, VMEM, VMEM, HBM],
        scratch_shapes=[
            pltpu.VMEM((group, rows, width), BF16),
            *gather_sems(group),
            DMA((3,)),
            DMA((group,)),
            DMA((group,)),
            DMA((group,)),
            DMA((group,)),
            DMA,
            DMA,
        ],
        compiler_params=params(cid),
    )(tokens, w_cut, payload)


def attend_kernel(
    group, n_dp,
    q_ref, k_ref, v_ref, bias_ref, w_ref, pay_ref,
    attn_ref, lse_ref, sum_ref, pay_out,
    part, r_sib, r_x, r_z, s_x, s_z, send, recv, local, dp_send, dp_recv,
):
    rows = sum_ref.shape[0]
    count = k_ref.shape[0]
    greet_all(group, n_dp)
    pay_start, pay_finish = joined(pay_ref, pay_out, local, dp_send, dp_recv)
    pay_start()

    def produce(block):
        first = block * rows
        scores = mm_t(q_ref[pl.ds(first, rows), :], k_ref[...]) * SCALE
        scores = scores + bias_ref[pl.ds(block, 1), :]
        key = lax.broadcasted_iota(jnp.int32, (rows, count), 1)
        query = first + lax.broadcasted_iota(jnp.int32, (rows, count), 0)
        scores = jnp.where(key <= query, scores, NEGATIVE)
        row_max = jnp.max(scores, axis=-1, keepdims=True)
        weights = jnp.exp(scores - row_max)
        total = jnp.sum(weights, axis=-1, keepdims=True)
        attn = mm(weights.astype(BF16), v_ref[...]) / total
        attn_ref[pl.ds(first, rows), :] = attn
        lse_ref[pl.ds(first, rows), :] = jnp.broadcast_to(row_max + jnp.log(total), (rows, HEAD_DIM))
        part[block] = mm(attn.astype(BF16), w_ref[...]).astype(BF16)

    scatter_blocks(group // 4, part, sum_ref, r_sib, r_x, r_z, s_x, s_z, send, recv, produce)
    pay_finish()


def attend(queries, keys, values, bias, w_rows, payload, n_dp, cid):
    group = bias.shape[0]
    count, width = queries.shape[0], w_rows.shape[1]
    rows = count // group
    return pl.pallas_call(
        functools.partial(attend_kernel, group, n_dp),
        out_shape=[
            jax.ShapeDtypeStruct((count, HEAD_DIM), F32),
            jax.ShapeDtypeStruct((count, HEAD_DIM), F32),
            jax.ShapeDtypeStruct((rows, width), F32),
            jax.ShapeDtypeStruct((n_dp * payload.shape[0], payload.shape[1]), payload.dtype),
        ],
        in_specs=[VMEM] * 5 + [HBM],
        out_specs=[VMEM, VMEM, VMEM, HBM],
        scratch_shapes=[
            pltpu.VMEM((group, rows, width), BF16),
            *scatter_scratch(group, rows, width),
            DMA,
            DMA,
            DMA,
        ],
        compiler_params=params(cid),
    )(queries, keys, values, bias, w_rows, payload)


def attend_back_kernel(
    group, n_dp,
    g_ref, q_ref, k_ref, v_ref, bias_ref, w_ref, attn_ref, lse_ref, pay_ref, more_ref,
    dq_ref, dk_ref, dv_ref, dw_ref, pay_out, more_out,
    g_all, send, recv, local, dp_send, dp_recv,
):
    me = lax.axis_index("expert")
    rows, width = g_ref.shape
    quad = 4 * rows
    mine = pltpu.make_async_copy(g_ref, g_all.at[me], local)
    mine.start()
    greet_all(group, n_dp)
    mine.wait()
    some = more_out.shape[0]
    payloads = [
        over_dp(pay_ref, pay_out, dp_send.at[0], dp_recv.at[0]),
        over_dp(more_ref.at[pl.ds(0, some)], more_out, dp_send.at[1], dp_recv.at[1]),
    ]
    for payload in payloads:
        payload.start()
    dk_ref[...] = jnp.zeros_like(dk_ref)
    dv_ref[...] = jnp.zeros_like(dv_ref)
    dw_ref[...] = jnp.zeros_like(dw_ref)
    query = lax.broadcasted_iota(jnp.int32, (quad, quad), 0)
    key = lax.broadcasted_iota(jnp.int32, (quad, quad), 1)

    def process(d, zz):
        here = pl.ds(zz * quad, quad)
        grad = g_all[pl.ds(zz * 4, 4)].reshape(quad, width)
        attn = attn_ref[here, :]
        mixed_grad = mm_t(grad, w_ref[...]).astype(BF16)
        dw_ref[...] += t_mm(attn.astype(BF16), grad)
        delta = jnp.sum(mixed_grad.astype(F32) * attn, axis=-1, keepdims=True)
        queries = q_ref[here, :]
        lse = lse_ref[here, :][:, :1]

        def turn_keys(j, dq):
            cut = pl.ds(pl.multiple_of(j * quad, quad), quad)
            keys = k_ref[cut, :]
            bias = jnp.concatenate(
                [
                    jnp.broadcast_to(bias_ref[pl.ds(zz * 4 + i, 1), cut], (rows, quad))
                    for i in range(4)
                ]
            )
            scores = mm_t(queries, keys) * SCALE + bias - lse
            seen = key + (j - zz) * quad <= query
            probs = jnp.exp(jnp.where(seen, scores, NEGATIVE))
            score_grad = (probs * (mm_t(mixed_grad, v_ref[cut, :]) - delta)).astype(BF16)
            dk_ref[cut, :] += t_mm(score_grad, queries)
            dv_ref[cut, :] += t_mm(probs.astype(BF16), mixed_grad)
            return dq + mm(score_grad, keys)

        dq_ref[here, :] = lax.fori_loop(
            0, zz + 1, turn_keys, jnp.zeros((quad, HEAD_DIM), F32)
        )

    gather_blocks(group // 4, [(g_all, send, recv)], process)
    for payload in payloads:
        payload.wait()


def attend_back(grad, queries, keys, values, bias, w_rows, attn, lse, payload, more, n_dp, cid):
    group = bias.shape[0]
    rows, width = grad.shape
    count = queries.shape[0]
    long = jax.ShapeDtypeStruct((count, HEAD_DIM), F32)
    return pl.pallas_call(
        functools.partial(attend_back_kernel, group, n_dp),
        out_shape=[
            long, long, long,
            jax.ShapeDtypeStruct((HEAD_DIM, width), F32),
            jax.ShapeDtypeStruct(payload.shape, payload.dtype),
            jax.ShapeDtypeStruct((more.shape[0] // 2, more.shape[1]), more.dtype),
        ],
        in_specs=[HBM] + [VMEM] * 7 + [HBM] * 2,
        out_specs=[VMEM] * 4 + [HBM] * 2,
        scratch_shapes=[
            pltpu.VMEM((group, rows, width), BF16),
            *gather_sems(group),
            DMA,
            DMA((2,)),
            DMA((2,)),
        ],
        compiler_params=params(cid),
    )(grad, queries, keys, values, bias, w_rows, attn, lse, payload, more)


def unproject_kernel(
    group, n_dp, shard,
    low_ref, w_ref, normed_ref, more_ref,
    sum_ref, got_ref, more_out,
    part, r_sib, r_x, r_z, s_x, s_z, send, recv,
    mine, theirs, w_send, w_recv, dp_send, dp_recv, pay_send, pay_recv,
):
    me, dp = lax.axis_index("expert"), lax.axis_index("dp")
    rows = sum_ref.shape[0]
    half = group * shard
    greet_all(group, n_dp)
    step = min(half, 256)

    some = more_out.shape[0]
    payloads = [
        over_dp(more_ref.at[pl.ds(some, some)], more_out, pay_send, pay_recv),
    ]

    def slice_grad(d, ref):
        def one(i, carry):
            cols = pl.ds(pl.multiple_of(d * half + i * step, step), step)
            total = jnp.zeros((step, low_ref.shape[1]), F32)
            grad = t_mm(normed_ref[:, cols], low_ref[...])
            ref[pl.ds(i * step, step), :] = (total + grad).astype(ref.dtype)
            return carry

        lax.fori_loop(0, half // step, one, 0)

    to_dp = over_dp(theirs.at[0], theirs.at[1], dp_send, dp_recv)

    def produce(block):
        low = low_ref[pl.ds(block * rows, rows), :]
        part[block] = mm_t(low, w_ref[:, : 3 * HEAD_DIM]).astype(BF16)

    def make(d, src):
        return mine.at[pl.ds(d * shard, shard)], got_ref.at[src]

    start, finish_recv, finish_send = tree_swap(group, make, w_send, w_recv)

    def work(k):
        if k == 0:
            slice_grad(1 - dp, theirs.at[0])
            to_dp.start()
            for payload in payloads:
                payload.start()
        elif k == 1:
            slice_grad(dp, mine)
        elif k == 2:
            to_dp.wait_recv()
            mine[...] = (mine[...].astype(F32) + theirs[1].astype(F32)).astype(BF16)
            start()
            got_ref[me] = mine[pl.ds(me * shard, shard), :]

    scatter_blocks(
        group // 4, part, sum_ref, r_sib, r_x, r_z, s_x, s_z, send, recv, produce, None, work
    )
    finish_recv()
    finish_send()
    to_dp.wait_send()
    for payload in payloads:
        payload.wait()


def unproject(low, w_all, normed, more, rows, shard, n_dp, cid):
    count, wide = low.shape
    width = w_all.shape[0]
    group = count // rows
    return pl.pallas_call(
        functools.partial(unproject_kernel, group, n_dp, shard),
        out_shape=[
            jax.ShapeDtypeStruct((rows, width), F32),
            jax.ShapeDtypeStruct((group, shard, wide), BF16),
            jax.ShapeDtypeStruct((more.shape[0] // 2, more.shape[1]), more.dtype),
        ],
        in_specs=[VMEM] * 3 + [HBM],
        out_specs=[VMEM] * 2 + [HBM],
        scratch_shapes=[
            pltpu.VMEM((group, rows, width), BF16),
            *scatter_scratch(group, rows, width),
            pltpu.VMEM((group * shard, wide), BF16),
            pltpu.VMEM((2, group * shard, wide), BF16),
            DMA((group,)),
            DMA((group,)),
            DMA,
            DMA,
            DMA,
            DMA,
        ],
        compiler_params=params(cid),
    )(low, w_all, normed, more)


def swap_kernel(axes, sizes, in_ref, out_ref, send, recv, local):
    count = 1
    for size in sizes:
        count *= size
    me = jnp.int32(0)
    for axis, size in zip(axes, sizes):
        me = me * size + lax.axis_index(axis)
    same = in_ref.shape[0] == 1

    def spread(d):
        where = {}
        for axis, size in zip(axes[::-1], sizes[::-1]):
            where[axis] = d % size
            d = d // size
        return where

    barrier = pltpu.get_barrier_semaphore()

    def hello(k, carry):
        pl.semaphore_signal(
            barrier, inc=1, device_id=spread((me + k) % count), device_id_type=MESH
        )
        return carry

    lax.fori_loop(1, count, hello, 0)
    pl.semaphore_wait(barrier, count - 1)

    def copy(k):
        d = (me + k) % count
        return pltpu.make_async_remote_copy(
            src_ref=in_ref.at[0 if same else d],
            dst_ref=out_ref.at[me],
            send_sem=send.at[k],
            recv_sem=recv.at[me],
            device_id=spread(d),
            device_id_type=MESH,
        )

    def start(k, carry):
        copy(k).start()
        return carry

    lax.fori_loop(1, count, start, 0)
    mine = pltpu.make_async_copy(in_ref.at[0 if same else me], out_ref.at[me], local)
    mine.start()
    mine.wait()

    def finish(k, carry):
        d = (me + k) % count
        pltpu.make_async_remote_copy(
            src_ref=in_ref.at[0],
            dst_ref=out_ref.at[d],
            send_sem=send.at[k],
            recv_sem=recv.at[d],
            device_id=spread(d),
            device_id_type=MESH,
        ).wait_recv()
        copy(k).wait_send()
        return carry

    lax.fori_loop(1, count, finish, 0)


def swap(values, axes, cid):
    sizes = tuple(lax.axis_size(axis) for axis in axes)
    count = 1
    for size in sizes:
        count *= size
    return pl.pallas_call(
        functools.partial(swap_kernel, axes, sizes),
        out_shape=jax.ShapeDtypeStruct((count, *values.shape[1:]), values.dtype),
        in_specs=[pl.BlockSpec(memory_space=pltpu.VMEM)],
        out_specs=pl.BlockSpec(memory_space=pltpu.VMEM),
        scratch_shapes=[
            pltpu.SemaphoreType.DMA((count,)),
            pltpu.SemaphoreType.DMA((count,)),
            pltpu.SemaphoreType.DMA,
        ],
        compiler_params=pltpu.CompilerParams(
            collective_id=cid, has_side_effects=True, vmem_limit_bytes=32 * 2**20
        ),
    )(values)


def expert_kernel(
    group, n_dp, cap,
    x_ref, cot_ref, gate_ref, gate_w, up_w, down_ref,
    rows_out, grads_out, hidden_out, gate_out, up_out, sent_out, row_out, gate_grads,
    x_all, c_all, down_w, gates, picks, taken, grads, gate_pre_s, up_pre_s, hidden_s, gate_s, up_s, stage,
    x_send, x_recv, c_send, c_recv, g_send, g_recv, local, dp_send, dp_recv, out_sems,
):
    me = lax.axis_index("expert")
    rows, width = x_ref.shape
    pair, quad = 2 * cap, 4 * cap
    own = [
        pltpu.make_async_copy(x_ref, x_all.at[me], local.at[0]),
        pltpu.make_async_copy(cot_ref, c_all.at[me], local.at[1]),
    ]
    for copy in own:
        copy.start()
    greet_all(group, n_dp)
    start, finish_recv, finish_send = tree_swap(
        group, lambda d, src: (gate_ref.at[d], gates.at[src]), g_send, g_recv
    )
    start()
    down_start, down_finish = joined(down_ref, down_w, local.at[2], dp_send, dp_recv)
    down_start()
    gates[me] = gate_ref[me]
    for copy in own:
        copy.wait()

    def out(n, zz):
        src = (taken, grads, hidden_s, gate_s, up_s, stage.at[0], stage.at[1])[n]
        dst = (rows_out, grads_out, hidden_out, gate_out, up_out, sent_out, row_out)[n]
        size = quad if n < 5 else 4 * rows
        return pltpu.make_async_copy(src, dst.at[pl.ds(zz * size, size)], out_sems.at[n])

    lane = lax.broadcasted_iota(jnp.int32, (rows, rows), 1)
    row = lax.broadcasted_iota(jnp.int32, (rows, rows), 0)
    before = jnp.where(row < lane, 1.0, 0.0).astype(BF16)
    pick_row = lax.broadcasted_iota(jnp.int32, (pair, 2 * rows), 0)
    pick_lane = lax.broadcasted_iota(jnp.int32, (pair, 2 * rows), 1)
    together = (pick_row >= cap) == (pick_lane >= rows)
    slot = jnp.where(pick_row >= cap, pick_row - cap, pick_row).astype(F32)

    def gate_row(p):
        return jnp.concatenate([gates[p * 2], gates[p * 2 + 1]], axis=1)

    def forward(d, zz):
        @pl.when(d > 0)
        def _():
            out(0, zz).wait()

        for j in range(2):
            p = zz * 2 + j
            ranks = []
            for i in range(2):
                routed = jnp.where(gates[p * 2 + i] > 0.0, 1.0, 0.0)
                ranks.append(mm(jnp.broadcast_to(routed, (16, rows)).astype(BF16), before)[0:1, :])
            rank = jnp.concatenate(ranks, axis=1)
            hit = together & (slot == rank) & (gate_row(p) > 0.0)
            pick = jnp.where(hit, 1.0, 0.0).astype(BF16)
            here = slice(j * pair, (j + 1) * pair)
            picks[here, :] = pick
            segments = x_all[pl.ds(p * 2, 2)].reshape(2 * rows, width)
            taken[here, :] = mm(pick, segments).astype(BF16)
        out(0, zz).start()
        gate_pre_s[...] = mm(taken[...], gate_w[...])
        up_pre_s[...] = mm(taken[...], up_w[...])

    def backward(d, zz):
        @pl.when(d > 0)
        def _():
            for n in range(1, 7):
                out(n, zz).wait()

        gate_cols = []
        for j in range(2):
            p = zz * 2 + j
            here = slice(j * pair, (j + 1) * pair)
            pick = picks[here, :]
            gate_cols.append(jnp.sum(pick.astype(F32) * gate_row(p), axis=1, keepdims=True))
            segments = c_all[pl.ds(p * 2, 2)].reshape(2 * rows, width)
            grads[here, :] = mm(pick, segments).astype(BF16)
        gate_col = jnp.concatenate(gate_cols)
        gate_pre, up_pre = gate_pre_s[...], up_pre_s[...]
        sig = 1.0 / (1.0 + jnp.exp(-gate_pre))
        silu = gate_pre * sig
        hidden_s[...] = (silu * up_pre).astype(BF16)
        out(2, zz).start()
        dots = jnp.zeros((quad, 1), F32)
        half = width // 2
        for h in range(2):
            cols = slice(h * half, (h + 1) * half)
            result = mm(hidden_s[...], down_w[:, cols]).astype(BF16).astype(F32)
            cot = grads[:, cols].astype(F32)
            dots = dots + jnp.sum(cot * result, axis=1, keepdims=True)
            grads[:, cols] = (gate_col * cot).astype(BF16)
            sent = (gate_col * result).astype(BF16)
            for j in range(2):
                here = slice(j * pair, (j + 1) * pair)
                there = slice(j * 2 * rows, (j + 1) * 2 * rows)
                stage[0, there, cols] = t_mm(picks[here, :], sent[here]).astype(BF16)
        out(1, zz).start()
        out(5, zz).start()
        for j in range(2):
            here = slice(j * pair, (j + 1) * pair)
            gate_grad = jnp.sum(picks[here, :].astype(F32) * dots[here], axis=0, keepdims=True)
            for i in range(2):
                gate_grads[(zz * 2 + j) * 2 + i] = gate_grad[:, i * rows : (i + 1) * rows]
        hidden_grad = mm_t(grads[...], down_w[...]).astype(BF16).astype(F32)
        slope = sig * (1.0 + gate_pre * (1.0 - sig))
        gate_s[...] = (hidden_grad * up_pre * slope).astype(BF16)
        up_s[...] = (hidden_grad * silu).astype(BF16)
        out(3, zz).start()
        out(4, zz).start()
        for h in range(2):
            cols = slice(h * half, (h + 1) * half)
            grad = mm_t(gate_s[...], gate_w[cols, :]) + mm_t(up_s[...], up_w[cols, :])
            grad = grad.astype(BF16)
            for j in range(2):
                here = slice(j * pair, (j + 1) * pair)
                there = slice(j * 2 * rows, (j + 1) * 2 * rows)
                stage[1, there, cols] = t_mm(picks[here, :], grad[here]).astype(BF16)
        out(6, zz).start()

    first = lax.axis_index("expert") // 4

    def process(d, zz):
        @pl.when(zz == first)
        def _():
            finish_recv()

        forward(d, zz)

        @pl.when(zz == first)
        def _():
            down_finish()

        backward(d, zz)

    gather_blocks(group // 4, [(x_all, x_send, x_recv), (c_all, c_send, c_recv)], process)
    for n in range(7):
        out(n, first).wait()
    finish_send()


def expert(x, cot, gates, gate_w, up_w, down_w, n_dp, cap, cid):
    group = gates.shape[0]
    rows, width = x.shape
    hidden = gate_w.shape[1]
    total = group * cap
    quad = 4 * cap

    def shape(*dims, dtype=BF16):
        return jax.ShapeDtypeStruct(dims, dtype)

    def buffer(*dims):
        return pltpu.VMEM(dims, BF16)

    return pl.pallas_call(
        functools.partial(expert_kernel, group, n_dp, cap),
        out_shape=[
            shape(total, width),
            shape(total, width),
            shape(total, hidden),
            shape(total, hidden),
            shape(total, hidden),
            shape(group * rows, width),
            shape(group * rows, width),
            shape(*gates.shape, dtype=F32),
        ],
        in_specs=[HBM, HBM, VMEM, VMEM, VMEM, HBM],
        out_specs=[HBM] * 7 + [VMEM],
        scratch_shapes=[
            buffer(group, rows, width),
            buffer(group, rows, width),
            buffer(n_dp * down_w.shape[0], width),
            pltpu.VMEM(gates.shape, F32),
            buffer(quad, 2 * rows),
            buffer(quad, width),
            buffer(quad, width),
            pltpu.VMEM((quad, hidden), F32),
            pltpu.VMEM((quad, hidden), F32),
            buffer(quad, hidden),
            buffer(quad, hidden),
            buffer(quad, hidden),
            buffer(2, 4 * rows, width),
            *gather_sems(group),
            *gather_sems(group),
            DMA((group,)),
            DMA((group,)),
            DMA((3,)),
            DMA,
            DMA,
            DMA((7,)),
        ],
        compiler_params=pltpu.CompilerParams(
            collective_id=cid, has_side_effects=True, vmem_limit_bytes=60 * 2**20
        ),
    )(x, cot, gates, gate_w, up_w, down_w)


def collect_kernel(
    group, n_dp,
    part, gate_ref, taken, grads, hidden, gate_grad, up_grad,
    sum_ref, gates_ref, gate_own, up_own, down_own, gate_dp, up_dp, down_dp, gate_in,
    r_sib, r_x, r_z, s_x, s_z, send, recv, g_send, g_recv, tile, tile_low, sems, dp_send, dp_recv,
):
    me, dp = lax.axis_index("expert"), lax.axis_index("dp")
    greet_all(group, n_dp)
    start, finish_recv, finish_send = tree_swap(
        group, lambda d, src: (gate_ref.at[d], gates_ref.at[src]), g_send, g_recv
    )
    start()
    gates_ref[me] = gate_ref[me]
    step, wide = tile.shape

    def product(left, right, own_out, dp_out, cols):
        half = own_out.shape[0]
        pieces = half // step

        def one(i, carry):
            there = pl.ds(i * step, step)
            for whose, buffer, ref, sem in (
                (1 - dp, tile_low, dp_out, sems.at[0]),
                (dp, tile, own_out, sems.at[1]),
            ):
                rows = pl.ds(pl.multiple_of(whose * half + i * step, step), step)
                buffer[...] = t_mm(left[:, rows], right[:, cols]).astype(buffer.dtype)
                put = pltpu.make_async_copy(buffer, ref.at[there, cols], sem)
                put.start()
                put.wait()
            return carry

        lax.fori_loop(0, pieces, one, 0)

    exchange = over_dp(gate_dp, gate_in, dp_send, dp_recv)

    def work(k):
        if k == 0:
            product(taken, gate_grad, gate_own, gate_dp, slice(0, wide))
            exchange.start()
        elif k == 1:
            product(taken, up_grad, up_own, up_dp, slice(0, wide))
        elif k == 2:
            for h in range(grads.shape[1] // wide):
                product(hidden, grads, down_own, down_dp, slice(h * wide, (h + 1) * wide))

    scatter_blocks(
        group // 4, part, sum_ref, r_sib, r_x, r_z, s_x, s_z, send, recv,
        lambda block: None, None, work,
    )
    finish_recv()
    finish_send()
    exchange.wait()


def collect(parts, gates, taken, grads, hidden, gate_grad, up_grad, n_dp, cid):
    group, rows, width = parts.shape
    narrow = hidden.shape[1]

    def halves(a, b):
        return a.shape[1] // n_dp, b.shape[1]

    shapes = [halves(taken, gate_grad), halves(taken, up_grad), halves(hidden, grads)]
    return pl.pallas_call(
        functools.partial(collect_kernel, group, n_dp),
        out_shape=[
            jax.ShapeDtypeStruct((rows, width), F32),
            jax.ShapeDtypeStruct(gates.shape, gates.dtype),
            *(jax.ShapeDtypeStruct(s, F32) for s in shapes),
            *(jax.ShapeDtypeStruct(s, BF16) for s in shapes),
            jax.ShapeDtypeStruct(shapes[0], BF16),
        ],
        in_specs=[VMEM] * 7,
        out_specs=[VMEM, VMEM] + [HBM] * 7,
        scratch_shapes=[
            *scatter_scratch(group, rows, width),
            DMA((group,)),
            DMA((group,)),
            pltpu.VMEM((256, narrow), F32),
            pltpu.VMEM((256, narrow), BF16),
            DMA((2,)),
            DMA,
            DMA,
        ],
        compiler_params=pltpu.CompilerParams(
            collective_id=cid, has_side_effects=True, vmem_limit_bytes=60 * 2**20
        ),
    )(parts, gates, taken, grads, hidden, gate_grad, up_grad)


def attention(queries, mask, keys, values):
    scores = jnp.where(mask, mm_t(queries, keys) * SCALE, NEGATIVE)
    row_max = jnp.max(scores, axis=-1, keepdims=True)
    weights = jnp.exp(scores - row_max)
    total = jnp.sum(weights, axis=-1, keepdims=True)
    attn = mm(weights.astype(BF16), values) / total
    return attn, row_max + jnp.log(total)


def attention_back(queries, mask, log_total, mixed_grad, row_delta, keys, values):
    probs = jnp.exp(jnp.where(mask, mm_t(queries, keys) * SCALE - log_total, NEGATIVE))
    score_grad = (probs * (mm_t(mixed_grad, values) - row_delta)).astype(BF16)
    query_grad = mm(score_grad, keys) * SCALE
    key_grad = t_mm(score_grad, queries) * SCALE
    return query_grad, key_grad, t_mm(probs.astype(BF16), mixed_grad)


def expert_step(rows_in, cot_in, gates, gate_w, up_w, down_w):
    cot_in = cot_in.astype(F32)
    gate_pre = mm(rows_in, gate_w)
    up_pre = mm(rows_in, up_w)
    sig = jax.nn.sigmoid(gate_pre)
    silu = gate_pre * sig
    hidden = (silu * up_pre).astype(BF16)
    expert_out = mm(hidden, down_w).astype(BF16).astype(F32)
    sent_out = (gates * expert_out).astype(BF16)
    gate_grad = jnp.sum(cot_in * expert_out, axis=-1)
    out_grad = (gates * cot_in).astype(BF16)
    hidden_grad = mm_t(out_grad, down_w).astype(BF16).astype(F32)
    gate_pre_grad = (hidden_grad * up_pre * sig * (1.0 + gate_pre * (1.0 - sig))).astype(BF16)
    up_pre_grad = (hidden_grad * silu).astype(BF16)
    row_grad = (mm_t(gate_pre_grad, gate_w) + mm_t(up_pre_grad, up_w)).astype(BF16)
    sums = (t_mm(rows_in, gate_pre_grad), t_mm(rows_in, up_pre_grad), t_mm(hidden, out_grad))
    return (sent_out, gate_grad, row_grad), sums


def per_device(
    tokens, attn_gain, q_gain, k_gain, ffn_gain, w_query, w_key, w_value, w_out, router,
    w_gate, w_up, w_down, cotangent, routes, parents,
):
    rows, width = tokens.shape
    heads = width // HEAD_DIM
    group = lax.axis_size("expert")
    n_dp = lax.axis_size("dp")
    devices = group * n_dp
    share = max(1, group // heads)
    tree_rows = group * rows
    own_rows = tree_rows // share
    shard = w_query.shape[0]
    dp = lax.axis_index("dp")
    me = lax.axis_index("expert")
    head = me // share
    part = me % share
    peers = [[h * share + j for h in range(heads)] for j in range(share)]
    siblings = [[h * share + j for j in range(share)] for h in range(heads)]

    reach = ancestry(parents)
    start = dp * group
    tree = lax.dynamic_slice(reach, (start, start), (group, group))
    depth = jnp.sum(lax.dynamic_slice_in_dim(reach, start, group, 0), axis=1)
    sees = tree + jnp.eye(group, dtype=F32)
    own_segs = own_rows // rows
    first_seg = part * own_segs
    my_depth = lax.dynamic_slice_in_dim(depth, first_seg, own_segs, 0)
    my_sees = lax.dynamic_slice_in_dim(sees, first_seg, own_segs, 0)
    place = jnp.arange(rows, dtype=F32)
    positions = (my_depth[:, None] * rows + place[None, :]).reshape(own_rows)
    frequencies = THETA ** (-2.0 * jnp.arange(HEAD_DIM // 2, dtype=F32) / HEAD_DIM)
    angles = positions[:, None] * frequencies[None, :]
    cosine, sine = jnp.cos(angles), jnp.sin(angles)
    key_index = jnp.arange(tree_rows, dtype=jnp.int32)
    query_index = first_seg * rows + jnp.arange(own_rows, dtype=jnp.int32)
    seen = jnp.repeat(jnp.repeat(my_sees, rows, axis=0), rows, axis=1) > 0.5
    mask = seen & (key_index[None, :] <= query_index[:, None])

    def own_part(values):
        return lax.dynamic_slice_in_dim(values, first_seg * rows, own_rows, 0)

    def head_sum(values):
        return lax.psum(values, "expert", axis_index_groups=peers if share > 1 else None)

    def tree_gather(values):
        return lax.all_gather(values, "expert", axis=0, tiled=True)

    def tree_scatter(values):
        return lax.psum_scatter(values, "expert", scatter_dimension=0, tiled=True).astype(F32)

    def both_swap(values):
        return lax.all_to_all(values, BOTH, 0, 0, tiled=True)

    def expert_swap(values):
        return lax.all_to_all(values, "expert", 0, 0, tiled=True)

    others = [(d, (d + 1) % n_dp) for d in range(n_dp)]

    def dp_join(values):
        if n_dp != 2:
            return lax.all_gather(values, "dp", axis=0, tiled=True)
        other = lax.ppermute(values, "dp", others)
        return jnp.where(
            dp == 0, jnp.concatenate([values, other]), jnp.concatenate([other, values])
        )

    def dp_sum(values):
        if n_dp != 2:
            return lax.psum_scatter(values, "dp", scatter_dimension=0, tiled=True)
        halves = values.reshape(2, values.shape[0] // 2, -1)
        theirs = lax.dynamic_index_in_dim(halves, 1 - dp, 0, keepdims=False)
        ours = lax.dynamic_index_in_dim(halves, dp, 0, keepdims=False)
        return ours.astype(F32) + lax.ppermute(theirs, "dp", others).astype(F32)

    gains = lax.all_gather(
        jnp.stack([attn_gain, q_gain, k_gain, ffn_gain], axis=1), BOTH, axis=0, tiled=True
    ).astype(F32)
    attn_g, query_g, key_g, ffn_g = gains[:, 0], gains[:, 1], gains[:, 2], gains[:, 3]
    my_query_g = lax.dynamic_slice_in_dim(query_g, head * HEAD_DIM, HEAD_DIM, 0)[None, :]
    my_key_g = lax.dynamic_slice_in_dim(key_g, head * HEAD_DIM, HEAD_DIM, 0)[None, :]
    by_head = jnp.stack([w_query, w_key, w_value], axis=1).reshape(shard, 3, heads, HEAD_DIM)
    by_head = by_head.transpose(2, 0, 1, 3).reshape(1, heads, 1, shard, 3 * HEAD_DIM)
    by_head = jnp.broadcast_to(by_head, (n_dp, heads, share, shard, 3 * HEAD_DIM))
    w_head = both_swap(by_head.reshape(devices, shard, 3 * HEAD_DIM)).reshape(
        width, 3 * HEAD_DIM
    )
    out_w = lax.all_gather(w_out, BOTH, axis=0, tiled=True)
    out_head = lax.dynamic_slice_in_dim(out_w, head * HEAD_DIM, HEAD_DIM, 0)
    router_w = lax.all_gather(router, BOTH, axis=0, tiled=True)
    gate_w = dp_join(w_gate[0])
    up_w = dp_join(w_up[0])
    down_w = dp_join(w_down[0])

    token_f = tokens.astype(F32)
    first_scale = inverse_rms(token_f)
    normed = (token_f * first_scale * attn_g[None, :]).astype(BF16)
    normed_all = own_part(tree_gather(normed))
    pre = mm(normed_all, w_head)
    query_pre, key_pre = pre[:, :HEAD_DIM], pre[:, HEAD_DIM : 2 * HEAD_DIM]
    values = pre[:, 2 * HEAD_DIM :].astype(BF16)
    squares = jnp.stack([jnp.sum(query_pre**2, axis=-1), jnp.sum(key_pre**2, axis=-1)])
    scales = lax.rsqrt(head_sum(squares) / width + EPSILON)
    query_scale, key_scale = scales[0][:, None], scales[1][:, None]
    queries = turn(query_pre * query_scale * my_query_g, cosine, sine).astype(BF16)
    keys = turn(key_pre * key_scale * my_key_g, cosine, sine).astype(BF16)
    if share > 1:
        keys_all = lax.all_gather(keys, "expert", axis=0, tiled=True, axis_index_groups=siblings)
        values_all = lax.all_gather(values, "expert", axis=0, tiled=True, axis_index_groups=siblings)
    else:
        keys_all, values_all = keys, values
    turns = max(1, tree_rows // 2048)

    def cut_rows(values):
        return values.reshape(turns, own_rows // turns, -1)

    def attend(cut):
        return attention(*cut, keys_all, values_all)

    if turns == 1:
        attn, log_total = attention(queries, mask, keys_all, values_all)
    else:
        attn, log_total = lax.map(attend, (cut_rows(queries), cut_rows(mask)))
        attn, log_total = attn.reshape(own_rows, HEAD_DIM), log_total.reshape(own_rows, 1)
    mixed_head = attn.astype(BF16)

    def to_owners(block):
        cut = block.reshape(own_segs, rows, -1)
        if share > 1:
            cut = lax.dynamic_update_slice_in_dim(
                jnp.zeros((group, *cut.shape[1:]), cut.dtype), cut, first_seg, 0
            )
        got = expert_swap(cut)
        if share > 1:
            got = jnp.sum(got.reshape(heads, share, rows, -1), axis=1, dtype=cut.dtype)
        return got

    mixed = to_owners(mixed_head).transpose(1, 0, 2).reshape(rows, width)
    residual = token_f + mm(mixed, out_w)
    second_scale = inverse_rms(residual)
    normed_two = (residual * second_scale * ffn_g[None, :]).astype(BF16)
    logits = mm(normed_two, router_w)
    router_probs = jax.nn.softmax(logits, axis=-1)
    experts = router_w.shape[1]
    labels = jnp.arange(experts, dtype=jnp.int32)
    routed = jnp.any(routes[:, :, None] == labels[None, None, :], axis=1)
    gates_own = jnp.where(routed, router_probs, 0.0)
    gates = expert_swap(gates_own.T[:, None]).reshape(tree_rows, 1)

    rows_in = tree_gather(normed_two)
    cot_in = lax.all_gather(cotangent, "expert", axis=0, tiled=True)
    pieces = max(1, tree_rows // 2048)
    if pieces == 1:
        (sent_out, gate_grad, row_grad), sums = expert_step(
            rows_in, cot_in, gates, gate_w, up_w, down_w
        )
    else:

        def expert_turn(sums, cut):
            result, more = expert_step(*cut, gate_w, up_w, down_w)
            return tuple(s + m for s, m in zip(sums, more)), result

        zeros = tuple(jnp.zeros(w.shape, F32) for w in (gate_w, up_w, down_w))
        cuts = tuple(v.reshape(pieces, -1, v.shape[1]) for v in (rows_in, cot_in, gates))
        sums, results = lax.scan(expert_turn, zeros, cuts)
        sent_out, gate_grad, row_grad = (
            r.reshape(tree_rows, *r.shape[2:]) for r in results
        )
    gate_w_grad, up_w_grad, down_w_grad = (s.astype(BF16) for s in sums)
    combined = lax.psum_scatter(sent_out, "expert", scatter_dimension=0, tiled=True)
    output = (residual + combined.astype(F32)).astype(BF16)
    gate_grad_own = expert_swap(gate_grad.reshape(group, 1, rows)).reshape(group, rows).T
    expert_grad = tree_scatter(row_grad)
    grad_gate, grad_up, grad_down = (
        dp_sum(g).astype(F32)[None]
        for g in (gate_w_grad, up_w_grad, down_w_grad)
    )

    prob_grad = jnp.where(routed, gate_grad_own, 0.0)
    logit_grad = (
        router_probs * (prob_grad - jnp.sum(router_probs * prob_grad, axis=-1, keepdims=True))
    ).astype(BF16)
    router_grad = t_mm(normed_two, logit_grad)
    normed_two_grad = expert_grad + mm_t(logit_grad, router_w)
    ffn_gain_grad = jnp.sum(normed_two_grad * residual * second_scale, axis=0)
    weighted = normed_two_grad * ffn_g[None, :]
    residual_grad = (
        cotangent.astype(F32)
        + second_scale * weighted
        - residual * second_scale**3 * jnp.mean(weighted * residual, axis=-1, keepdims=True)
    )
    proj_grad = residual_grad.astype(BF16)

    proj_all = own_part(tree_gather(proj_grad))
    mixed_grad = mm_t(proj_all, out_head).astype(BF16)
    out_w_grad = t_mm(mixed_head, proj_all)
    row_delta = jnp.sum(mixed_grad.astype(F32) * attn, axis=-1, keepdims=True)
    back_args = (queries, mask, log_total, mixed_grad, row_delta)
    if turns == 1:
        query_grad, key_grad, value_grad = attention_back(*back_args, keys_all, values_all)
    else:

        def attention_turn(sums, cut):
            first, *more = attention_back(*cut, keys_all, values_all)
            return tuple(s + m for s, m in zip(sums, more)), first

        zeros = jnp.zeros((tree_rows, HEAD_DIM), F32)
        (key_grad, value_grad), query_grad = lax.scan(
            attention_turn, (zeros, zeros), tuple(cut_rows(v) for v in back_args)
        )
        query_grad = query_grad.reshape(own_rows, HEAD_DIM)
    if share > 1:
        key_grad = lax.psum_scatter(
            key_grad, "expert", scatter_dimension=0, tiled=True, axis_index_groups=siblings
        )
        value_grad = lax.psum_scatter(
            value_grad, "expert", scatter_dimension=0, tiled=True, axis_index_groups=siblings
        )
    query_turned = turn(query_grad, cosine, -sine)
    key_turned = turn(key_grad, cosine, -sine)
    dots = jnp.stack(
        [
            jnp.sum(query_turned * my_query_g * query_pre, axis=-1),
            jnp.sum(key_turned * my_key_g * key_pre, axis=-1),
        ]
    )
    means = head_sum(dots) / width
    query_low = query_scale * my_query_g * query_turned - query_pre * query_scale**3 * means[0][:, None]
    key_low = key_scale * my_key_g * key_turned - key_pre * key_scale**3 * means[1][:, None]
    low = jnp.concatenate([query_low, key_low, value_grad], axis=1).astype(BF16)
    query_gain_grad = jnp.sum(query_turned * query_pre * query_scale, axis=0)
    key_gain_grad = jnp.sum(key_turned * key_pre * key_scale, axis=0)
    normed_part = mm_t(low, w_head).astype(BF16)
    if share > 1:
        normed_part = lax.dynamic_update_slice_in_dim(
            jnp.zeros((tree_rows, width), BF16), normed_part, first_seg * rows, 0
        )
    normed_grad = tree_scatter(normed_part)
    attn_gain_grad = jnp.sum(normed_grad * token_f * first_scale, axis=0)
    weighted = normed_grad * attn_g[None, :]
    token_grad = (
        residual_grad
        + first_scale * weighted
        - token_f * first_scale**3 * jnp.mean(weighted * token_f, axis=-1, keepdims=True)
    )

    head_grad = t_mm(normed_all, low)
    got = both_swap(head_grad.reshape(devices, shard, 3 * HEAD_DIM)).reshape(n_dp, heads, share, shard, 3, HEAD_DIM)
    got = jnp.sum(got, axis=(0, 2)).transpose(2, 1, 0, 3).reshape(3, shard, width)
    shards_a_head = HEAD_DIM // shard
    source = dp * share + part
    flat = [(d, h * share + j) for d in range(n_dp) for h in range(heads) for j in range(share)]
    grad_out = jnp.zeros((shard, width), F32)
    for turn_index in range(shards_a_head):
        pairs = []
        for d, e in flat:
            s = d * share + e % share
            target = (e // share) * shards_a_head + (s + turn_index) % shards_a_head
            pairs.append((d * group + e, target))
        block = lax.dynamic_slice_in_dim(
            out_w_grad, ((source + turn_index) % shards_a_head) * shard, shard, 0
        )
        grad_out = grad_out + lax.ppermute(block, BOTH, pairs)
    head_gains = jnp.stack([query_gain_grad, key_gain_grad], axis=1)
    head_gains = lax.dynamic_update_slice_in_dim(
        jnp.zeros((width, 2), F32), head_gains, head * HEAD_DIM, 0
    )
    small = jnp.concatenate(
        [router_grad, attn_gain_grad[:, None], head_gains, ffn_gain_grad[:, None]], axis=1
    )
    small = jnp.sum(both_swap(small.reshape(devices, shard, -1)), axis=0)
    return (
        output,
        token_grad,
        small[:, experts],
        small[:, experts + 1],
        small[:, experts + 2],
        small[:, experts + 3],
        got[0],
        got[1],
        got[2],
        grad_out,
        small[:, :experts],
        grad_gate,
        grad_up,
        grad_down,
    )


def per_head(
    tokens, attn_gain, q_gain, k_gain, ffn_gain, w_query, w_key, w_value, w_out, router,
    w_gate, w_up, w_down, cotangent, routes, parents,
):
    rows, width = tokens.shape
    group = lax.axis_size("expert")
    n_dp = lax.axis_size("dp")
    devices = group * n_dp
    count = group * rows
    shard = w_query.shape[0]
    dp = lax.axis_index("dp")
    me = lax.axis_index("expert")
    experts = router.shape[1]

    reach = ancestry(parents)
    start = dp * group
    tree = lax.dynamic_slice(reach, (start, start), (group, group))
    depth = jnp.sum(lax.dynamic_slice_in_dim(reach, start, group, 0), axis=1)
    sees = tree + jnp.eye(group, dtype=F32)
    bias = jnp.repeat(jnp.where(sees > 0.5, 0.0, NEGATIVE), rows, axis=1)
    positions = (depth[:, None] * rows + jnp.arange(rows, dtype=F32)[None, :]).reshape(count)
    frequencies = THETA ** (-2.0 * jnp.arange(HEAD_DIM // 2, dtype=F32) / HEAD_DIM)
    angles = positions[:, None] * frequencies[None, :]
    cosine, sine = jnp.cos(angles), jnp.sin(angles)

    by_head = jnp.stack([w_query, w_key, w_value], axis=1).reshape(shard, 3, group, HEAD_DIM)
    by_head = by_head.transpose(2, 0, 1, 3).reshape(group, shard, 3 * HEAD_DIM)
    extra = jnp.concatenate(
        [
            jnp.stack([attn_gain, q_gain, k_gain, ffn_gain], axis=1),
            router,
            jnp.zeros((shard, HEAD_DIM - 4 - experts), BF16),
        ],
        axis=1,
    )
    extra = jnp.broadcast_to(extra[None], (group, shard, HEAD_DIM))
    w_cut = jnp.concatenate([by_head, extra], axis=2)
    normed_all, pre, w_all, gains, gate_w = project(tokens, w_cut, w_gate[0], n_dp, 0)
    attn_g, ffn_g = gains[0:1], gains[3:4]
    my_query_g = lax.dynamic_slice_in_dim(gains[1:2], me * HEAD_DIM, HEAD_DIM, 1)
    my_key_g = lax.dynamic_slice_in_dim(gains[2:3], me * HEAD_DIM, HEAD_DIM, 1)
    router_w = w_all[:, 3 * HEAD_DIM + 4 : 3 * HEAD_DIM + 4 + experts]
    flat = range(devices)
    blocks = []
    for r in range(n_dp):
        pairs = [(f, ((f + r) % n_dp) * group + f // n_dp) for f in flat]
        blocks.append(lax.ppermute(w_out, BOTH, pairs))
    blocks = jnp.stack(blocks)
    out_head = jnp.concatenate(
        [
            lax.dynamic_index_in_dim(blocks, (dp - i) % n_dp, 0, keepdims=False)
            for i in range(n_dp)
        ]
    )

    query_pre, key_pre = pre[:, :HEAD_DIM], pre[:, HEAD_DIM : 2 * HEAD_DIM]
    values = pre[:, 2 * HEAD_DIM :].astype(BF16)

    def head_sum(a, b, cid):
        sums = jnp.stack([jnp.sum(a, axis=-1), jnp.sum(b, axis=-1)]).reshape(1, -1, HEAD_DIM)
        sums = jnp.sum(swap(sums, ("expert",), cid), axis=0).reshape(2, count, 1)
        return sums[0] / width, sums[1] / width

    query_mean, key_mean = head_sum(query_pre**2, key_pre**2, 1)
    query_scale = lax.rsqrt(query_mean + EPSILON)
    key_scale = lax.rsqrt(key_mean + EPSILON)
    queries = turn(query_pre * query_scale * my_query_g, cosine, sine).astype(BF16)
    keys = turn(key_pre * key_scale * my_key_g, cosine, sine).astype(BF16)
    attn, lse, projected, up_w = attend(
        queries, keys, values, bias, out_head, w_up[0], n_dp, 2
    )
    token_f = tokens.astype(F32)
    residual = token_f + projected
    second_scale = inverse_rms(residual)
    normed_two = (residual * second_scale * ffn_g).astype(BF16)
    logits = mm(normed_two, router_w)
    router_probs = jax.nn.softmax(logits, axis=-1)
    labels = jnp.arange(experts, dtype=jnp.int32)
    routed = jnp.any(routes[:, :, None] == labels[None, None, :], axis=1)
    gates_own = jnp.where(routed, router_probs, 0.0)

    cap = 3 * rows * routes.shape[1] // (2 * experts)
    taken, taken_grad, hidden, gate_pre_grad, up_pre_grad, sent_out, row_grad, gate_grad = expert(
        normed_two, cotangent, gates_own.T[:, None], gate_w, up_w, w_down[0], n_dp, cap, 3
    )
    expert_grad, gate_grad_own, gate_own, up_own, down_own, _, up_dp, down_dp, gate_in = collect(
        row_grad.reshape(group, rows, width),
        gate_grad, taken, taken_grad, hidden, gate_pre_grad, up_pre_grad, n_dp, 4,
    )
    gate_grad_own = gate_grad_own.reshape(group, rows).T
    combined = lax.psum_scatter(sent_out, "expert", scatter_dimension=0, tiled=True)

    prob_grad = jnp.where(routed, gate_grad_own, 0.0)
    logit_grad = (
        router_probs * (prob_grad - jnp.sum(router_probs * prob_grad, axis=-1, keepdims=True))
    ).astype(BF16)
    router_grad = t_mm(logit_grad, normed_two)
    normed_two_grad = expert_grad + mm_t(logit_grad, router_w)
    ffn_gain_grad = jnp.sum(normed_two_grad * residual * second_scale, axis=0)
    weighted = normed_two_grad * ffn_g
    residual_grad = (
        cotangent.astype(F32)
        + second_scale * weighted
        - residual * second_scale**3 * jnp.mean(weighted * residual, axis=-1, keepdims=True)
    )
    proj_grad = residual_grad.astype(BF16)

    query_grad, key_grad, value_grad, out_w_grad, up_in, down_first = attend_back(
        proj_grad, queries, keys, values, bias, out_head, attn, lse, up_dp, down_dp, n_dp, 5
    )
    query_turned = turn(query_grad * SCALE, cosine, -sine)
    key_turned = turn(key_grad * SCALE, cosine, -sine)
    query_mean, key_mean = head_sum(
        query_turned * my_query_g * query_pre, key_turned * my_key_g * key_pre, 6
    )
    query_low = query_scale * my_query_g * query_turned - query_pre * query_scale**3 * query_mean
    key_low = key_scale * my_key_g * key_turned - key_pre * key_scale**3 * key_mean
    low = jnp.concatenate([query_low, key_low, value_grad], axis=1).astype(BF16)
    combined, low = lax.optimization_barrier((combined, low))
    output = (residual + combined.astype(F32)).astype(BF16)
    query_gain_grad = jnp.sum(query_turned * query_pre * query_scale, axis=0)
    key_gain_grad = jnp.sum(key_turned * key_pre * key_scale, axis=0)
    normed_grad, got, down_second = unproject(
        low, w_all, normed_all.reshape(count, width), down_dp, rows, shard, n_dp, 7
    )
    grad_gate = (gate_own + gate_in.astype(F32))[None]
    grad_up = (up_own + up_in.astype(F32))[None]
    grad_down = (down_own + jnp.concatenate([down_first, down_second]).astype(F32))[None]
    attn_scale = inverse_rms(token_f)
    attn_gain_grad = jnp.sum(normed_grad * token_f * attn_scale, axis=0)
    weighted = normed_grad * attn_g
    token_grad = (
        residual_grad
        + attn_scale * weighted
        - token_f * attn_scale**3 * jnp.mean(weighted * token_f, axis=-1, keepdims=True)
    )

    got = got.reshape(group, shard, 3, HEAD_DIM).transpose(2, 1, 0, 3).reshape(3, shard, width)
    got = got.astype(F32)
    grad_out = jnp.zeros((shard, width), F32)
    halves = out_w_grad.reshape(n_dp, shard, width)
    for r in range(n_dp):
        pairs = []
        for d in range(n_dp):
            for e in range(group):
                pairs.append((d * group + e, e * n_dp + (d + r) % n_dp))
        block = lax.dynamic_index_in_dim(halves, (dp + r) % n_dp, 0, keepdims=False)
        grad_out = grad_out + lax.ppermute(block, BOTH, pairs)
    head_gains = jnp.stack([query_gain_grad, key_gain_grad])
    head_gains = lax.dynamic_update_slice_in_dim(
        jnp.zeros((2, width), F32), head_gains, me * HEAD_DIM, 1
    )
    small = jnp.concatenate([router_grad, head_gains, ffn_gain_grad[None], attn_gain_grad[None]])
    small = small.reshape(-1, devices, shard).transpose(1, 0, 2)
    small = jnp.sum(swap(small, BOTH, 8), axis=0)
    return (
        output,
        token_grad,
        small[experts + 3],
        small[experts],
        small[experts + 1],
        small[experts + 2],
        got[0],
        got[1],
        got[2],
        grad_out,
        small[:experts].T,
        grad_gate,
        grad_up,
        grad_down,
    )


def solution(mesh):
    row, vec = P(BOTH, None), P(BOTH)
    expert = P("expert", "dp", None)
    wide = mesh.shape["expert"] != HEADS or mesh.shape["dp"] != 2
    return jax.shard_map(
        per_device if wide else per_head,
        mesh=mesh,
        in_specs=(row, vec, vec, vec, vec, row, row, row, row, row, expert, expert, expert, row, row, P()),
        out_specs=(row, row, vec, vec, vec, vec, row, row, row, row, row, expert, expert, expert),
        check_vma=False,
    )
```

```python
import functools
import math

import jax
import jax.numpy as jnp
from jax import lax
from jax.experimental import pallas as pl
from jax.experimental.pallas import tpu as pltpu
from jax.sharding import PartitionSpec as P

HEAD_DIM = 128
HEADS = 16
EPSILON = 1e-05
THETA = 10000.0
NEGATIVE = -1e30
BOTH = ("dp", "expert")
F32 = jnp.float32
BF16 = jnp.bfloat16
MESH = pl.DeviceIdType.MESH


def mm(a, b):
    return lax.dot_general(a, b, (((1,), (0,)), ((), ())), preferred_element_type=F32)


def mm_t(a, b):
    return lax.dot_general(a, b, (((1,), (1,)), ((), ())), preferred_element_type=F32)


def t_mm(a, b):
    return lax.dot_general(a, b, (((0,), (0,)), ((), ())), preferred_element_type=F32)


def inverse_rms(values):
    return lax.rsqrt(jnp.mean(values * values, axis=-1, keepdims=True) + EPSILON)


def turn(values, cosine, sine):
    half = HEAD_DIM // 2
    a, b = values[:, :half], values[:, half:]
    return jnp.concatenate([a * cosine - b * sine, b * cosine + a * sine], axis=-1)


def ancestry(parents):
    count = parents.shape[0]
    labels = jnp.arange(count, dtype=jnp.int32)
    table = (parents[:, None] == labels[None, :]).astype(F32)
    for _ in range((count - 1).bit_length()):
        product = jnp.dot(table, table, precision=lax.Precision.HIGHEST, preferred_element_type=F32)
        table = jnp.minimum(table + product, 1.0)
    return table


SCALE = HEAD_DIM ** (-0.5)


SIB, ACROSS, UP, DOWN = range(4)


def spot():
    me = lax.axis_index("expert")
    return me // 4, (me // 2) % 2, me % 2


def at(z, x, c):
    return (z * 2 + x) * 2 + c


def greet_all(group, n_dp):
    me, dp = lax.axis_index("expert"), lax.axis_index("dp")
    barrier = pltpu.get_barrier_semaphore()

    def hello(k, carry):
        pl.semaphore_signal(
            barrier, inc=1, device_id={"expert": (me + k) % group}, device_id_type=MESH
        )
        return carry

    lax.fori_loop(1, group, hello, 0)
    if n_dp == 2:
        pl.semaphore_signal(barrier, inc=1, device_id={"dp": 1 - dp}, device_id_type=MESH)
    pl.semaphore_wait(barrier, group if n_dp == 2 else group - 1)


def gather_blocks(zs, buffers, process):
    z, x, c = spot()
    far = zs - 1

    def copy(n, block, kind, e):
        all_ref, send, recv = buffers[n]
        return pltpu.make_async_remote_copy(
            src_ref=all_ref.at[block],
            dst_ref=all_ref.at[block],
            send_sem=send.at[kind, block],
            recv_sem=recv.at[block],
            device_id={"expert": e},
            device_id_type=MESH,
        )

    def to_sibling(n, block):
        return copy(n, block, SIB, at(z, x, 1 - c))

    def to_across(n, block):
        return copy(n, block, ACROSS, at(z, 1 - x, c))

    def to_up(n, block):
        return copy(n, block, UP, at(z + 1, x, c))

    def to_down(n, block):
        return copy(n, block, DOWN, at(z - 1, x, c))

    def sides(d, do):
        def side(s, carry):
            zz = jnp.where(s == 0, z - d, z + d)

            @pl.when((zz >= 0) & (zz <= far) & ((d > 0) | (s == 0)))
            def _():
                do(zz)

            return carry

        lax.fori_loop(0, 2, side, 0)

    def column(n, d, zz):
        block = at(zz, x, c)

        @pl.when(d > 0)
        def _():
            to_sibling(n, block).wait_recv()

        @pl.when((zz <= z) & (z < far))
        def _():
            to_up(n, block).start()

        @pl.when((zz >= z) & (z > 0))
        def _():
            to_down(n, block).start()

        to_across(n, block).start()
        to_sibling(n, block).start()

    def across(n, zz):
        over = to_sibling(n, at(zz, 1 - x, c))
        over.wait_recv()
        over.start()

    def ready(d, zz):
        for n in range(len(buffers)):
            for xx in range(2):
                to_sibling(n, at(zz, xx, 1 - c)).wait_recv()
        process(d, zz)

    def step(d, carry):
        @pl.when(d < zs)
        def _():
            for n in range(len(buffers)):
                sides(d, lambda zz, n=n: column(n, d, zz))

        @pl.when(d > 0)
        def _():
            sides(d - 1, lambda zz: ready(d - 1, zz))

        @pl.when(d < zs)
        def _():
            for n in range(len(buffers)):
                sides(d, lambda zz, n=n: across(n, zz))

        return carry

    lax.fori_loop(0, zs + 1, step, 0)

    def done(zz, carry):
        block = at(zz, x, c)
        for n in range(len(buffers)):
            to_across(n, block).wait_send()
            to_sibling(n, block).wait_send()
            to_sibling(n, at(zz, 1 - x, c)).wait_send()

            @pl.when((zz <= z) & (z < far))
            def _():
                to_up(n, block).wait_send()

            @pl.when((zz >= z) & (z > 0))
            def _():
                to_down(n, block).wait_send()

        return carry

    lax.fori_loop(0, zs, done, 0)


def joined(own_ref, full_ref, local, send, recv):
    dp = lax.axis_index("dp")
    half = own_ref.shape[0]
    here = full_ref.at[pl.ds(dp * half, half)]
    mine = pltpu.make_async_copy(own_ref, here, local)
    theirs = over_dp(own_ref, here, send, recv)

    def start():
        mine.start()
        theirs.start()

    def finish():
        mine.wait()
        theirs.wait()

    return start, finish


def gather_sems(group):
    return [pltpu.SemaphoreType.DMA((4, group)), pltpu.SemaphoreType.DMA((group,))]


def scatter_blocks(zs, part_ref, out_ref, r_sib, r_x, r_z, s_x, s_z, send, recv, produce, pause=None, work=None):
    z, x, c = spot()
    far = zs - 1

    def to_sibling(zz, xx):
        return pltpu.make_async_remote_copy(
            src_ref=part_ref.at[at(zz, xx, 1 - c)],
            dst_ref=r_sib.at[zz * 2 + xx],
            send_sem=send.at[SIB, zz * 2 + xx],
            recv_sem=recv.at[SIB, zz * 2 + xx],
            device_id={"expert": at(z, x, 1 - c)},
            device_id_type=MESH,
        )

    def to_across(zz):
        return pltpu.make_async_remote_copy(
            src_ref=s_x.at[zz],
            dst_ref=r_x.at[zz],
            send_sem=send.at[ACROSS, zz],
            recv_sem=recv.at[ACROSS, zz],
            device_id={"expert": at(z, 1 - x, c)},
            device_id_type=MESH,
        )

    def along(zz, kind, e):
        return pltpu.make_async_remote_copy(
            src_ref=s_z.at[zz],
            dst_ref=r_z.at[kind - UP, zz],
            send_sem=send.at[kind, zz],
            recv_sem=recv.at[kind, zz],
            device_id={"expert": e},
            device_id_type=MESH,
        )

    def up(zz):
        return along(zz, UP, at(z + 1, x, c))

    def down(zz):
        return along(zz, DOWN, at(z - 1, x, c))

    def order(do, between=None):
        for d in range(far, 0, -1):
            if between is not None:
                between(far - d)

            @pl.when(z + d <= far)
            def _():
                do(z + d)

            @pl.when(z >= d)
            def _():
                do(z - d)

        if between is not None:
            between(far)
        do(z)

    def cross(zz):
        produce(at(zz, 1 - x, 1 - c))
        to_sibling(zz, 1 - x).start()
        produce(at(zz, 1 - x, c))
        to_sibling(zz, 1 - x).wait_recv()
        mine = part_ref[at(zz, 1 - x, c)].astype(F32)
        s_x[zz] = (mine + r_sib[zz * 2 + 1 - x].astype(F32)).astype(BF16)
        to_across(zz).start()

    order(cross)

    def near(zz):
        produce(at(zz, x, 1 - c))
        to_sibling(zz, x).start()
        produce(at(zz, x, c))

    order(near)
    if pause is not None:
        pause()

    def finish(zz):
        to_sibling(zz, x).wait_recv()
        to_across(zz).wait_recv()

        def here():
            mine = part_ref[at(zz, x, c)].astype(F32)
            return mine + r_sib[zz * 2 + x].astype(F32) + r_x[zz].astype(F32)

        @pl.when(zz > z)
        def _():
            @pl.when(z > 0)
            def _():
                up(zz).wait_recv()
                s_z[zz] = (here() + r_z[0, zz].astype(F32)).astype(BF16)

            @pl.when(z == 0)
            def _():
                s_z[zz] = here().astype(BF16)

            up(zz).start()

        @pl.when(zz < z)
        def _():
            @pl.when(z < far)
            def _():
                down(zz).wait_recv()
                s_z[zz] = (here() + r_z[1, zz].astype(F32)).astype(BF16)

            @pl.when(z == far)
            def _():
                s_z[zz] = here().astype(BF16)

            down(zz).start()

        @pl.when(zz == z)
        def _():
            out_ref[...] = here()

            @pl.when(z > 0)
            def _():
                up(zz).wait_recv()
                out_ref[...] += r_z[0, zz].astype(F32)

            @pl.when(z < far)
            def _():
                down(zz).wait_recv()
                out_ref[...] += r_z[1, zz].astype(F32)

    order(finish, work)

    def done(zz, carry):
        to_sibling(zz, 0).wait_send()
        to_sibling(zz, 1).wait_send()
        to_across(zz).wait_send()

        @pl.when(zz > z)
        def _():
            up(zz).wait_send()

        @pl.when(zz < z)
        def _():
            down(zz).wait_send()

        return carry

    lax.fori_loop(0, zs, done, 0)


def scatter_scratch(group, rows, width):
    zs = group // 4

    def buffer(*n):
        return pltpu.VMEM((*n, rows, width), BF16)

    return [
        buffer(2 * zs),
        buffer(zs),
        buffer(2, zs),
        buffer(zs),
        buffer(zs),
        pltpu.SemaphoreType.DMA((4, 2 * zs)),
        pltpu.SemaphoreType.DMA((4, 2 * zs)),
    ]


def over_dp(src, dst, send, recv):
    return pltpu.make_async_remote_copy(
        src_ref=src,
        dst_ref=dst,
        send_sem=send,
        recv_sem=recv,
        device_id={"dp": 1 - lax.axis_index("dp")},
        device_id_type=MESH,
    )


def tree_swap(group, make, send, recv):
    me = lax.axis_index("expert")

    def copy(k, back):
        d = (me + k) % group
        src, _ = make(d, me)
        _, dst = make(d, d if back else me)
        return pltpu.make_async_remote_copy(
            src_ref=src,
            dst_ref=dst,
            send_sem=send.at[k],
            recv_sem=recv.at[d if back else me],
            device_id={"expert": d},
            device_id_type=MESH,
        )

    def start():
        def one(k, carry):
            copy(k, False).start()
            return carry

        lax.fori_loop(1, group, one, 0)

    def finish_recv():
        def one(k, carry):
            copy(k, True).wait_recv()
            return carry

        lax.fori_loop(1, group, one, 0)

    def finish_send():
        def one(k, carry):
            copy(k, False).wait_send()
            return carry

        lax.fori_loop(1, group, one, 0)

    return start, finish_recv, finish_send


VMEM = pl.BlockSpec(memory_space=pltpu.VMEM)
HBM = pl.BlockSpec(memory_space=pl.ANY)
DMA = pltpu.SemaphoreType.DMA


def params(cid):
    return pltpu.CompilerParams(
        collective_id=cid, has_side_effects=True, vmem_limit_bytes=56 * 2**20
    )


def project_kernel(
    group, n_dp, shard,
    x_ref, w_ref, pay_ref,
    normed_ref, pre_ref, w_all, gains_ref, pay_out,
    x_all, send, recv, local, w_send, w_recv, dp_send, dp_recv, pay_send, pay_recv,
):
    me, dp = lax.axis_index("expert"), lax.axis_index("dp")
    rows = x_ref.shape[0]
    half = group * shard

    def rows_of(d, e):
        return w_all.at[pl.ds(d * half + e * shard, shard)]

    mine = pltpu.make_async_copy(x_ref, x_all.at[me], local.at[0])
    own = pltpu.make_async_copy(w_ref.at[me], rows_of(dp, me), local.at[1])
    pay_start, pay_finish = joined(pay_ref, pay_out, local.at[2], pay_send, pay_recv)
    mine.start()
    own.start()
    greet_all(group, n_dp)

    def piece(e):
        return over_dp(rows_of(dp, e), rows_of(dp, e), dp_send.at[e], dp_recv.at[e])

    def w_copy(d, src, k):
        return pltpu.make_async_remote_copy(
            src_ref=w_ref.at[d],
            dst_ref=rows_of(dp, src),
            send_sem=w_send.at[k],
            recv_sem=w_recv.at[src],
            device_id={"expert": d},
            device_id_type=MESH,
        )

    def w_start(k, carry):
        w_copy((me + k) % group, me, k).start()
        return carry

    def w_pass(k, carry):
        e = (me + group - k) % group
        w_copy((me + k) % group, e, k).wait_recv()
        piece(e).start()
        return carry

    lax.fori_loop(1, group, w_start, 0)
    pay_start()
    own.wait()
    piece(me).start()
    lax.fori_loop(1, group, w_pass, 0)
    mine.wait()
    pick = lax.broadcasted_iota(jnp.int32, (8, HEAD_DIM), 0)
    lane = lax.broadcasted_iota(jnp.int32, (8, HEAD_DIM), 1)
    pick = jnp.where(pick == lane, 1.0, 0.0).astype(BF16)

    def w_done(e, carry):
        piece(e).wait()
        return carry

    def compute(block, carry):
        values = x_all[block].astype(F32)
        scale = lax.rsqrt(jnp.mean(values * values, axis=-1, keepdims=True) + EPSILON)
        normed = (values * scale * gains_ref[0:1, :]).astype(BF16)
        normed_ref[block] = normed
        pre_ref[pl.ds(block * rows, rows), :] = mm(normed, w_all[:, : 3 * HEAD_DIM])
        return carry

    def process(d, zz):
        @pl.when(d == 0)
        def _():
            lax.fori_loop(0, group, w_done, 0)
            gains_ref[...] = mm_t(pick, w_all[:, 3 * HEAD_DIM :])

        lax.fori_loop(zz * 4, zz * 4 + 4, compute, 0)

    gather_blocks(group // 4, [(x_all, send, recv)], process)

    def w_sent(k, carry):
        w_copy((me + k) % group, me, k).wait_send()
        return carry

    lax.fori_loop(1, group, w_sent, 0)
    pay_finish()


def project(tokens, w_cut, payload, n_dp, cid):
    group, shard = w_cut.shape[0], w_cut.shape[1]
    rows, width = tokens.shape
    wide = w_cut.shape[2]
    return pl.pallas_call(
        functools.partial(project_kernel, group, n_dp, shard),
        out_shape=[
            jax.ShapeDtypeStruct((group, rows, width), BF16),
            jax.ShapeDtypeStruct((group * rows, 3 * HEAD_DIM), F32),
            jax.ShapeDtypeStruct((n_dp * group * shard, wide), BF16),
            jax.ShapeDtypeStruct((8, width), F32),
            jax.ShapeDtypeStruct((n_dp * payload.shape[0], payload.shape[1]), payload.dtype),
        ],
        in_specs=[HBM, VMEM, HBM],
        out_specs=[VMEM, VMEM, VMEM, VMEM, HBM],
        scratch_shapes=[
            pltpu.VMEM((group, rows, width), BF16),
            *gather_sems(group),
            DMA((3,)),
            DMA((group,)),
            DMA((group,)),
            DMA((group,)),
            DMA((group,)),
            DMA,
            DMA,
        ],
        compiler_params=params(cid),
    )(tokens, w_cut, payload)


def attend_kernel(
    group, n_dp,
    q_ref, k_ref, v_ref, bias_ref, w_ref, pay_ref,
    attn_ref, lse_ref, sum_ref, pay_out,
    part, r_sib, r_x, r_z, s_x, s_z, send, recv, local, dp_send, dp_recv,
):
    rows = sum_ref.shape[0]
    count = k_ref.shape[0]
    greet_all(group, n_dp)
    pay_start, pay_finish = joined(pay_ref, pay_out, local, dp_send, dp_recv)
    pay_start()

    def produce(block):
        first = block * rows
        scores = mm_t(q_ref[pl.ds(first, rows), :], k_ref[...]) * SCALE
        scores = scores + bias_ref[pl.ds(block, 1), :]
        key = lax.broadcasted_iota(jnp.int32, (rows, count), 1)
        query = first + lax.broadcasted_iota(jnp.int32, (rows, count), 0)
        scores = jnp.where(key <= query, scores, NEGATIVE)
        row_max = jnp.max(scores, axis=-1, keepdims=True)
        weights = jnp.exp(scores - row_max)
        total = jnp.sum(weights, axis=-1, keepdims=True)
        attn = mm(weights.astype(BF16), v_ref[...]) / total
        attn_ref[pl.ds(first, rows), :] = attn
        lse_ref[pl.ds(first, rows), :] = jnp.broadcast_to(row_max + jnp.log(total), (rows, HEAD_DIM))
        part[block] = mm(attn.astype(BF16), w_ref[...]).astype(BF16)

    scatter_blocks(group // 4, part, sum_ref, r_sib, r_x, r_z, s_x, s_z, send, recv, produce)
    pay_finish()


def attend(queries, keys, values, bias, w_rows, payload, n_dp, cid):
    group = bias.shape[0]
    count, width = queries.shape[0], w_rows.shape[1]
    rows = count // group
    return pl.pallas_call(
        functools.partial(attend_kernel, group, n_dp),
        out_shape=[
            jax.ShapeDtypeStruct((count, HEAD_DIM), F32),
            jax.ShapeDtypeStruct((count, HEAD_DIM), F32),
            jax.ShapeDtypeStruct((rows, width), F32),
            jax.ShapeDtypeStruct((n_dp * payload.shape[0], payload.shape[1]), payload.dtype),
        ],
        in_specs=[VMEM] * 5 + [HBM],
        out_specs=[VMEM, VMEM, VMEM, HBM],
        scratch_shapes=[
            pltpu.VMEM((group, rows, width), BF16),
            *scatter_scratch(group, rows, width),
            DMA,
            DMA,
            DMA,
        ],
        compiler_params=params(cid),
    )(queries, keys, values, bias, w_rows, payload)


def attend_back_kernel(
    group, n_dp,
    g_ref, q_ref, k_ref, v_ref, bias_ref, w_ref, attn_ref, lse_ref, pay_ref, more_ref,
    dq_ref, dk_ref, dv_ref, dw_ref, pay_out, more_out,
    g_all, send, recv, local, dp_send, dp_recv,
):
    me = lax.axis_index("expert")
    rows, width = g_ref.shape
    quad = 4 * rows
    mine = pltpu.make_async_copy(g_ref, g_all.at[me], local)
    mine.start()
    greet_all(group, n_dp)
    mine.wait()
    some = more_out.shape[0]
    payloads = [
        over_dp(pay_ref, pay_out, dp_send.at[0], dp_recv.at[0]),
        over_dp(more_ref.at[pl.ds(0, some)], more_out, dp_send.at[1], dp_recv.at[1]),
    ]
    for payload in payloads:
        payload.start()
    dk_ref[...] = jnp.zeros_like(dk_ref)
    dv_ref[...] = jnp.zeros_like(dv_ref)
    dw_ref[...] = jnp.zeros_like(dw_ref)
    query = lax.broadcasted_iota(jnp.int32, (quad, quad), 0)
    key = lax.broadcasted_iota(jnp.int32, (quad, quad), 1)

    def process(d, zz):
        here = pl.ds(zz * quad, quad)
        grad = g_all[pl.ds(zz * 4, 4)].reshape(quad, width)
        attn = attn_ref[here, :]
        mixed_grad = mm_t(grad, w_ref[...]).astype(BF16)
        dw_ref[...] += t_mm(attn.astype(BF16), grad)
        delta = jnp.sum(mixed_grad.astype(F32) * attn, axis=-1, keepdims=True)
        queries = q_ref[here, :]
        lse = lse_ref[here, :][:, :1]

        def turn_keys(j, dq):
            cut = pl.ds(pl.multiple_of(j * quad, quad), quad)
            keys = k_ref[cut, :]
            bias = jnp.concatenate(
                [
                    jnp.broadcast_to(bias_ref[pl.ds(zz * 4 + i, 1), cut], (rows, quad))
                    for i in range(4)
                ]
            )
            scores = mm_t(queries, keys) * SCALE + bias - lse
            seen = key + (j - zz) * quad <= query
            probs = jnp.exp(jnp.where(seen, scores, NEGATIVE))
            score_grad = (probs * (mm_t(mixed_grad, v_ref[cut, :]) - delta)).astype(BF16)
            dk_ref[cut, :] += t_mm(score_grad, queries)
            dv_ref[cut, :] += t_mm(probs.astype(BF16), mixed_grad)
            return dq + mm(score_grad, keys)

        dq_ref[here, :] = lax.fori_loop(
            0, zz + 1, turn_keys, jnp.zeros((quad, HEAD_DIM), F32)
        )

    gather_blocks(group // 4, [(g_all, send, recv)], process)
    for payload in payloads:
        payload.wait()


def attend_back(grad, queries, keys, values, bias, w_rows, attn, lse, payload, more, n_dp, cid):
    group = bias.shape[0]
    rows, width = grad.shape
    count = queries.shape[0]
    long = jax.ShapeDtypeStruct((count, HEAD_DIM), F32)
    return pl.pallas_call(
        functools.partial(attend_back_kernel, group, n_dp),
        out_shape=[
            long, long, long,
            jax.ShapeDtypeStruct((HEAD_DIM, width), F32),
            jax.ShapeDtypeStruct(payload.shape, payload.dtype),
            jax.ShapeDtypeStruct((more.shape[0] // 2, more.shape[1]), more.dtype),
        ],
        in_specs=[HBM] + [VMEM] * 7 + [HBM] * 2,
        out_specs=[VMEM] * 4 + [HBM] * 2,
        scratch_shapes=[
            pltpu.VMEM((group, rows, width), BF16),
            *gather_sems(group),
            DMA,
            DMA((2,)),
            DMA((2,)),
        ],
        compiler_params=params(cid),
    )(grad, queries, keys, values, bias, w_rows, attn, lse, payload, more)


def unproject_kernel(
    group, n_dp, shard,
    low_ref, w_ref, normed_ref, more_ref,
    sum_ref, wq_ref, wk_ref, wv_ref, more_out,
    got_ref, part, r_sib, r_x, r_z, s_x, s_z, send, recv,
    mine, theirs, w_send, w_recv, dp_send, dp_recv, pay_send, pay_recv,
):
    me, dp = lax.axis_index("expert"), lax.axis_index("dp")
    rows = sum_ref.shape[0]
    half = group * shard
    greet_all(group, n_dp)
    step = min(half, 256)

    some = more_out.shape[0]
    payloads = [
        over_dp(more_ref.at[pl.ds(some, some)], more_out, pay_send, pay_recv),
    ]

    def slice_grad(d, ref):
        def one(i, carry):
            cols = pl.ds(pl.multiple_of(d * half + i * step, step), step)
            total = jnp.zeros((step, low_ref.shape[1]), F32)
            grad = t_mm(normed_ref[:, cols], low_ref[...])
            ref[pl.ds(i * step, step), :] = (total + grad).astype(ref.dtype)
            return carry

        lax.fori_loop(0, half // step, one, 0)

    to_dp = over_dp(theirs.at[0], theirs.at[1], dp_send, dp_recv)

    def produce(block):
        low = low_ref[pl.ds(block * rows, rows), :]
        part[block] = mm_t(low, w_ref[:, : 3 * HEAD_DIM]).astype(BF16)

    def make(d, src):
        return mine.at[pl.ds(d * shard, shard)], got_ref.at[src]

    start, finish_recv, finish_send = tree_swap(group, make, w_send, w_recv)

    def work(k):
        if k == 0:
            slice_grad(1 - dp, theirs.at[0])
            to_dp.start()
            for payload in payloads:
                payload.start()
        elif k == 1:
            slice_grad(dp, mine)
        elif k == 2:
            to_dp.wait_recv()
            mine[...] = (mine[...].astype(F32) + theirs[1].astype(F32)).astype(BF16)
            start()
            got_ref[me] = mine[pl.ds(me * shard, shard), :]

    scatter_blocks(
        group // 4, part, sum_ref, r_sib, r_x, r_z, s_x, s_z, send, recv, produce, None, work
    )
    finish_recv()
    for e in range(group):
        for n, ref in enumerate((wq_ref, wk_ref, wv_ref)):
            cols = slice(n * HEAD_DIM, (n + 1) * HEAD_DIM)
            ref[:, e * HEAD_DIM : (e + 1) * HEAD_DIM] = got_ref[e, :, cols].astype(F32)
    finish_send()
    to_dp.wait_send()
    for payload in payloads:
        payload.wait()


def unproject(low, w_all, normed, more, rows, shard, n_dp, cid):
    count, wide = low.shape
    width = w_all.shape[0]
    group = count // rows
    return pl.pallas_call(
        functools.partial(unproject_kernel, group, n_dp, shard),
        out_shape=[
            jax.ShapeDtypeStruct((rows, width), F32),
            *(jax.ShapeDtypeStruct((shard, width), F32) for _ in range(3)),
            jax.ShapeDtypeStruct((more.shape[0] // 2, more.shape[1]), more.dtype),
        ],
        in_specs=[VMEM] * 3 + [HBM],
        out_specs=[VMEM] * 4 + [HBM],
        scratch_shapes=[
            pltpu.VMEM((group, shard, wide), BF16),
            pltpu.VMEM((group, rows, width), BF16),
            *scatter_scratch(group, rows, width),
            pltpu.VMEM((group * shard, wide), BF16),
            pltpu.VMEM((2, group * shard, wide), BF16),
            DMA((group,)),
            DMA((group,)),
            DMA,
            DMA,
            DMA,
            DMA,
        ],
        compiler_params=params(cid),
    )(low, w_all, normed, more)


def swap_kernel(axes, sizes, in_ref, out_ref, send, recv, local):
    count = 1
    for size in sizes:
        count *= size
    me = jnp.int32(0)
    for axis, size in zip(axes, sizes):
        me = me * size + lax.axis_index(axis)
    same = in_ref.shape[0] == 1

    def spread(d):
        where = {}
        for axis, size in zip(axes[::-1], sizes[::-1]):
            where[axis] = d % size
            d = d // size
        return where

    barrier = pltpu.get_barrier_semaphore()

    def hello(k, carry):
        pl.semaphore_signal(
            barrier, inc=1, device_id=spread((me + k) % count), device_id_type=MESH
        )
        return carry

    lax.fori_loop(1, count, hello, 0)
    pl.semaphore_wait(barrier, count - 1)

    def copy(k):
        d = (me + k) % count
        return pltpu.make_async_remote_copy(
            src_ref=in_ref.at[0 if same else d],
            dst_ref=out_ref.at[me],
            send_sem=send.at[k],
            recv_sem=recv.at[me],
            device_id=spread(d),
            device_id_type=MESH,
        )

    def start(k, carry):
        copy(k).start()
        return carry

    lax.fori_loop(1, count, start, 0)
    mine = pltpu.make_async_copy(in_ref.at[0 if same else me], out_ref.at[me], local)
    mine.start()
    mine.wait()

    def finish(k, carry):
        d = (me + k) % count
        pltpu.make_async_remote_copy(
            src_ref=in_ref.at[0],
            dst_ref=out_ref.at[d],
            send_sem=send.at[k],
            recv_sem=recv.at[d],
            device_id=spread(d),
            device_id_type=MESH,
        ).wait_recv()
        copy(k).wait_send()
        return carry

    lax.fori_loop(1, count, finish, 0)


def swap(values, axes, cid):
    sizes = tuple(lax.axis_size(axis) for axis in axes)
    count = 1
    for size in sizes:
        count *= size
    return pl.pallas_call(
        functools.partial(swap_kernel, axes, sizes),
        out_shape=jax.ShapeDtypeStruct((count, *values.shape[1:]), values.dtype),
        in_specs=[pl.BlockSpec(memory_space=pltpu.VMEM)],
        out_specs=pl.BlockSpec(memory_space=pltpu.VMEM),
        scratch_shapes=[
            pltpu.SemaphoreType.DMA((count,)),
            pltpu.SemaphoreType.DMA((count,)),
            pltpu.SemaphoreType.DMA,
        ],
        compiler_params=pltpu.CompilerParams(
            collective_id=cid, has_side_effects=True, vmem_limit_bytes=32 * 2**20
        ),
    )(values)


def expert_kernel(
    group, n_dp, cap,
    x_ref, cot_ref, gate_ref, gate_w, up_w, down_ref,
    rows_out, grads_out, hidden_out, gate_out, up_out, sent_out, row_out, gate_grads,
    x_all, c_all, down_w, gates, picks, taken, grads, gate_pre_s, up_pre_s, hidden_s, gate_s, up_s, stage,
    x_send, x_recv, c_send, c_recv, g_send, g_recv, local, dp_send, dp_recv, out_sems,
):
    me = lax.axis_index("expert")
    rows, width = x_ref.shape
    pair, quad = 2 * cap, 4 * cap
    own = [
        pltpu.make_async_copy(x_ref, x_all.at[me], local.at[0]),
        pltpu.make_async_copy(cot_ref, c_all.at[me], local.at[1]),
    ]
    for copy in own:
        copy.start()
    greet_all(group, n_dp)
    start, finish_recv, finish_send = tree_swap(
        group, lambda d, src: (gate_ref.at[d], gates.at[src]), g_send, g_recv
    )
    start()
    down_start, down_finish = joined(down_ref, down_w, local.at[2], dp_send, dp_recv)
    down_start()
    gates[me] = gate_ref[me]
    for copy in own:
        copy.wait()

    def out(n, zz):
        src = (taken, grads, hidden_s, gate_s, up_s, stage.at[0], stage.at[1])[n]
        dst = (rows_out, grads_out, hidden_out, gate_out, up_out, sent_out, row_out)[n]
        size = quad if n < 5 else 4 * rows
        return pltpu.make_async_copy(src, dst.at[pl.ds(zz * size, size)], out_sems.at[n])

    lane = lax.broadcasted_iota(jnp.int32, (rows, rows), 1)
    row = lax.broadcasted_iota(jnp.int32, (rows, rows), 0)
    before = jnp.where(row < lane, 1.0, 0.0).astype(BF16)
    pick_row = lax.broadcasted_iota(jnp.int32, (pair, 2 * rows), 0)
    pick_lane = lax.broadcasted_iota(jnp.int32, (pair, 2 * rows), 1)
    together = (pick_row >= cap) == (pick_lane >= rows)
    slot = jnp.where(pick_row >= cap, pick_row - cap, pick_row).astype(F32)

    def gate_row(p):
        return jnp.concatenate([gates[p * 2], gates[p * 2 + 1]], axis=1)

    def forward(d, zz):
        @pl.when(d > 0)
        def _():
            out(0, zz).wait()

        for j in range(2):
            p = zz * 2 + j
            ranks = []
            for i in range(2):
                routed = jnp.where(gates[p * 2 + i] > 0.0, 1.0, 0.0)
                ranks.append(mm(jnp.broadcast_to(routed, (16, rows)).astype(BF16), before)[0:1, :])
            rank = jnp.concatenate(ranks, axis=1)
            hit = together & (slot == rank) & (gate_row(p) > 0.0)
            pick = jnp.where(hit, 1.0, 0.0).astype(BF16)
            here = slice(j * pair, (j + 1) * pair)
            picks[here, :] = pick
            segments = x_all[pl.ds(p * 2, 2)].reshape(2 * rows, width)
            taken[here, :] = mm(pick, segments).astype(BF16)
        out(0, zz).start()
        gate_pre_s[...] = mm(taken[...], gate_w[...])
        up_pre_s[...] = mm(taken[...], up_w[...])

    def backward(d, zz):
        @pl.when(d > 0)
        def _():
            for n in range(1, 7):
                out(n, zz).wait()

        gate_cols = []
        for j in range(2):
            p = zz * 2 + j
            here = slice(j * pair, (j + 1) * pair)
            pick = picks[here, :]
            gate_cols.append(jnp.sum(pick.astype(F32) * gate_row(p), axis=1, keepdims=True))
            segments = c_all[pl.ds(p * 2, 2)].reshape(2 * rows, width)
            grads[here, :] = mm(pick, segments).astype(BF16)
        gate_col = jnp.concatenate(gate_cols)
        gate_pre, up_pre = gate_pre_s[...], up_pre_s[...]
        sig = 1.0 / (1.0 + jnp.exp(-gate_pre))
        silu = gate_pre * sig
        hidden_s[...] = (silu * up_pre).astype(BF16)
        out(2, zz).start()
        dots = jnp.zeros((quad, 1), F32)
        half = width // 2
        for h in range(2):
            cols = slice(h * half, (h + 1) * half)
            result = mm(hidden_s[...], down_w[:, cols]).astype(BF16).astype(F32)
            cot = grads[:, cols].astype(F32)
            dots = dots + jnp.sum(cot * result, axis=1, keepdims=True)
            grads[:, cols] = (gate_col * cot).astype(BF16)
            sent = (gate_col * result).astype(BF16)
            for j in range(2):
                here = slice(j * pair, (j + 1) * pair)
                there = slice(j * 2 * rows, (j + 1) * 2 * rows)
                stage[0, there, cols] = t_mm(picks[here, :], sent[here]).astype(BF16)
        out(1, zz).start()
        out(5, zz).start()
        for j in range(2):
            here = slice(j * pair, (j + 1) * pair)
            gate_grad = jnp.sum(picks[here, :].astype(F32) * dots[here], axis=0, keepdims=True)
            for i in range(2):
                gate_grads[(zz * 2 + j) * 2 + i] = gate_grad[:, i * rows : (i + 1) * rows]
        hidden_grad = mm_t(grads[...], down_w[...]).astype(BF16).astype(F32)
        slope = sig * (1.0 + gate_pre * (1.0 - sig))
        gate_s[...] = (hidden_grad * up_pre * slope).astype(BF16)
        up_s[...] = (hidden_grad * silu).astype(BF16)
        out(3, zz).start()
        out(4, zz).start()
        for h in range(2):
            cols = slice(h * half, (h + 1) * half)
            grad = mm_t(gate_s[...], gate_w[cols, :]) + mm_t(up_s[...], up_w[cols, :])
            grad = grad.astype(BF16)
            for j in range(2):
                here = slice(j * pair, (j + 1) * pair)
                there = slice(j * 2 * rows, (j + 1) * 2 * rows)
                stage[1, there, cols] = t_mm(picks[here, :], grad[here]).astype(BF16)
        out(6, zz).start()

    first = lax.axis_index("expert") // 4

    def process(d, zz):
        @pl.when(zz == first)
        def _():
            finish_recv()

        forward(d, zz)

        @pl.when(zz == first)
        def _():
            down_finish()

        backward(d, zz)

    gather_blocks(group // 4, [(x_all, x_send, x_recv), (c_all, c_send, c_recv)], process)
    for n in range(7):
        out(n, first).wait()
    finish_send()


def expert(x, cot, gates, gate_w, up_w, down_w, n_dp, cap, cid):
    group = gates.shape[0]
    rows, width = x.shape
    hidden = gate_w.shape[1]
    total = group * cap
    quad = 4 * cap

    def shape(*dims, dtype=BF16):
        return jax.ShapeDtypeStruct(dims, dtype)

    def buffer(*dims):
        return pltpu.VMEM(dims, BF16)

    return pl.pallas_call(
        functools.partial(expert_kernel, group, n_dp, cap),
        out_shape=[
            shape(total, width),
            shape(total, width),
            shape(total, hidden),
            shape(total, hidden),
            shape(total, hidden),
            shape(group * rows, width),
            shape(group * rows, width),
            shape(*gates.shape, dtype=F32),
        ],
        in_specs=[HBM, HBM, VMEM, VMEM, VMEM, HBM],
        out_specs=[HBM] * 7 + [VMEM],
        scratch_shapes=[
            buffer(group, rows, width),
            buffer(group, rows, width),
            buffer(n_dp * down_w.shape[0], width),
            pltpu.VMEM(gates.shape, F32),
            buffer(quad, 2 * rows),
            buffer(quad, width),
            buffer(quad, width),
            pltpu.VMEM((quad, hidden), F32),
            pltpu.VMEM((quad, hidden), F32),
            buffer(quad, hidden),
            buffer(quad, hidden),
            buffer(quad, hidden),
            buffer(2, 4 * rows, width),
            *gather_sems(group),
            *gather_sems(group),
            DMA((group,)),
            DMA((group,)),
            DMA((3,)),
            DMA,
            DMA,
            DMA((7,)),
        ],
        compiler_params=pltpu.CompilerParams(
            collective_id=cid, has_side_effects=True, vmem_limit_bytes=60 * 2**20
        ),
    )(x, cot, gates, gate_w, up_w, down_w)


def collect_kernel(
    group, n_dp,
    part, gate_ref, taken, grads, hidden, gate_grad, up_grad,
    sum_ref, gates_ref, gate_own, up_own, down_own, gate_dp, up_dp, down_dp, gate_in,
    r_sib, r_x, r_z, s_x, s_z, send, recv, g_send, g_recv, tile, tile_low, sems, dp_send, dp_recv,
):
    me, dp = lax.axis_index("expert"), lax.axis_index("dp")
    greet_all(group, n_dp)
    start, finish_recv, finish_send = tree_swap(
        group, lambda d, src: (gate_ref.at[d], gates_ref.at[src]), g_send, g_recv
    )
    start()
    gates_ref[me] = gate_ref[me]
    step, wide = tile.shape

    def product(left, right, own_out, dp_out, cols):
        half = own_out.shape[0]
        pieces = half // step

        def one(i, carry):
            there = pl.ds(i * step, step)
            for whose, buffer, ref, sem in (
                (1 - dp, tile_low, dp_out, sems.at[0]),
                (dp, tile, own_out, sems.at[1]),
            ):
                rows = pl.ds(pl.multiple_of(whose * half + i * step, step), step)
                buffer[...] = t_mm(left[:, rows], right[:, cols]).astype(buffer.dtype)
                put = pltpu.make_async_copy(buffer, ref.at[there, cols], sem)
                put.start()
                put.wait()
            return carry

        lax.fori_loop(0, pieces, one, 0)

    exchange = over_dp(gate_dp, gate_in, dp_send, dp_recv)

    def work(k):
        if k == 0:
            product(taken, gate_grad, gate_own, gate_dp, slice(0, wide))
            exchange.start()
        elif k == 1:
            product(taken, up_grad, up_own, up_dp, slice(0, wide))
        elif k == 2:
            for h in range(grads.shape[1] // wide):
                product(hidden, grads, down_own, down_dp, slice(h * wide, (h + 1) * wide))

    scatter_blocks(
        group // 4, part, sum_ref, r_sib, r_x, r_z, s_x, s_z, send, recv,
        lambda block: None, None, work,
    )
    finish_recv()
    finish_send()
    exchange.wait()


def collect(parts, gates, taken, grads, hidden, gate_grad, up_grad, n_dp, cid):
    group, rows, width = parts.shape
    narrow = hidden.shape[1]

    def halves(a, b):
        return a.shape[1] // n_dp, b.shape[1]

    shapes = [halves(taken, gate_grad), halves(taken, up_grad), halves(hidden, grads)]
    return pl.pallas_call(
        functools.partial(collect_kernel, group, n_dp),
        out_shape=[
            jax.ShapeDtypeStruct((rows, width), F32),
            jax.ShapeDtypeStruct(gates.shape, gates.dtype),
            *(jax.ShapeDtypeStruct(s, F32) for s in shapes),
            *(jax.ShapeDtypeStruct(s, BF16) for s in shapes),
            jax.ShapeDtypeStruct(shapes[0], BF16),
        ],
        in_specs=[VMEM] * 7,
        out_specs=[VMEM, VMEM] + [HBM] * 7,
        scratch_shapes=[
            *scatter_scratch(group, rows, width),
            DMA((group,)),
            DMA((group,)),
            pltpu.VMEM((256, narrow), F32),
            pltpu.VMEM((256, narrow), BF16),
            DMA((2,)),
            DMA,
            DMA,
        ],
        compiler_params=pltpu.CompilerParams(
            collective_id=cid, has_side_effects=True, vmem_limit_bytes=60 * 2**20
        ),
    )(parts, gates, taken, grads, hidden, gate_grad, up_grad)


def attention(queries, mask, keys, values):
    scores = jnp.where(mask, mm_t(queries, keys) * SCALE, NEGATIVE)
    row_max = jnp.max(scores, axis=-1, keepdims=True)
    weights = jnp.exp(scores - row_max)
    total = jnp.sum(weights, axis=-1, keepdims=True)
    attn = mm(weights.astype(BF16), values) / total
    return attn, row_max + jnp.log(total)


def attention_back(queries, mask, log_total, mixed_grad, row_delta, keys, values):
    probs = jnp.exp(jnp.where(mask, mm_t(queries, keys) * SCALE - log_total, NEGATIVE))
    score_grad = (probs * (mm_t(mixed_grad, values) - row_delta)).astype(BF16)
    query_grad = mm(score_grad, keys) * SCALE
    key_grad = t_mm(score_grad, queries) * SCALE
    return query_grad, key_grad, t_mm(probs.astype(BF16), mixed_grad)


def expert_step(rows_in, cot_in, gates, gate_w, up_w, down_w):
    cot_in = cot_in.astype(F32)
    gate_pre = mm(rows_in, gate_w)
    up_pre = mm(rows_in, up_w)
    sig = jax.nn.sigmoid(gate_pre)
    silu = gate_pre * sig
    hidden = (silu * up_pre).astype(BF16)
    expert_out = mm(hidden, down_w).astype(BF16).astype(F32)
    sent_out = (gates * expert_out).astype(BF16)
    gate_grad = jnp.sum(cot_in * expert_out, axis=-1)
    out_grad = (gates * cot_in).astype(BF16)
    hidden_grad = mm_t(out_grad, down_w).astype(BF16).astype(F32)
    gate_pre_grad = (hidden_grad * up_pre * sig * (1.0 + gate_pre * (1.0 - sig))).astype(BF16)
    up_pre_grad = (hidden_grad * silu).astype(BF16)
    row_grad = (mm_t(gate_pre_grad, gate_w) + mm_t(up_pre_grad, up_w)).astype(BF16)
    sums = (t_mm(rows_in, gate_pre_grad), t_mm(rows_in, up_pre_grad), t_mm(hidden, out_grad))
    return (sent_out, gate_grad, row_grad), sums


def per_device(
    tokens, attn_gain, q_gain, k_gain, ffn_gain, w_query, w_key, w_value, w_out, router,
    w_gate, w_up, w_down, cotangent, routes, parents,
):
    rows, width = tokens.shape
    heads = width // HEAD_DIM
    group = lax.axis_size("expert")
    n_dp = lax.axis_size("dp")
    devices = group * n_dp
    share = max(1, group // heads)
    tree_rows = group * rows
    own_rows = tree_rows // share
    shard = w_query.shape[0]
    dp = lax.axis_index("dp")
    me = lax.axis_index("expert")
    head = me // share
    part = me % share
    peers = [[h * share + j for h in range(heads)] for j in range(share)]
    siblings = [[h * share + j for j in range(share)] for h in range(heads)]

    reach = ancestry(parents)
    start = dp * group
    tree = lax.dynamic_slice(reach, (start, start), (group, group))
    depth = jnp.sum(lax.dynamic_slice_in_dim(reach, start, group, 0), axis=1)
    sees = tree + jnp.eye(group, dtype=F32)
    own_segs = own_rows // rows
    first_seg = part * own_segs
    my_depth = lax.dynamic_slice_in_dim(depth, first_seg, own_segs, 0)
    my_sees = lax.dynamic_slice_in_dim(sees, first_seg, own_segs, 0)
    place = jnp.arange(rows, dtype=F32)
    positions = (my_depth[:, None] * rows + place[None, :]).reshape(own_rows)
    frequencies = THETA ** (-2.0 * jnp.arange(HEAD_DIM // 2, dtype=F32) / HEAD_DIM)
    angles = positions[:, None] * frequencies[None, :]
    cosine, sine = jnp.cos(angles), jnp.sin(angles)
    key_index = jnp.arange(tree_rows, dtype=jnp.int32)
    query_index = first_seg * rows + jnp.arange(own_rows, dtype=jnp.int32)
    seen = jnp.repeat(jnp.repeat(my_sees, rows, axis=0), rows, axis=1) > 0.5
    mask = seen & (key_index[None, :] <= query_index[:, None])

    def own_part(values):
        return lax.dynamic_slice_in_dim(values, first_seg * rows, own_rows, 0)

    def head_sum(values):
        return lax.psum(values, "expert", axis_index_groups=peers if share > 1 else None)

    def tree_gather(values):
        return lax.all_gather(values, "expert", axis=0, tiled=True)

    def tree_scatter(values):
        return lax.psum_scatter(values, "expert", scatter_dimension=0, tiled=True).astype(F32)

    def both_swap(values):
        return lax.all_to_all(values, BOTH, 0, 0, tiled=True)

    def expert_swap(values):
        return lax.all_to_all(values, "expert", 0, 0, tiled=True)

    others = [(d, (d + 1) % n_dp) for d in range(n_dp)]

    def dp_join(values):
        if n_dp != 2:
            return lax.all_gather(values, "dp", axis=0, tiled=True)
        other = lax.ppermute(values, "dp", others)
        return jnp.where(
            dp == 0, jnp.concatenate([values, other]), jnp.concatenate([other, values])
        )

    def dp_sum(values):
        if n_dp != 2:
            return lax.psum_scatter(values, "dp", scatter_dimension=0, tiled=True)
        halves = values.reshape(2, values.shape[0] // 2, -1)
        theirs = lax.dynamic_index_in_dim(halves, 1 - dp, 0, keepdims=False)
        ours = lax.dynamic_index_in_dim(halves, dp, 0, keepdims=False)
        return ours.astype(F32) + lax.ppermute(theirs, "dp", others).astype(F32)

    gains = lax.all_gather(
        jnp.stack([attn_gain, q_gain, k_gain, ffn_gain], axis=1), BOTH, axis=0, tiled=True
    ).astype(F32)
    attn_g, query_g, key_g, ffn_g = gains[:, 0], gains[:, 1], gains[:, 2], gains[:, 3]
    my_query_g = lax.dynamic_slice_in_dim(query_g, head * HEAD_DIM, HEAD_DIM, 0)[None, :]
    my_key_g = lax.dynamic_slice_in_dim(key_g, head * HEAD_DIM, HEAD_DIM, 0)[None, :]
    by_head = jnp.stack([w_query, w_key, w_value], axis=1).reshape(shard, 3, heads, HEAD_DIM)
    by_head = by_head.transpose(2, 0, 1, 3).reshape(1, heads, 1, shard, 3 * HEAD_DIM)
    by_head = jnp.broadcast_to(by_head, (n_dp, heads, share, shard, 3 * HEAD_DIM))
    w_head = both_swap(by_head.reshape(devices, shard, 3 * HEAD_DIM)).reshape(
        width, 3 * HEAD_DIM
    )
    out_w = lax.all_gather(w_out, BOTH, axis=0, tiled=True)
    out_head = lax.dynamic_slice_in_dim(out_w, head * HEAD_DIM, HEAD_DIM, 0)
    router_w = lax.all_gather(router, BOTH, axis=0, tiled=True)
    gate_w = dp_join(w_gate[0])
    up_w = dp_join(w_up[0])
    down_w = dp_join(w_down[0])

    token_f = tokens.astype(F32)
    first_scale = inverse_rms(token_f)
    normed = (token_f * first_scale * attn_g[None, :]).astype(BF16)
    normed_all = own_part(tree_gather(normed))
    pre = mm(normed_all, w_head)
    query_pre, key_pre = pre[:, :HEAD_DIM], pre[:, HEAD_DIM : 2 * HEAD_DIM]
    values = pre[:, 2 * HEAD_DIM :].astype(BF16)
    squares = jnp.stack([jnp.sum(query_pre**2, axis=-1), jnp.sum(key_pre**2, axis=-1)])
    scales = lax.rsqrt(head_sum(squares) / width + EPSILON)
    query_scale, key_scale = scales[0][:, None], scales[1][:, None]
    queries = turn(query_pre * query_scale * my_query_g, cosine, sine).astype(BF16)
    keys = turn(key_pre * key_scale * my_key_g, cosine, sine).astype(BF16)
    if share > 1:
        keys_all = lax.all_gather(keys, "expert", axis=0, tiled=True, axis_index_groups=siblings)
        values_all = lax.all_gather(values, "expert", axis=0, tiled=True, axis_index_groups=siblings)
    else:
        keys_all, values_all = keys, values
    turns = max(1, tree_rows // 2048)

    def cut_rows(values):
        return values.reshape(turns, own_rows // turns, -1)

    def attend(cut):
        return attention(*cut, keys_all, values_all)

    if turns == 1:
        attn, log_total = attention(queries, mask, keys_all, values_all)
    else:
        attn, log_total = lax.map(attend, (cut_rows(queries), cut_rows(mask)))
        attn, log_total = attn.reshape(own_rows, HEAD_DIM), log_total.reshape(own_rows, 1)
    mixed_head = attn.astype(BF16)

    def to_owners(block):
        cut = block.reshape(own_segs, rows, -1)
        if share > 1:
            cut = lax.dynamic_update_slice_in_dim(
                jnp.zeros((group, *cut.shape[1:]), cut.dtype), cut, first_seg, 0
            )
        got = expert_swap(cut)
        if share > 1:
            got = jnp.sum(got.reshape(heads, share, rows, -1), axis=1, dtype=cut.dtype)
        return got

    mixed = to_owners(mixed_head).transpose(1, 0, 2).reshape(rows, width)
    residual = token_f + mm(mixed, out_w)
    second_scale = inverse_rms(residual)
    normed_two = (residual * second_scale * ffn_g[None, :]).astype(BF16)
    logits = mm(normed_two, router_w)
    router_probs = jax.nn.softmax(logits, axis=-1)
    experts = router_w.shape[1]
    labels = jnp.arange(experts, dtype=jnp.int32)
    routed = jnp.any(routes[:, :, None] == labels[None, None, :], axis=1)
    gates_own = jnp.where(routed, router_probs, 0.0)
    gates = expert_swap(gates_own.T[:, None]).reshape(tree_rows, 1)

    rows_in = tree_gather(normed_two)
    cot_in = lax.all_gather(cotangent, "expert", axis=0, tiled=True)
    pieces = max(1, tree_rows // 2048)
    if pieces == 1:
        (sent_out, gate_grad, row_grad), sums = expert_step(
            rows_in, cot_in, gates, gate_w, up_w, down_w
        )
    else:

        def expert_turn(sums, cut):
            result, more = expert_step(*cut, gate_w, up_w, down_w)
            return tuple(s + m for s, m in zip(sums, more)), result

        zeros = tuple(jnp.zeros(w.shape, F32) for w in (gate_w, up_w, down_w))
        cuts = tuple(v.reshape(pieces, -1, v.shape[1]) for v in (rows_in, cot_in, gates))
        sums, results = lax.scan(expert_turn, zeros, cuts)
        sent_out, gate_grad, row_grad = (
            r.reshape(tree_rows, *r.shape[2:]) for r in results
        )
    gate_w_grad, up_w_grad, down_w_grad = (s.astype(BF16) for s in sums)
    combined = lax.psum_scatter(sent_out, "expert", scatter_dimension=0, tiled=True)
    output = (residual + combined.astype(F32)).astype(BF16)
    gate_grad_own = expert_swap(gate_grad.reshape(group, 1, rows)).reshape(group, rows).T
    expert_grad = tree_scatter(row_grad)
    grad_gate, grad_up, grad_down = (
        dp_sum(g).astype(F32)[None]
        for g in (gate_w_grad, up_w_grad, down_w_grad)
    )

    prob_grad = jnp.where(routed, gate_grad_own, 0.0)
    logit_grad = (
        router_probs * (prob_grad - jnp.sum(router_probs * prob_grad, axis=-1, keepdims=True))
    ).astype(BF16)
    router_grad = t_mm(normed_two, logit_grad)
    normed_two_grad = expert_grad + mm_t(logit_grad, router_w)
    ffn_gain_grad = jnp.sum(normed_two_grad * residual * second_scale, axis=0)
    weighted = normed_two_grad * ffn_g[None, :]
    residual_grad = (
        cotangent.astype(F32)
        + second_scale * weighted
        - residual * second_scale**3 * jnp.mean(weighted * residual, axis=-1, keepdims=True)
    )
    proj_grad = residual_grad.astype(BF16)

    proj_all = own_part(tree_gather(proj_grad))
    mixed_grad = mm_t(proj_all, out_head).astype(BF16)
    out_w_grad = t_mm(mixed_head, proj_all)
    row_delta = jnp.sum(mixed_grad.astype(F32) * attn, axis=-1, keepdims=True)
    back_args = (queries, mask, log_total, mixed_grad, row_delta)
    if turns == 1:
        query_grad, key_grad, value_grad = attention_back(*back_args, keys_all, values_all)
    else:

        def attention_turn(sums, cut):
            first, *more = attention_back(*cut, keys_all, values_all)
            return tuple(s + m for s, m in zip(sums, more)), first

        zeros = jnp.zeros((tree_rows, HEAD_DIM), F32)
        (key_grad, value_grad), query_grad = lax.scan(
            attention_turn, (zeros, zeros), tuple(cut_rows(v) for v in back_args)
        )
        query_grad = query_grad.reshape(own_rows, HEAD_DIM)
    if share > 1:
        key_grad = lax.psum_scatter(
            key_grad, "expert", scatter_dimension=0, tiled=True, axis_index_groups=siblings
        )
        value_grad = lax.psum_scatter(
            value_grad, "expert", scatter_dimension=0, tiled=True, axis_index_groups=siblings
        )
    query_turned = turn(query_grad, cosine, -sine)
    key_turned = turn(key_grad, cosine, -sine)
    dots = jnp.stack(
        [
            jnp.sum(query_turned * my_query_g * query_pre, axis=-1),
            jnp.sum(key_turned * my_key_g * key_pre, axis=-1),
        ]
    )
    means = head_sum(dots) / width
    query_low = query_scale * my_query_g * query_turned - query_pre * query_scale**3 * means[0][:, None]
    key_low = key_scale * my_key_g * key_turned - key_pre * key_scale**3 * means[1][:, None]
    low = jnp.concatenate([query_low, key_low, value_grad], axis=1).astype(BF16)
    query_gain_grad = jnp.sum(query_turned * query_pre * query_scale, axis=0)
    key_gain_grad = jnp.sum(key_turned * key_pre * key_scale, axis=0)
    normed_part = mm_t(low, w_head).astype(BF16)
    if share > 1:
        normed_part = lax.dynamic_update_slice_in_dim(
            jnp.zeros((tree_rows, width), BF16), normed_part, first_seg * rows, 0
        )
    normed_grad = tree_scatter(normed_part)
    attn_gain_grad = jnp.sum(normed_grad * token_f * first_scale, axis=0)
    weighted = normed_grad * attn_g[None, :]
    token_grad = (
        residual_grad
        + first_scale * weighted
        - token_f * first_scale**3 * jnp.mean(weighted * token_f, axis=-1, keepdims=True)
    )

    head_grad = t_mm(normed_all, low)
    got = both_swap(head_grad.reshape(devices, shard, 3 * HEAD_DIM)).reshape(n_dp, heads, share, shard, 3, HEAD_DIM)
    got = jnp.sum(got, axis=(0, 2)).transpose(2, 1, 0, 3).reshape(3, shard, width)
    shards_a_head = HEAD_DIM // shard
    source = dp * share + part
    flat = [(d, h * share + j) for d in range(n_dp) for h in range(heads) for j in range(share)]
    grad_out = jnp.zeros((shard, width), F32)
    for turn_index in range(shards_a_head):
        pairs = []
        for d, e in flat:
            s = d * share + e % share
            target = (e // share) * shards_a_head + (s + turn_index) % shards_a_head
            pairs.append((d * group + e, target))
        block = lax.dynamic_slice_in_dim(
            out_w_grad, ((source + turn_index) % shards_a_head) * shard, shard, 0
        )
        grad_out = grad_out + lax.ppermute(block, BOTH, pairs)
    head_gains = jnp.stack([query_gain_grad, key_gain_grad], axis=1)
    head_gains = lax.dynamic_update_slice_in_dim(
        jnp.zeros((width, 2), F32), head_gains, head * HEAD_DIM, 0
    )
    small = jnp.concatenate(
        [router_grad, attn_gain_grad[:, None], head_gains, ffn_gain_grad[:, None]], axis=1
    )
    small = jnp.sum(both_swap(small.reshape(devices, shard, -1)), axis=0)
    return (
        output,
        token_grad,
        small[:, experts],
        small[:, experts + 1],
        small[:, experts + 2],
        small[:, experts + 3],
        got[0],
        got[1],
        got[2],
        grad_out,
        small[:, :experts],
        grad_gate,
        grad_up,
        grad_down,
    )


def per_head(
    tokens, attn_gain, q_gain, k_gain, ffn_gain, w_query, w_key, w_value, w_out, router,
    w_gate, w_up, w_down, cotangent, routes, parents,
):
    rows, width = tokens.shape
    group = lax.axis_size("expert")
    n_dp = lax.axis_size("dp")
    devices = group * n_dp
    count = group * rows
    shard = w_query.shape[0]
    dp = lax.axis_index("dp")
    me = lax.axis_index("expert")
    experts = router.shape[1]

    reach = ancestry(parents)
    start = dp * group
    tree = lax.dynamic_slice(reach, (start, start), (group, group))
    depth = jnp.sum(lax.dynamic_slice_in_dim(reach, start, group, 0), axis=1)
    sees = tree + jnp.eye(group, dtype=F32)
    bias = jnp.repeat(jnp.where(sees > 0.5, 0.0, NEGATIVE), rows, axis=1)
    positions = (depth[:, None] * rows + jnp.arange(rows, dtype=F32)[None, :]).reshape(count)
    frequencies = THETA ** (-2.0 * jnp.arange(HEAD_DIM // 2, dtype=F32) / HEAD_DIM)
    angles = positions[:, None] * frequencies[None, :]
    cosine, sine = jnp.cos(angles), jnp.sin(angles)

    by_head = jnp.stack([w_query, w_key, w_value], axis=1).reshape(shard, 3, group, HEAD_DIM)
    by_head = by_head.transpose(2, 0, 1, 3).reshape(group, shard, 3 * HEAD_DIM)
    extra = jnp.concatenate(
        [
            jnp.stack([attn_gain, q_gain, k_gain, ffn_gain], axis=1),
            router,
            jnp.zeros((shard, HEAD_DIM - 4 - experts), BF16),
        ],
        axis=1,
    )
    extra = jnp.broadcast_to(extra[None], (group, shard, HEAD_DIM))
    w_cut = jnp.concatenate([by_head, extra], axis=2)
    normed_all, pre, w_all, gains, gate_w = project(tokens, w_cut, w_gate[0], n_dp, 0)
    attn_g, ffn_g = gains[0:1], gains[3:4]
    my_query_g = lax.dynamic_slice_in_dim(gains[1:2], me * HEAD_DIM, HEAD_DIM, 1)
    my_key_g = lax.dynamic_slice_in_dim(gains[2:3], me * HEAD_DIM, HEAD_DIM, 1)
    router_w = w_all[:, 3 * HEAD_DIM + 4 : 3 * HEAD_DIM + 4 + experts]
    flat = range(devices)
    blocks = []
    for r in range(n_dp):
        pairs = [(f, ((f + r) % n_dp) * group + f // n_dp) for f in flat]
        blocks.append(lax.ppermute(w_out, BOTH, pairs))
    blocks = jnp.stack(blocks)
    out_head = jnp.concatenate(
        [
            lax.dynamic_index_in_dim(blocks, (dp - i) % n_dp, 0, keepdims=False)
            for i in range(n_dp)
        ]
    )

    query_pre, key_pre = pre[:, :HEAD_DIM], pre[:, HEAD_DIM : 2 * HEAD_DIM]
    values = pre[:, 2 * HEAD_DIM :].astype(BF16)

    def head_sum(a, b, cid):
        sums = jnp.stack([jnp.sum(a, axis=-1), jnp.sum(b, axis=-1)]).reshape(1, -1, HEAD_DIM)
        sums = jnp.sum(swap(sums, ("expert",), cid), axis=0).reshape(2, count, 1)
        return sums[0] / width, sums[1] / width

    query_mean, key_mean = head_sum(query_pre**2, key_pre**2, 1)
    query_scale = lax.rsqrt(query_mean + EPSILON)
    key_scale = lax.rsqrt(key_mean + EPSILON)
    queries = turn(query_pre * query_scale * my_query_g, cosine, sine).astype(BF16)
    keys = turn(key_pre * key_scale * my_key_g, cosine, sine).astype(BF16)
    attn, lse, projected, up_w = attend(
        queries, keys, values, bias, out_head, w_up[0], n_dp, 2
    )
    token_f = tokens.astype(F32)
    residual = token_f + projected
    second_scale = inverse_rms(residual)
    normed_two = (residual * second_scale * ffn_g).astype(BF16)
    logits = mm(normed_two, router_w)
    router_probs = jax.nn.softmax(logits, axis=-1)
    labels = jnp.arange(experts, dtype=jnp.int32)
    routed = jnp.any(routes[:, :, None] == labels[None, None, :], axis=1)
    gates_own = jnp.where(routed, router_probs, 0.0)

    cap = 3 * rows * routes.shape[1] // (2 * experts)
    taken, taken_grad, hidden, gate_pre_grad, up_pre_grad, sent_out, row_grad, gate_grad = expert(
        normed_two, cotangent, gates_own.T[:, None], gate_w, up_w, w_down[0], n_dp, cap, 3
    )
    expert_grad, gate_grad_own, gate_own, up_own, down_own, _, up_dp, down_dp, gate_in = collect(
        row_grad.reshape(group, rows, width),
        gate_grad, taken, taken_grad, hidden, gate_pre_grad, up_pre_grad, n_dp, 4,
    )
    gate_grad_own = gate_grad_own.reshape(group, rows).T
    combined = lax.psum_scatter(sent_out, "expert", scatter_dimension=0, tiled=True)

    prob_grad = jnp.where(routed, gate_grad_own, 0.0)
    logit_grad = (
        router_probs * (prob_grad - jnp.sum(router_probs * prob_grad, axis=-1, keepdims=True))
    ).astype(BF16)
    router_grad = t_mm(logit_grad, normed_two)
    normed_two_grad = expert_grad + mm_t(logit_grad, router_w)
    ffn_gain_grad = jnp.sum(normed_two_grad * residual * second_scale, axis=0)
    weighted = normed_two_grad * ffn_g
    residual_grad = (
        cotangent.astype(F32)
        + second_scale * weighted
        - residual * second_scale**3 * jnp.mean(weighted * residual, axis=-1, keepdims=True)
    )
    proj_grad = residual_grad.astype(BF16)

    query_grad, key_grad, value_grad, out_w_grad, up_in, down_first = attend_back(
        proj_grad, queries, keys, values, bias, out_head, attn, lse, up_dp, down_dp, n_dp, 5
    )
    query_turned = turn(query_grad * SCALE, cosine, -sine)
    key_turned = turn(key_grad * SCALE, cosine, -sine)
    query_mean, key_mean = head_sum(
        query_turned * my_query_g * query_pre, key_turned * my_key_g * key_pre, 6
    )
    query_low = query_scale * my_query_g * query_turned - query_pre * query_scale**3 * query_mean
    key_low = key_scale * my_key_g * key_turned - key_pre * key_scale**3 * key_mean
    low = jnp.concatenate([query_low, key_low, value_grad], axis=1).astype(BF16)
    combined, low = lax.optimization_barrier((combined, low))
    output = (residual + combined.astype(F32)).astype(BF16)
    query_gain_grad = jnp.sum(query_turned * query_pre * query_scale, axis=0)
    key_gain_grad = jnp.sum(key_turned * key_pre * key_scale, axis=0)
    normed_grad, grad_query, grad_key, grad_value, down_second = unproject(
        low, w_all, normed_all.reshape(count, width), down_dp, rows, shard, n_dp, 7
    )
    grad_gate = (gate_own + gate_in.astype(F32))[None]
    grad_up = (up_own + up_in.astype(F32))[None]
    grad_down = (down_own + jnp.concatenate([down_first, down_second]).astype(F32))[None]
    attn_scale = inverse_rms(token_f)
    attn_gain_grad = jnp.sum(normed_grad * token_f * attn_scale, axis=0)
    weighted = normed_grad * attn_g
    token_grad = (
        residual_grad
        + attn_scale * weighted
        - token_f * attn_scale**3 * jnp.mean(weighted * token_f, axis=-1, keepdims=True)
    )

    grad_out = jnp.zeros((shard, width), F32)
    halves = out_w_grad.reshape(n_dp, shard, width)
    for r in range(n_dp):
        pairs = []
        for d in range(n_dp):
            for e in range(group):
                pairs.append((d * group + e, e * n_dp + (d + r) % n_dp))
        block = lax.dynamic_index_in_dim(halves, (dp + r) % n_dp, 0, keepdims=False)
        grad_out = grad_out + lax.ppermute(block, BOTH, pairs)
    head_gains = jnp.stack([query_gain_grad, key_gain_grad])
    head_gains = lax.dynamic_update_slice_in_dim(
        jnp.zeros((2, width), F32), head_gains, me * HEAD_DIM, 1
    )
    small = jnp.concatenate([router_grad, head_gains, ffn_gain_grad[None], attn_gain_grad[None]])
    small = small.reshape(-1, devices, shard).transpose(1, 0, 2)
    small = jnp.sum(swap(small, BOTH, 8), axis=0)
    return (
        output,
        token_grad,
        small[experts + 3],
        small[experts],
        small[experts + 1],
        small[experts + 2],
        grad_query,
        grad_key,
        grad_value,
        grad_out,
        small[:experts].T,
        grad_gate,
        grad_up,
        grad_down,
    )


def solution(mesh):
    row, vec = P(BOTH, None), P(BOTH)
    expert = P("expert", "dp", None)
    wide = mesh.shape["expert"] != HEADS or mesh.shape["dp"] != 2
    return jax.shard_map(
        per_device if wide else per_head,
        mesh=mesh,
        in_specs=(row, vec, vec, vec, vec, row, row, row, row, row, expert, expert, expert, row, row, P()),
        out_specs=(row, row, vec, vec, vec, vec, row, row, row, row, row, expert, expert, expert),
        check_vma=False,
    )
```
